32 devices in a mesh: grp: 8 (over z, y), blk: 4 (over x, core).
Axes of the slice: x: 2, y: 2, z: 4, core: 2. Of those that a mesh axis runs over, the one named last changes fastest.
Arguments:
- embeddings: bfloat16 [24576, 768], P(('grp', 'blk'))
- send_slot: int32 [24576], P(('grp', 'blk')), may hold values from 0 to 1535, as said below
Outputs:
- similarity: float32 [24576], P(('grp', 'blk'))
The draws below stay inside these ranges and needn't reach their ends.
Inputs may be any that keep to these rules, and one draw needn't show every extreme that they name: `send_slot`: within the 768 rows of one arrival block the values are distinct; value // 48 is the target device in the order grp then blk. Every arrival block uses every multiple of 48 and the value 1536 - 1, and in every draw one target device receives all 48 of its slots from every arrival block.
All inputs are finite; a program needn't handle non-finite values.
Results may differ from the reference program's by a relative error of at most 0.00052.
Values may be sent and summed in bfloat16 or wider, within the bound.
No kernel may reach another device: no remote copies, remote signals or barrier semaphores. Data moves between devices by JAX's collectives and lax.ppermute only.
A program may use at most 64 MiB of HBM per device.

```python
import math
import jax
import jax.numpy as jnp
from jax import lax

D = 768
ROWS_DEV = 768
GROUP = 4
CLUSTERS = 8
PAIR = 48
HOLD = 1536
SPAN = 6144
N_BLK = 4


def slot_table(key):
    base_key = jax.random.fold_in(key, 101)
    key_bias, key_jitter, key_order, key_hot = jax.random.split(base_key, 4)
    target_count = HOLD // PAIR
    group_bias = jax.random.randint(key_bias, (target_count // N_BLK,), 0, 8192)
    slot_bias = jnp.repeat(group_bias, N_BLK * PAIR)
    jitter = jax.random.randint(key_jitter, (target_count, HOLD), 0, 4096)
    slot_ids = jnp.arange(HOLD).astype(jnp.int32)
    hot_target = jax.random.randint(key_hot, (), 0, target_count)
    forced = (slot_ids // PAIR == hot_target) | (slot_ids % PAIR == 0) | (slot_ids == HOLD - 1)
    scores = jnp.where(forced[None, :], slot_ids[None, :] - HOLD, (jitter + slot_bias[None, :]) * HOLD + slot_ids[None, :])
    chosen = jnp.argsort(scores, axis=1, stable=True)[:, :ROWS_DEV].astype(jnp.int32)
    shuffled = jax.random.permutation(key_order, chosen, axis=1, independent=True)
    return shuffled.reshape(-1).astype(jnp.int32)


def draw_send_slot(key, part):
    slot_values = slot_table(key)
    return slot_values


def draw_embeddings(key, part):
    slot_values = slot_table(key)
    key = jax.random.fold_in(key, 5)
    key_jitter = jax.random.fold_in(key, 0)
    key_strength = jax.random.fold_in(key, 1)
    key_proto = jax.random.fold_in(key, 2)
    key_cluster = jax.random.fold_in(key, 4)
    key_anti = jax.random.fold_in(key, 5)
    key_partner = jax.random.fold_in(key, 6)
    row_total = slot_values.shape[0]
    source_count = row_total // ROWS_DEV
    cluster_count = HOLD // PAIR // N_BLK
    source_index = (jnp.arange(row_total) // ROWS_DEV).astype(jnp.int32)
    target = slot_values // PAIR
    group_index = target // N_BLK
    within = slot_values % PAIR
    feature_ids = jnp.arange(D).astype(jnp.int32)
    lower_half = (feature_ids < D // 2).astype(jnp.float32)
    upper_half = 1.0 - lower_half
    proto_count = ROWS_DEV * N_BLK // 4
    partner_pick = jax.random.randint(key_partner, (row_total,), 0, proto_count).astype(jnp.int32)
    prototype_id = (group_index * proto_count + partner_pick).astype(jnp.int32)
    prototype = jax.vmap(lambda ident: jax.random.normal(jax.random.fold_in(key_proto, ident), (D,), jnp.float32))(prototype_id) * lower_half[None, :]
    cluster_table = jax.random.normal(key_cluster, (cluster_count, D), jnp.float32) * upper_half[None, :]
    cluster_direction = cluster_table[group_index]
    anti_source = jax.random.randint(key_anti, (cluster_count,), 0, source_count)
    anti_row = (source_index == anti_source[group_index]) & (target % N_BLK == 0) & (within == 0)
    strength = jnp.exp(jax.random.uniform(key_strength, (row_total, 1), jnp.float32, math.log(0.1), math.log(10.0)))
    jitter = jax.random.normal(key_jitter, (row_total, D), jnp.float32)
    row_scale = jnp.ones((row_total, 1), jnp.float32)
    drawn = jitter + strength * prototype + 2.0 * cluster_direction
    values = jnp.where(anti_row[:, None], -cluster_direction, drawn)
    return (values * row_scale).astype(jnp.bfloat16)


def setup_inputs(seed: int = 0) -> dict:
    keys = jax.random.split(jax.random.key(seed), 3)
    embeddings = draw_embeddings(jax.random.fold_in(keys[2], 71), 0)
    send_slot = draw_send_slot(jax.random.fold_in(keys[2], 71), 0)
    return dict(embeddings=embeddings, send_slot=send_slot)


def reference(embeddings, send_slot):
    widened = embeddings.astype(jnp.float32)
    normed = (widened * lax.rsqrt(lax.optimization_barrier(jnp.sum(widened * widened, axis=-1, keepdims=True)) + 1e-06)).astype(jnp.bfloat16)
    row_total = embeddings.shape[0]
    source_index = (jnp.arange(row_total) // ROWS_DEV).astype(jnp.int32)
    target = (send_slot // PAIR).astype(jnp.int32)
    position = (target // GROUP * SPAN + target % GROUP * HOLD + source_index * PAIR + send_slot % PAIR).astype(jnp.int32)
    packed = jnp.zeros((CLUSTERS * SPAN, D), jnp.bfloat16).at[position].set(normed).reshape(CLUSTERS, SPAN, D)
    live_slots = jnp.zeros((CLUSTERS * SPAN,), jnp.float32).at[position].set(1.0).reshape(CLUSTERS, SPAN)
    slot_ids = jnp.arange(SPAN).astype(jnp.int32)

    def cluster_best(operands):
        members, member_live = operands

        def block_best(block_number):
            first = block_number * 512
            row_block = lax.dynamic_slice_in_dim(members, first, 512, 0)
            scores = jnp.dot(row_block, members.T, preferred_element_type=jnp.float32)
            row_ids = (first + jnp.arange(512)).astype(jnp.int32)
            usable = (member_live[None, :] > 0) & (row_ids[:, None] != slot_ids[None, :])
            return lax.optimization_barrier(jnp.max(jnp.where(usable, scores, -3.0), axis=1))
        return lax.map(block_best, jnp.arange(SPAN // 512).astype(jnp.int32)).reshape(SPAN)
    similar = lax.map(cluster_best, (packed, live_slots)).reshape(CLUSTERS * SPAN)
    return similar[position]
```

```python
import functools

import jax
import jax.numpy as jnp
from jax import lax
from jax.experimental import pallas as pl
from jax.experimental.pallas import tpu as pltpu
from jax.sharding import PartitionSpec as P

sentinel = -3.0
epsilon = 1e-06
dead_mark = 2.0
dead_bias = -8.0
lanes = 128


def chunk_sizes(capacity):
    count = 4 if capacity % 64 == 0 else 3
    return (capacity // count,) * count


def head_kernel(capacity, chunks, groups, slot_ref, x_ref, *out_refs):
    rows = x_ref.shape[0]
    wide = x_ref[...].astype(jnp.float32)
    normed = (
        wide * lax.rsqrt(jnp.sum(wide * wide, axis=-1, keepdims=True) + epsilon)
    ).astype(jnp.bfloat16)
    slots = slot_ref[...]
    first = 0
    for size, out_ref in zip(chunks, out_refs):
        place = lax.broadcasted_iota(jnp.int32, (groups, size, 1), 1)
        group = lax.broadcasted_iota(jnp.int32, (groups, size, 1), 0)
        wanted = (group * capacity + place + first).reshape(groups * size, 1)
        hit = wanted == slots
        pick = jnp.where(hit, 1.0, 0.0)
        live = jnp.max(pick, axis=1, keepdims=True)
        placed = jnp.dot(pick.astype(jnp.bfloat16), normed, preferred_element_type=jnp.float32)
        lane = lax.broadcasted_iota(jnp.int32, (1, placed.shape[1]), 1)
        mark = jnp.where(lane == 0, dead_mark, 0.0)
        placed = placed + (1.0 - live) * mark
        out_ref[...] = placed.astype(jnp.bfloat16)
        first += size


def head(embeddings, send_slot, capacity, chunks, groups):
    rows, features = embeddings.shape
    return pl.pallas_call(
        functools.partial(head_kernel, capacity, chunks, groups),
        out_shape=[
            jax.ShapeDtypeStruct((groups * size, features), jnp.bfloat16) for size in chunks
        ],
        compiler_params=pltpu.CompilerParams(vmem_limit_bytes=40 * 2**20),
        name="place_rows",
    )(send_slot.reshape(1, rows), embeddings)


def lane_fold(values):
    best = values[:, :lanes]
    for start in range(lanes, values.shape[1], lanes):
        best = jnp.maximum(best, values[:, start : start + lanes])
    return best


def gram_kernel(step, last, tile, me_ref, *refs):
    owns = refs[: step + 1]
    x_ref = refs[step + 1]
    states = refs[step + 2 : 2 * step + 2]
    outs = refs[2 * step + 2 :]
    row_outs = outs[: step + 1]
    col_out = outs[step + 1]
    index = pl.program_id(0)

    @pl.when(index == 0)
    def _():
        for state, out in zip(states, row_outs):
            out[...] = state[...]
        row_outs[step][...] = jnp.full(row_outs[step].shape, sentinel, jnp.float32)

    x = x_ref[...]
    features = x.shape[1]
    unit = jnp.where(lax.broadcasted_iota(jnp.int32, (16, features), 1) == 0, 1.0, 0.0)
    nt = (((1,), (1,)), ((), ()))
    marks = lax.dot_general(unit.astype(jnp.bfloat16), x, nt, preferred_element_type=jnp.float32)
    col_bias = jnp.where(marks[0:1, :] > 1.5, dead_bias, 0.0)
    col_best = jnp.full((1, tile), sentinel, jnp.float32)
    for j in range(step + 1):
        count = owns[j].shape[0]
        block = 128
        for start in range(0, count, block):
            own = owns[j][start : start + block, :]
            scores = lax.dot_general(own, x, nt, preferred_element_type=jnp.float32)
            usable = scores + col_bias
            if j == step:
                rows = lax.broadcasted_iota(jnp.int32, (block, tile), 0)
                cols = lax.broadcasted_iota(jnp.int32, (block, tile), 1)
                offset = index * tile - (me_ref[0] * count + start)
                usable = jnp.where(rows - cols == offset, dead_bias, usable)
            else:
                row_bias = jnp.where(own[:, 0:1].astype(jnp.float32) > 1.5, dead_bias, 0.0)
                col_best = jnp.maximum(
                    col_best, jnp.max(scores + row_bias, axis=0, keepdims=True)
                )
            row_outs[j][start : start + block, :] = jnp.maximum(
                row_outs[j][start : start + block, :], lane_fold(usable)
            )
    col_out[...] = col_best


def gram_step(step, last, me, owns, gathered, states):
    total, features = gathered.shape
    tile = 512
    while total % tile:
        tile -= 128
    const = lambda i, me_ref: (0, 0)
    counts = [own.shape[0] for own in owns]
    row_specs = [pl.BlockSpec((count, lanes), const) for count in counts]
    results = pl.pallas_call(
        functools.partial(gram_kernel, step, last, tile),
        grid_spec=pltpu.PrefetchScalarGridSpec(
            num_scalar_prefetch=1,
            grid=(total // tile,),
            in_specs=[pl.BlockSpec((count, features), const) for count in counts]
            + [pl.BlockSpec((tile, features), lambda i, me_ref: (i, 0))]
            + row_specs[:-1],
            out_specs=row_specs + [pl.BlockSpec((1, tile), lambda i, me_ref: (0, i))],
        ),
        out_shape=[jax.ShapeDtypeStruct((count, lanes), jnp.float32) for count in counts]
        + [jax.ShapeDtypeStruct((1, total), jnp.float32)],
        compiler_params=pltpu.CompilerParams(vmem_limit_bytes=40 * 2**20),
        cost_estimate=pl.CostEstimate(
            flops=2 * sum(counts) * total * features,
            bytes_accessed=2 * features * (sum(counts) + total),
            transcendentals=0,
        ),
        name="gram_step",
    )(me, *owns, gathered, *states)
    return list(results[:-1]), results[-1]


def tail_kernel(capacity, members, slot_ref, part_ref, out_ref, table):
    groups = part_ref.shape[0] // members
    width = table.shape[1]
    table[...] = jnp.full(table.shape, sentinel, jnp.float32)
    for g in range(groups):
        table[g : g + 1, :capacity] = jnp.max(
            part_ref[g * members : (g + 1) * members, :], axis=0, keepdims=True
        )
    rows = out_ref.shape[1]
    lane = lax.broadcasted_iota(jnp.int32, (lanes, lanes), 1)
    for start in range(0, rows, lanes):
        slot = jnp.broadcast_to(slot_ref[0:1, start : start + lanes], (lanes, lanes)).T
        best = jnp.full((lanes, lanes), sentinel, jnp.float32)
        for g in range(groups):
            for c in range(0, width, lanes):
                entry = table[g : g + 1, c : c + lanes]
                best = jnp.maximum(
                    best, jnp.where(slot - (g * capacity + c) == lane, entry, sentinel)
                )
        out_ref[0:1, start : start + lanes] = jnp.max(best.T, axis=0, keepdims=True)


def tail(partials, send_slot, capacity, members):
    rows = send_slot.shape[0]
    groups = partials.shape[0] // members
    width = -(-capacity // lanes) * lanes
    return pl.pallas_call(
        functools.partial(tail_kernel, capacity, members),
        out_shape=jax.ShapeDtypeStruct((1, rows), jnp.float32),
        scratch_shapes=[pltpu.VMEM((groups, width), jnp.float32)],
        name="pick_rows",
    )(send_slot.reshape(1, rows), partials).reshape(rows)


def on_device(embeddings, send_slot):
    row_count, features = embeddings.shape
    groups = lax.axis_size("grp")
    members = lax.axis_size("blk")
    slot_count = 2 * row_count
    capacity = slot_count // groups
    chunks = chunk_sizes(capacity)
    me = lax.axis_index("blk").astype(jnp.int32)
    placed = head(embeddings, send_slot, capacity, chunks, groups)
    owns, states, cols = [], [], []
    for step, size in enumerate(chunks):
        own = lax.all_to_all(
            placed[step].reshape(groups, size, features), "grp", 0, 0, tiled=True
        ).reshape(groups * size, features)
        gathered = lax.all_gather(own, "blk", axis=0, tiled=True)
        owns.append(own)
        states, col = gram_step(
            step, step == len(chunks) - 1, me.reshape(1), owns, gathered, states
        )
        cols.append(col)
    pieces = []
    for size, state, col in zip(chunks, states, cols):
        row = jnp.max(state, axis=1).reshape(1, groups, size)
        col = col.reshape(members, groups, size)
        is_me = (jnp.arange(members) == me)[:, None, None]
        pieces.append(jnp.where(is_me, jnp.maximum(row, col), col))
    best = jnp.concatenate(pieces, axis=2).transpose(1, 0, 2)
    homeward = lax.all_to_all(
        best.reshape(groups * members, capacity), ("grp", "blk"), 0, 0, tiled=True
    )
    return tail(homeward, send_slot, capacity, members)


def solution(mesh):
    in_specs = (P(("grp", "blk"), None), P(("grp", "blk")))
    out_specs = P(("grp", "blk"))
    return jax.shard_map(
        on_device, mesh=mesh, in_specs=in_specs, out_specs=out_specs, check_vma=False
    )
```

```python
import functools

import jax
import jax.numpy as jnp
from jax import lax
from jax.experimental import pallas as pl
from jax.experimental.pallas import tpu as pltpu
from jax.sharding import PartitionSpec as P

sentinel = -3.0
epsilon = 1e-06
dead_mark = 2.0
dead_bias = -8.0
lanes = 128
smem = pl.BlockSpec(memory_space=pltpu.SMEM)
vmem = pl.BlockSpec(memory_space=pltpu.VMEM)


def chunk_sizes(capacity):
    count = 4 if capacity % 64 == 0 else 3
    return (capacity // count,) * count


def swap(value, axis, size, bit):
    return lax.ppermute(value, axis, [(i, i ^ bit) for i in range(size)])


def head_kernel(capacity, chunks, groups, me_ref, slot_ref, x_ref, *out_refs):
    wide = x_ref[...].astype(jnp.float32)
    normed = (
        wide * lax.rsqrt(jnp.sum(wide * wide, axis=-1, keepdims=True) + epsilon)
    ).astype(jnp.bfloat16)
    slots = jnp.concatenate([slot_ref[q : q + 1, :] for q in range(slot_ref.shape[0])], axis=1)
    first = 0
    for step, size in enumerate(chunks):
        place = lax.broadcasted_iota(jnp.int32, (groups, size, 1), 1)
        group = lax.broadcasted_iota(jnp.int32, (groups, size, 1), 0) ^ me_ref[0]
        wanted = (group * capacity + place + first).reshape(groups * size, 1)
        pick = jnp.where(wanted == slots, 1.0, 0.0)
        live = jnp.max(pick, axis=1, keepdims=True)
        placed = jnp.dot(pick.astype(jnp.bfloat16), normed, preferred_element_type=jnp.float32)
        lane = lax.broadcasted_iota(jnp.int32, (1, placed.shape[1]), 1)
        mark = jnp.where(lane == 0, dead_mark, 0.0)
        placed = (placed + (1.0 - live) * mark).astype(jnp.bfloat16)
        for r in range(groups):
            out_refs[step * groups + r][...] = placed[r * size : (r + 1) * size, :]
        first += size


def head(me, embeddings, slots, capacity, chunks, groups):
    rows, features = embeddings.shape
    return pl.pallas_call(
        functools.partial(head_kernel, capacity, chunks, groups),
        in_specs=[smem, vmem, vmem],
        out_specs=[vmem] * (groups * len(chunks)),
        out_shape=[
            jax.ShapeDtypeStruct((size, features), jnp.bfloat16)
            for size in chunks
            for _ in range(groups)
        ],
        compiler_params=pltpu.CompilerParams(vmem_limit_bytes=32 * 2**20),
        name="place_rows",
    )(me, slots, embeddings)


def lane_fold(values):
    best = values[:, :lanes]
    for start in range(lanes, values.shape[1], lanes):
        best = jnp.maximum(best, values[:, start : start + lanes])
    return best


def gram_body(own_refs, piece_refs, row_refs, col_ref, stack, tile):
    step = len(own_refs) - 1
    count = own_refs[step].shape[0]
    for p, piece_ref in enumerate(piece_refs):
        stack[p * count : (p + 1) * count, :] = piece_ref[...]
    row_refs[step][...] = jnp.full(row_refs[step].shape, sentinel, jnp.float32)
    nt = (((1,), (1,)), ((), ()))

    @pl.loop(0, stack.shape[0] // tile)
    def _(n):
        first = pl.multiple_of(n * tile, tile)
        x = stack[pl.ds(first, tile), :]
        marks = x[:, :lanes].astype(jnp.float32).T[0:1, :]
        col_bias = jnp.where(marks > 1.5, dead_bias, 0.0)
        col_best = jnp.full((1, tile), sentinel, jnp.float32)
        for j in range(step + 1):
            own = own_refs[j][...]
            scores = lax.dot_general(own, x, nt, preferred_element_type=jnp.float32)
            usable = scores + col_bias
            if j == step:
                rows = lax.broadcasted_iota(jnp.int32, usable.shape, 0)
                cols = lax.broadcasted_iota(jnp.int32, usable.shape, 1)
                usable = jnp.where(rows - cols == first, dead_bias, usable)
            else:
                row_bias = jnp.where(own[:, 0:1].astype(jnp.float32) > 1.5, dead_bias, 0.0)
                col_best = jnp.maximum(
                    col_best, jnp.max(scores + row_bias, axis=0, keepdims=True)
                )
            row_refs[j][...] = jnp.maximum(row_refs[j][...], lane_fold(usable))
        col_ref[0:1, pl.ds(first, tile)] = col_best


def gram_kernel(step, pieces, tile, *refs):
    owns = refs[: step + 1]
    others = refs[step + 1 : step + pieces]
    refs = refs[step + pieces :]
    states, refs = refs[:step], refs[step:]
    rows, col, stack = refs[: step + 1], refs[step + 1], refs[step + 2]
    for state, row in zip(states, rows):
        row[...] = state[...]
    gram_body(owns, (owns[step],) + others, rows, col, stack, tile)


def gram_last_kernel(step, relatives, chunks, groups, tile, me_ref, *refs):
    pieces = len(relatives)
    owns = refs[: step + 1]
    others = refs[step + 1 : step + pieces]
    refs = refs[step + pieces :]
    states, refs = refs[:step], refs[step:]
    cols, refs = refs[:step], refs[step:]
    out_ref, stack, col, table = refs[:4]
    rows = refs[4:]
    for state, row in zip(states, rows):
        row[...] = state[...]
    gram_body(owns, (owns[step],) + others, rows, col, stack, tile)
    first = 0
    for k, size in enumerate(chunks):
        col_k = (cols[k] if k < step else col)[0:1, :]
        row_k = jnp.max(rows[k][...].T, axis=0, keepdims=True)
        count = groups * size
        for p, relative in enumerate(relatives):
            for r in range(groups):
                start = p * count + r * size
                best = col_k[:, start : start + size]
                if p == 0:
                    best = jnp.maximum(best, row_k[:, r * size : (r + 1) * size])
                row = r * pieces + p
                table[row : row + 1, first : first + size] = best
        first += size
    for r in range(groups):
        for p, relative in enumerate(relatives):
            row = r * pieces + p
            target = (me_ref[0] ^ r) * pieces + (me_ref[1] ^ relative)
            out_ref[pl.ds(target, 1), :] = table[row : row + 1, :]


def gram_step(step, me, owns, others, states, cols, relatives, chunks, groups):
    pieces = len(relatives)
    count, features = owns[step].shape
    total = pieces * count
    counts = [own.shape[0] for own in owns]
    tile = 256
    row_shapes = [(c, lanes) for c in counts]
    stack = pltpu.VMEM((total, features), jnp.bfloat16)
    params = dict(
        compiler_params=pltpu.CompilerParams(vmem_limit_bytes=24 * 2**20),
        cost_estimate=pl.CostEstimate(
            flops=2 * sum(counts) * total * features,
            bytes_accessed=2 * features * (sum(counts) + total),
            transcendentals=0,
        ),
    )
    if step < len(chunks) - 1:
        results = pl.pallas_call(
            functools.partial(gram_kernel, step, pieces, tile),
            in_specs=[vmem] * (step + pieces + step),
            out_specs=[vmem] * (step + 2),
            out_shape=[jax.ShapeDtypeStruct(s, jnp.float32) for s in row_shapes]
            + [jax.ShapeDtypeStruct((1, total), jnp.float32)],
            scratch_shapes=[stack],
            name="gram_step",
            **params,
        )(*owns, *others, *states)
        return list(results[:-1]), cols + [results[-1]]
    return pl.pallas_call(
        functools.partial(gram_last_kernel, step, relatives, chunks, groups, tile),
        in_specs=[smem] + [vmem] * (step + pieces + 2 * step),
        out_specs=vmem,
        out_shape=jax.ShapeDtypeStruct((groups * pieces, sum(chunks)), jnp.float32),
        scratch_shapes=[
            stack,
            pltpu.VMEM((1, total), jnp.float32),
            pltpu.VMEM((groups * pieces, sum(chunks)), jnp.float32),
        ]
        + [pltpu.VMEM(s, jnp.float32) for s in row_shapes],
        name="gram_last",
        **params,
    )(me, *owns, *others, *states, *cols)


def tail_kernel(capacity, members, slot_ref, part_ref, out_ref, table):
    groups = part_ref.shape[0] // members
    width = table.shape[1]
    table[...] = jnp.full(table.shape, sentinel, jnp.float32)
    for g in range(groups):
        table[g : g + 1, :capacity] = jnp.max(
            part_ref[g * members : (g + 1) * members, :], axis=0, keepdims=True
        )
    lane = lax.broadcasted_iota(jnp.int32, (lanes, lanes), 1)
    for q in range(out_ref.shape[0]):
        slot = jnp.broadcast_to(slot_ref[q : q + 1, :], (lanes, lanes)).T
        best = jnp.full((lanes, lanes), sentinel, jnp.float32)
        for g in range(groups):
            for c in range(0, width, lanes):
                entry = table[g : g + 1, c : c + lanes]
                best = jnp.maximum(
                    best, jnp.where(slot - (g * capacity + c) == lane, entry, sentinel)
                )
        out_ref[q : q + 1, :] = jnp.max(best.T, axis=0, keepdims=True)


def tail(partials, slots, capacity, members):
    groups = partials.shape[0] // members
    width = -(-capacity // lanes) * lanes
    return pl.pallas_call(
        functools.partial(tail_kernel, capacity, members),
        in_specs=[vmem, vmem],
        out_specs=vmem,
        out_shape=jax.ShapeDtypeStruct(slots.shape, jnp.float32),
        scratch_shapes=[pltpu.VMEM((groups, width), jnp.float32)],
        name="pick_rows",
    )(slots, partials)


def on_device(embeddings, send_slot):
    row_count, features = embeddings.shape
    groups = lax.axis_size("grp")
    members = lax.axis_size("blk")
    slot_count = 2 * row_count
    capacity = slot_count // groups
    chunks = chunk_sizes(capacity)
    me = jnp.stack([lax.axis_index("grp"), lax.axis_index("blk")]).astype(jnp.int32)
    slots = send_slot.reshape(row_count // lanes, lanes)
    placed = head(me, embeddings, slots, capacity, chunks, groups)
    owns, states, cols = [], [], []
    for step, size in enumerate(chunks):
        mine = placed[step * groups : (step + 1) * groups]
        arrived = {0: mine[0]}
        for r in reversed(range(1, groups)):
            arrived[r] = swap(mine[r], "grp", groups, r)
        own = jnp.concatenate([arrived[r] for r in range(groups)], axis=0)
        pieces, relatives = [own], [0]
        bit = members // 2
        while bit:
            pieces = pieces + [swap(piece, "blk", members, bit) for piece in pieces]
            relatives = relatives + [relative ^ bit for relative in relatives]
            bit //= 2
        owns.append(own)
        result = gram_step(
            step, me, owns, pieces[1:], states, cols, relatives, chunks, groups
        )
        if step < len(chunks) - 1:
            states, cols = result
    homeward = lax.all_to_all(result, ("grp", "blk"), 0, 0, tiled=True)
    return tail(homeward, slots, capacity, members).reshape(row_count)


def solution(mesh):
    in_specs = (P(("grp", "blk"), None), P(("grp", "blk")))
    out_specs = P(("grp", "blk"))
    return jax.shard_map(
        on_device, mesh=mesh, in_specs=in_specs, out_specs=out_specs, check_vma=False
    )
```

```python
import functools

import jax
import jax.numpy as jnp
from jax import lax
from jax.experimental import pallas as pl
from jax.experimental.pallas import tpu as pltpu
from jax.sharding import PartitionSpec as P

sentinel = -3.0
epsilon = 1e-06
dead_mark = 2.0
dead_bias = -8.0
lanes = 128
smem = pl.BlockSpec(memory_space=pltpu.SMEM)
vmem = pl.BlockSpec(memory_space=pltpu.VMEM)


def chunk_sizes(capacity):
    count = 4 if capacity % 64 == 0 else 3
    return (capacity // count,) * count


def after(value, *earlier):
    return lax.optimization_barrier((value,) + earlier)[0]


def swap(value, axis, size, bit):
    return lax.ppermute(value, axis, [(i, i ^ bit) for i in range(size)])


def head_kernel(capacity, chunks, groups, me_ref, slot_ref, x_ref, *out_refs):
    wide = x_ref[...].astype(jnp.float32)
    normed = (
        wide * lax.rsqrt(jnp.sum(wide * wide, axis=-1, keepdims=True) + epsilon)
    ).astype(jnp.bfloat16)
    slots = jnp.concatenate([slot_ref[q : q + 1, :] for q in range(slot_ref.shape[0])], axis=1)
    first, high = 0, groups // 2
    for step, size in enumerate(chunks):
        place = lax.broadcasted_iota(jnp.int32, (groups, size, 1), 1)
        order = lax.broadcasted_iota(jnp.int32, (groups, size, 1), 0)
        group = (order % high * 2 + order // high) ^ me_ref[0]
        wanted = (group * capacity + place + first).reshape(groups * size, 1)
        pick = jnp.where(wanted == slots, 1.0, 0.0)
        live = jnp.max(pick, axis=1, keepdims=True)
        placed = jnp.dot(pick.astype(jnp.bfloat16), normed, preferred_element_type=jnp.float32)
        lane = lax.broadcasted_iota(jnp.int32, (1, placed.shape[1]), 1)
        mark = jnp.where(lane == 0, dead_mark, 0.0)
        placed = (placed + (1.0 - live) * mark).astype(jnp.bfloat16)
        out_refs[2 * step][...] = placed[: high * size, :]
        out_refs[2 * step + 1][...] = placed[high * size :, :]
        first += size


def head(me, embeddings, slots, capacity, chunks, groups):
    rows, features = embeddings.shape
    return pl.pallas_call(
        functools.partial(head_kernel, capacity, chunks, groups),
        in_specs=[smem, vmem, vmem],
        out_specs=[vmem] * (2 * len(chunks)),
        out_shape=[
            jax.ShapeDtypeStruct((groups // 2 * size, features), jnp.bfloat16)
            for size in chunks
            for _ in range(2)
        ],
        compiler_params=pltpu.CompilerParams(vmem_limit_bytes=32 * 2**20),
        name="place_rows",
    )(me, slots, embeddings)


def lane_fold(values):
    best = values[:, :lanes]
    for start in range(lanes, values.shape[1], lanes):
        best = jnp.maximum(best, values[:, start : start + lanes])
    return best


def gram_body(own_refs, piece_refs, row_refs, col_ref, stack, tile):
    step = len(own_refs) - 1
    start = 0
    for piece_ref in piece_refs:
        stack[start : start + piece_ref.shape[0], :] = piece_ref[...]
        start += piece_ref.shape[0]
    row_refs[step][...] = jnp.full(row_refs[step].shape, sentinel, jnp.float32)
    nt = (((1,), (1,)), ((), ()))

    @pl.loop(0, stack.shape[0] // tile)
    def _(n):
        first = pl.multiple_of(n * tile, tile)
        x = stack[pl.ds(first, tile), :]
        marks = x[:, :lanes].astype(jnp.float32).T[0:1, :]
        col_bias = jnp.where(marks > 1.5, dead_bias, 0.0)
        col_best = jnp.full((1, tile), sentinel, jnp.float32)
        for j in range(step + 1):
            own = own_refs[j][...]
            scores = lax.dot_general(own, x, nt, preferred_element_type=jnp.float32)
            usable = scores + col_bias
            if j == step:
                rows = lax.broadcasted_iota(jnp.int32, usable.shape, 0)
                cols = lax.broadcasted_iota(jnp.int32, usable.shape, 1)
                usable = jnp.where(rows - cols == first, dead_bias, usable)
            else:
                row_bias = jnp.where(own[:, 0:1].astype(jnp.float32) > 1.5, dead_bias, 0.0)
                col_best = jnp.maximum(
                    col_best, jnp.max(scores + row_bias, axis=0, keepdims=True)
                )
            row_refs[j][...] = jnp.maximum(row_refs[j][...], lane_fold(usable))
        col_ref[0:1, pl.ds(first, tile)] = col_best


def gram_kernel(step, tile, *refs):
    owns, pieces, refs = refs[: step + 1], refs[step + 1 : step + 3], refs[step + 3 :]
    states, refs = refs[:step], refs[step:]
    rows, col, stack = refs[: step + 1], refs[step + 1], refs[step + 2]
    for state, row in zip(states, rows):
        row[...] = state[...]
    gram_body(owns, pieces, rows, col, stack, tile)


def gram_last_kernel(step, relatives, chunks, groups, tile, me_ref, *refs):
    members = len(relatives)
    owns, pieces, refs = refs[: step + 1], refs[step + 1 : step + 3], refs[step + 3 :]
    states, refs = refs[:step], refs[step:]
    cols, refs = refs[:step], refs[step:]
    out_ref, stack, col, table = refs[:4]
    rows = refs[4:]
    for state, row in zip(states, rows):
        row[...] = state[...]
    gram_body(owns, pieces, rows, col, stack, tile)
    first = 0
    for k, size in enumerate(chunks):
        col_k = (cols[k] if k < step else col)[0:1, :]
        row_k = jnp.max(rows[k][...].T, axis=0, keepdims=True)
        count = groups * size
        for p, relative in enumerate(relatives):
            for r in range(groups):
                start = p * count + r * size
                best = col_k[:, start : start + size]
                if p == 0:
                    best = jnp.maximum(best, row_k[:, r * size : (r + 1) * size])
                row = r * members + p
                table[row : row + 1, first : first + size] = best
        first += size
    for r in range(groups):
        for p, relative in enumerate(relatives):
            row = r * members + p
            target = (me_ref[0] ^ r) * members + (me_ref[1] ^ relative)
            out_ref[pl.ds(target, 1), :] = table[row : row + 1, :]


def gram_step(step, me, owns, pieces, states, cols, relatives, chunks, groups):
    members = len(relatives)
    features = owns[step].shape[1]
    total = members * owns[step].shape[0]
    counts = [own.shape[0] for own in owns]
    tile = 256
    row_shapes = [(c, lanes) for c in counts]
    stack = pltpu.VMEM((total, features), jnp.bfloat16)
    params = dict(
        compiler_params=pltpu.CompilerParams(vmem_limit_bytes=24 * 2**20),
        cost_estimate=pl.CostEstimate(
            flops=2 * sum(counts) * total * features,
            bytes_accessed=2 * features * (sum(counts) + total),
            transcendentals=0,
        ),
    )
    if step < len(chunks) - 1:
        results = pl.pallas_call(
            functools.partial(gram_kernel, step, tile),
            in_specs=[vmem] * (step + 3 + step),
            out_specs=[vmem] * (step + 2),
            out_shape=[jax.ShapeDtypeStruct(s, jnp.float32) for s in row_shapes]
            + [jax.ShapeDtypeStruct((1, total), jnp.float32)],
            scratch_shapes=[stack],
            name="gram_step",
            **params,
        )(*owns, *pieces, *states)
        return list(results[:-1]), cols + [results[-1]]
    return pl.pallas_call(
        functools.partial(gram_last_kernel, step, relatives, chunks, groups, tile),
        in_specs=[smem] + [vmem] * (step + 3 + 2 * step),
        out_specs=vmem,
        out_shape=jax.ShapeDtypeStruct((groups * members, sum(chunks)), jnp.float32),
        scratch_shapes=[
            stack,
            pltpu.VMEM((1, total), jnp.float32),
            pltpu.VMEM((groups * members, sum(chunks)), jnp.float32),
        ]
        + [pltpu.VMEM(s, jnp.float32) for s in row_shapes],
        name="gram_last",
        **params,
    )(me, *owns, *pieces, *states, *cols)


def tail_kernel(capacity, members, slot_ref, part_ref, out_ref, table):
    groups = part_ref.shape[0] // members
    width = table.shape[1]
    table[...] = jnp.full(table.shape, sentinel, jnp.float32)
    for g in range(groups):
        table[g : g + 1, :capacity] = jnp.max(
            part_ref[g * members : (g + 1) * members, :], axis=0, keepdims=True
        )
    lane = lax.broadcasted_iota(jnp.int32, (lanes, lanes), 1)
    for q in range(out_ref.shape[0]):
        slot = jnp.broadcast_to(slot_ref[q : q + 1, :], (lanes, lanes)).T
        best = jnp.full((lanes, lanes), sentinel, jnp.float32)
        for g in range(groups):
            for c in range(0, width, lanes):
                entry = table[g : g + 1, c : c + lanes]
                best = jnp.maximum(
                    best, jnp.where(slot - (g * capacity + c) == lane, entry, sentinel)
                )
        out_ref[q : q + 1, :] = jnp.max(best.T, axis=0, keepdims=True)


def tail(partials, slots, capacity, members):
    groups = partials.shape[0] // members
    width = -(-capacity // lanes) * lanes
    return pl.pallas_call(
        functools.partial(tail_kernel, capacity, members),
        in_specs=[vmem, vmem],
        out_specs=vmem,
        out_shape=jax.ShapeDtypeStruct(slots.shape, jnp.float32),
        scratch_shapes=[pltpu.VMEM((groups, width), jnp.float32)],
        name="pick_rows",
    )(slots, partials)


def on_device(embeddings, send_slot):
    row_count, features = embeddings.shape
    groups = lax.axis_size("grp")
    members = lax.axis_size("blk")
    slot_count = 2 * row_count
    capacity = slot_count // groups
    chunks = chunk_sizes(capacity)
    me = jnp.stack([lax.axis_index("grp"), lax.axis_index("blk")]).astype(jnp.int32)
    slots = send_slot.reshape(row_count // lanes, lanes)
    placed = head(me, embeddings, slots, capacity, chunks, groups)
    high = groups // 2
    near, owns, across, done, states, cols = [], [], [], [], [], []
    for step, size in enumerate(chunks):
        keep, send = placed[2 * step : 2 * step + 2]
        near.append(swap(after(send, *near[: max(step - 1, 0)][-1:]), "grp", groups, 1))
        arrived = []
        for z in range(high):
            span = slice(z * size, (z + 1) * size)
            pair = jnp.concatenate([keep[span], near[step][span]], axis=0)
            if z > 0:
                earlier = owns[step - 2 : step - 1] if step >= 2 else []
                earlier = earlier + (across[step - 3 : step - 2] if step >= 3 else [])
                pair = swap(after(pair, *earlier), "grp", groups, 2 * z)
            arrived.append(pair)
        own = jnp.concatenate(arrived, axis=0)
        owns.append(own)
        earlier = done[step - 2 : step - 1] if step >= 2 else []
        across.append(swap(after(own, *earlier), "blk", members, 2))
        pair = jnp.concatenate([own, across[step]], axis=0)
        other = swap(pair, "blk", members, 1)
        result = gram_step(
            step, me, owns, (pair, other), states, cols, (0, 2, 1, 3), chunks, groups
        )
        if step < len(chunks) - 1:
            states, cols = result
            done.append(cols[-1])
    homeward = lax.all_to_all(result, ("grp", "blk"), 0, 0, tiled=True)
    return tail(homeward, slots, capacity, members).reshape(row_count)


def solution(mesh):
    in_specs = (P(("grp", "blk"), None), P(("grp", "blk")))
    out_specs = P(("grp", "blk"))
    return jax.shard_map(
        on_device, mesh=mesh, in_specs=in_specs, out_specs=out_specs, check_vma=False
    )
```

```python
import functools

import jax
import jax.numpy as jnp
from jax import lax
from jax.experimental import pallas as pl
from jax.experimental.pallas import tpu as pltpu
from jax.sharding import PartitionSpec as P

sentinel = -3.0
epsilon = 1e-06
dead_mark = 2.0
dead_bias = -8.0
lanes = 128
smem = pl.BlockSpec(memory_space=pltpu.SMEM)
vmem = pl.BlockSpec(memory_space=pltpu.VMEM)


def chunk_sizes(capacity):
    count = 4 if capacity % 64 == 0 else 3
    return (capacity // count,) * count


def after(value, *earlier):
    return lax.optimization_barrier((value,) + earlier)[0]


def swap(value, axis, size, bit):
    return lax.ppermute(value, axis, [(i, i ^ bit) for i in range(size)])


def head_kernel(capacity, chunks, groups, me_ref, slot_ref, x_ref, *out_refs):
    wide = x_ref[...].astype(jnp.float32)
    normed = (
        wide * lax.rsqrt(jnp.sum(wide * wide, axis=-1, keepdims=True) + epsilon)
    ).astype(jnp.bfloat16)
    slots = jnp.concatenate([slot_ref[q : q + 1, :] for q in range(slot_ref.shape[0])], axis=1)
    first, high = 0, groups // 2
    for step, size in enumerate(chunks):
        place = lax.broadcasted_iota(jnp.int32, (groups, size, 1), 1)
        order = lax.broadcasted_iota(jnp.int32, (groups, size, 1), 0)
        relative = order if step == 0 else order % high * 2 + order // high
        group = relative ^ me_ref[0]
        wanted = (group * capacity + place + first).reshape(groups * size, 1)
        pick = jnp.where(wanted == slots, 1.0, 0.0)
        live = jnp.max(pick, axis=1, keepdims=True)
        placed = jnp.dot(pick.astype(jnp.bfloat16), normed, preferred_element_type=jnp.float32)
        lane = lax.broadcasted_iota(jnp.int32, (1, placed.shape[1]), 1)
        mark = jnp.where(lane == 0, dead_mark, 0.0)
        placed = (placed + (1.0 - live) * mark).astype(jnp.bfloat16)
        out_refs[2 * step][...] = placed[: high * size, :]
        out_refs[2 * step + 1][...] = placed[high * size :, :]
        first += size


def head(me, embeddings, slots, capacity, chunks, groups):
    rows, features = embeddings.shape
    return pl.pallas_call(
        functools.partial(head_kernel, capacity, chunks, groups),
        in_specs=[smem, vmem, vmem],
        out_specs=[vmem] * (2 * len(chunks)),
        out_shape=[
            jax.ShapeDtypeStruct((groups // 2 * size, features), jnp.bfloat16)
            for size in chunks
            for _ in range(2)
        ],
        compiler_params=pltpu.CompilerParams(vmem_limit_bytes=32 * 2**20),
        name="place_rows",
    )(me, slots, embeddings)


def lane_fold(values):
    best = values[:, :lanes]
    for start in range(lanes, values.shape[1], lanes):
        best = jnp.maximum(best, values[:, start : start + lanes])
    return best


def gram_body(own_refs, piece_refs, row_refs, col_ref, stack, tile):
    step = len(own_refs) - 1
    start = 0
    for piece_ref in piece_refs:
        stack[start : start + piece_ref.shape[0], :] = piece_ref[...]
        start += piece_ref.shape[0]
    row_refs[step][...] = jnp.full(row_refs[step].shape, sentinel, jnp.float32)
    nt = (((1,), (1,)), ((), ()))

    @pl.loop(0, stack.shape[0] // tile)
    def _(n):
        first = pl.multiple_of(n * tile, tile)
        x = stack[pl.ds(first, tile), :]
        marks = x[:, :lanes].astype(jnp.float32).T[0:1, :]
        col_bias = jnp.where(marks > 1.5, dead_bias, 0.0)
        col_best = jnp.full((1, tile), sentinel, jnp.float32)
        for j in range(step + 1):
            own = own_refs[j][...]
            scores = lax.dot_general(own, x, nt, preferred_element_type=jnp.float32)
            usable = scores + col_bias
            if j == step:
                rows = lax.broadcasted_iota(jnp.int32, usable.shape, 0)
                cols = lax.broadcasted_iota(jnp.int32, usable.shape, 1)
                usable = jnp.where(rows - cols == first, dead_bias, usable)
            else:
                row_bias = jnp.where(own[:, 0:1].astype(jnp.float32) > 1.5, dead_bias, 0.0)
                col_best = jnp.maximum(
                    col_best, jnp.max(scores + row_bias, axis=0, keepdims=True)
                )
            row_refs[j][...] = jnp.maximum(row_refs[j][...], lane_fold(usable))
        col_ref[0:1, pl.ds(first, tile)] = col_best


def gram_kernel(step, tile, *refs):
    owns, pieces, refs = refs[: step + 1], refs[step + 1 : step + 3], refs[step + 3 :]
    states, refs = refs[:step], refs[step:]
    rows, col, stack = refs[: step + 1], refs[step + 1], refs[step + 2]
    for state, row in zip(states, rows):
        row[...] = state[...]
    gram_body(owns, pieces, rows, col, stack, tile)


def gram_last_kernel(step, relatives, chunks, groups, tile, me_ref, *refs):
    members = len(relatives)
    owns, pieces, refs = refs[: step + 1], refs[step + 1 : step + 3], refs[step + 3 :]
    states, refs = refs[:step], refs[step:]
    cols, refs = refs[:step], refs[step:]
    out_ref, stack, col, table = refs[:4]
    rows = refs[4:]
    for state, row in zip(states, rows):
        row[...] = state[...]
    gram_body(owns, pieces, rows, col, stack, tile)
    first = 0
    for k, size in enumerate(chunks):
        col_k = (cols[k] if k < step else col)[0:1, :]
        row_k = jnp.max(rows[k][...].T, axis=0, keepdims=True)
        count = groups * size
        for p, relative in enumerate(relatives):
            for r in range(groups):
                start = p * count + r * size
                best = col_k[:, start : start + size]
                if p == 0:
                    best = jnp.maximum(best, row_k[:, r * size : (r + 1) * size])
                row = r * members + p
                table[row : row + 1, first : first + size] = best
        first += size
    for r in range(groups):
        for p, relative in enumerate(relatives):
            row = r * members + p
            target = (me_ref[0] ^ r) * members + (me_ref[1] ^ relative)
            out_ref[pl.ds(target, 1), :] = table[row : row + 1, :]


def gram_step(step, me, owns, pieces, states, cols, relatives, chunks, groups):
    members = len(relatives)
    features = owns[step].shape[1]
    total = members * owns[step].shape[0]
    counts = [own.shape[0] for own in owns]
    tile = 256
    row_shapes = [(c, lanes) for c in counts]
    stack = pltpu.VMEM((total, features), jnp.bfloat16)
    params = dict(
        compiler_params=pltpu.CompilerParams(vmem_limit_bytes=24 * 2**20),
        cost_estimate=pl.CostEstimate(
            flops=2 * sum(counts) * total * features,
            bytes_accessed=2 * features * (sum(counts) + total),
            transcendentals=0,
        ),
    )
    if step < len(chunks) - 1:
        results = pl.pallas_call(
            functools.partial(gram_kernel, step, tile),
            in_specs=[vmem] * (step + 3 + step),
            out_specs=[vmem] * (step + 2),
            out_shape=[jax.ShapeDtypeStruct(s, jnp.float32) for s in row_shapes]
            + [jax.ShapeDtypeStruct((1, total), jnp.float32)],
            scratch_shapes=[stack],
            name="gram_step",
            **params,
        )(*owns, *pieces, *states)
        return list(results[:-1]), cols + [results[-1]]
    return pl.pallas_call(
        functools.partial(gram_last_kernel, step, relatives, chunks, groups, tile),
        in_specs=[smem] + [vmem] * (step + 3 + 2 * step),
        out_specs=vmem,
        out_shape=jax.ShapeDtypeStruct((groups * members, sum(chunks)), jnp.float32),
        scratch_shapes=[
            stack,
            pltpu.VMEM((1, total), jnp.float32),
            pltpu.VMEM((groups * members, sum(chunks)), jnp.float32),
        ]
        + [pltpu.VMEM(s, jnp.float32) for s in row_shapes],
        name="gram_last",
        **params,
    )(me, *owns, *pieces, *states, *cols)


def tail_kernel(capacity, members, slot_ref, part_ref, out_ref, table):
    groups = part_ref.shape[0] // members
    width = table.shape[1]
    table[...] = jnp.full(table.shape, sentinel, jnp.float32)
    for g in range(groups):
        table[g : g + 1, :capacity] = jnp.max(
            part_ref[g * members : (g + 1) * members, :], axis=0, keepdims=True
        )
    lane = lax.broadcasted_iota(jnp.int32, (lanes, lanes), 1)
    for q in range(out_ref.shape[0]):
        slot = jnp.broadcast_to(slot_ref[q : q + 1, :], (lanes, lanes)).T
        best = jnp.full((lanes, lanes), sentinel, jnp.float32)
        for g in range(groups):
            for c in range(0, width, lanes):
                entry = table[g : g + 1, c : c + lanes]
                best = jnp.maximum(
                    best, jnp.where(slot - (g * capacity + c) == lane, entry, sentinel)
                )
        out_ref[q : q + 1, :] = jnp.max(best.T, axis=0, keepdims=True)


def tail(partials, slots, capacity, members):
    groups = partials.shape[0] // members
    width = -(-capacity // lanes) * lanes
    return pl.pallas_call(
        functools.partial(tail_kernel, capacity, members),
        in_specs=[vmem, vmem],
        out_specs=vmem,
        out_shape=jax.ShapeDtypeStruct(slots.shape, jnp.float32),
        scratch_shapes=[pltpu.VMEM((groups, width), jnp.float32)],
        name="pick_rows",
    )(slots, partials)


def on_device(embeddings, send_slot):
    row_count, features = embeddings.shape
    groups = lax.axis_size("grp")
    members = lax.axis_size("blk")
    slot_count = 2 * row_count
    capacity = slot_count // groups
    chunks = chunk_sizes(capacity)
    me = jnp.stack([lax.axis_index("grp"), lax.axis_index("blk")]).astype(jnp.int32)
    slots = send_slot.reshape(row_count // lanes, lanes)
    placed = head(me, embeddings, slots, capacity, chunks, groups)
    count, high = len(chunks), groups // 2
    last = count - 1

    sent, owns, done, states, cols = {}, {}, {}, [], []
    pairs, window = {}, []

    def send(key, value, axis, size, bit, *earlier):
        earlier = earlier + tuple(window[-5:-4])
        sent[key] = swap(after(value, *earlier) if earlier else value, axis, size, bit)
        window.append(sent[key])

    def rows(value, index, size):
        return value[index * size : (index + 1) * size]

    def block(step, z):
        size = chunks[step]
        return jnp.concatenate(
            [rows(placed[2 * step], z, size), rows(sent["y", step], z, size)], axis=0
        )

    def start(kind, step, bit=0):
        size = chunks[step]
        if kind == "d":
            value = rows(placed[2 * bit // groups], bit % high, size)
            send((kind, step, bit), value, "grp", groups, bit)
        elif kind == "y":
            send((kind, step), placed[2 * step + 1], "grp", groups, 1)
        elif kind == "z":
            send((kind, step, bit), block(step, bit), "grp", groups, 2 * bit)
        elif kind == "x":
            if step == 0:
                parts = [rows(placed[0], 0, size)]
                parts += [sent["d", 0, r] for r in range(1, groups)]
            else:
                parts = [block(step, 0)] + [sent["z", step, z] for z in range(1, high)]
            owns[step] = jnp.concatenate(parts, axis=0)
            earlier = [sent["x", step - 1]] if step >= 1 else []
            earlier += [done[step - 2]] if step >= 2 else []
            send((kind, step), owns[step], "blk", members, 2, *earlier)
        elif kind == "c":
            pairs[step] = jnp.concatenate([owns[step], sent["x", step]], axis=0)
            earlier = [done[step - 1]] if step == last else []
            send((kind, step), pairs[step], "blk", members, 1, *earlier)

    def gram(step):
        nonlocal states, cols
        result = gram_step(
            step,
            me,
            [owns[j] for j in range(step + 1)],
            (pairs[step], sent["c", step]),
            states,
            cols,
            (0, 2, 1, 3),
            chunks,
            groups,
        )
        if step == last:
            return result
        states, cols = result
        done[step] = cols[-1]

    direct = [("d", 0, r) for r in reversed(range(1, groups))]
    order = direct[:4] + [("y", 1)] + direct[4:]
    for step in range(1, count):
        stages = [("z", step, z) for z in reversed(range(1, high))]
        order += stages[:2] + ([("y", step + 1)] if step < last else [])
        order += [("x", step - 1)] + stages[2:]
        order += [("c", step - 1), ("gram", step - 1)]
    order += [("x", last), ("c", last)]
    for item in order:
        if item[0] == "gram":
            gram(item[1])
        else:
            start(*item)
    result = gram(last)
    homeward = lax.all_to_all(result, ("grp", "blk"), 0, 0, tiled=True)
    return tail(homeward, slots, capacity, members).reshape(row_count)


def solution(mesh):
    in_specs = (P(("grp", "blk"), None), P(("grp", "blk")))
    out_specs = P(("grp", "blk"))
    return jax.shard_map(
        on_device, mesh=mesh, in_specs=in_specs, out_specs=out_specs, check_vma=False
    )
```

```python
import functools

import jax
import jax.numpy as jnp
from jax import lax
from jax.experimental import pallas as pl
from jax.experimental.pallas import tpu as pltpu
from jax.sharding import PartitionSpec as P

sentinel = -3.0
epsilon = 1e-06
dead_mark = 2.0
dead_bias = -8.0
lanes = 128
smem = pl.BlockSpec(memory_space=pltpu.SMEM)
vmem = pl.BlockSpec(memory_space=pltpu.VMEM)


def chunk_sizes(capacity):
    return (capacity // 3,) * 3


def after(value, *earlier):
    return lax.optimization_barrier((value,) + earlier)[0]


def swap(value, axis, size, bit):
    return lax.ppermute(value, axis, [(i, i ^ bit) for i in range(size)])


def head_kernel(capacity, chunks, groups, me_ref, slot_ref, x_ref, *out_refs):
    wide = x_ref[...].astype(jnp.float32)
    normed = (
        wide * lax.rsqrt(jnp.sum(wide * wide, axis=-1, keepdims=True) + epsilon)
    ).astype(jnp.bfloat16)
    slots = jnp.concatenate([slot_ref[q : q + 1, :] for q in range(slot_ref.shape[0])], axis=1)
    first, high = 0, groups // 2
    for step, size in enumerate(chunks):
        place = lax.broadcasted_iota(jnp.int32, (groups, size, 1), 1)
        order = lax.broadcasted_iota(jnp.int32, (groups, size, 1), 0)
        group = (order % high * 2 + order // high) ^ me_ref[0]
        wanted = (group * capacity + place + first).reshape(groups * size, 1)
        pick = jnp.where(wanted == slots, 1.0, 0.0)
        live = jnp.max(pick, axis=1, keepdims=True)
        placed = jnp.dot(pick.astype(jnp.bfloat16), normed, preferred_element_type=jnp.float32)
        lane = lax.broadcasted_iota(jnp.int32, (1, placed.shape[1]), 1)
        mark = jnp.where(lane == 0, dead_mark, 0.0)
        placed = (placed + (1.0 - live) * mark).astype(jnp.bfloat16)
        out_refs[2 * step][...] = placed[: high * size, :]
        out_refs[2 * step + 1][...] = placed[high * size :, :]
        first += size


def head(me, embeddings, slots, capacity, chunks, groups):
    rows, features = embeddings.shape
    return pl.pallas_call(
        functools.partial(head_kernel, capacity, chunks, groups),
        in_specs=[smem, vmem, vmem],
        out_specs=[vmem] * (2 * len(chunks)),
        out_shape=[
            jax.ShapeDtypeStruct((groups // 2 * size, features), jnp.bfloat16)
            for size in chunks
            for _ in range(2)
        ],
        compiler_params=pltpu.CompilerParams(vmem_limit_bytes=32 * 2**20),
        name="place_rows",
    )(me, slots, embeddings)


def lane_fold(values):
    best = values[:, :lanes]
    for start in range(lanes, values.shape[1], lanes):
        best = jnp.maximum(best, values[:, start : start + lanes])
    return best


def gram_body(own_refs, piece_refs, row_refs, col_ref, stack, tile):
    step = len(own_refs) - 1
    start = 0
    for piece_ref in piece_refs:
        stack[start : start + piece_ref.shape[0], :] = piece_ref[...]
        start += piece_ref.shape[0]
    row_refs[step][...] = jnp.full(row_refs[step].shape, sentinel, jnp.float32)
    nt = (((1,), (1,)), ((), ()))

    @pl.loop(0, stack.shape[0] // tile)
    def _(n):
        first = pl.multiple_of(n * tile, tile)
        x = stack[pl.ds(first, tile), :]
        marks = x[:, :lanes].astype(jnp.float32).T[0:1, :]
        col_bias = jnp.where(marks > 1.5, dead_bias, 0.0)
        col_best = jnp.full((1, tile), sentinel, jnp.float32)
        for j in range(step + 1):
            own = own_refs[j][...]
            scores = lax.dot_general(own, x, nt, preferred_element_type=jnp.float32)
            usable = scores + col_bias
            if j == step:
                rows = lax.broadcasted_iota(jnp.int32, usable.shape, 0)
                cols = lax.broadcasted_iota(jnp.int32, usable.shape, 1)
                usable = jnp.where(rows - cols == first, dead_bias, usable)
            else:
                row_bias = jnp.where(own[:, 0:1].astype(jnp.float32) > 1.5, dead_bias, 0.0)
                col_best = jnp.maximum(
                    col_best, jnp.max(scores + row_bias, axis=0, keepdims=True)
                )
            row_refs[j][...] = jnp.maximum(row_refs[j][...], lane_fold(usable))
        col_ref[0:1, pl.ds(first, tile)] = col_best


def gram_kernel(step, tile, *refs):
    owns, pieces, refs = refs[: step + 1], refs[step + 1 : step + 3], refs[step + 3 :]
    states, refs = refs[:step], refs[step:]
    rows, col, stack = refs[: step + 1], refs[step + 1], refs[step + 2]
    for state, row in zip(states, rows):
        row[...] = state[...]
    gram_body(owns, pieces, rows, col, stack, tile)


def gram_last_kernel(step, relatives, chunks, groups, tile, me_ref, *refs):
    members = len(relatives)
    owns, pieces, refs = refs[: step + 1], refs[step + 1 : step + 3], refs[step + 3 :]
    states, refs = refs[:step], refs[step:]
    cols, refs = refs[:step], refs[step:]
    out_ref, stack, col, table = refs[:4]
    rows = refs[4:]
    for state, row in zip(states, rows):
        row[...] = state[...]
    gram_body(owns, pieces, rows, col, stack, tile)
    first = 0
    for k, size in enumerate(chunks):
        col_k = (cols[k] if k < step else col)[0:1, :]
        row_k = jnp.max(rows[k][...].T, axis=0, keepdims=True)
        count = groups * size
        for p, relative in enumerate(relatives):
            for r in range(groups):
                start = p * count + r * size
                best = col_k[:, start : start + size]
                if p == 0:
                    best = jnp.maximum(best, row_k[:, r * size : (r + 1) * size])
                row = r * members + p
                table[row : row + 1, first : first + size] = best
        first += size
    for r in range(groups):
        for p, relative in enumerate(relatives):
            row = r * members + p
            target = (me_ref[0] ^ r) * members + (me_ref[1] ^ relative)
            out_ref[pl.ds(target, 1), :] = table[row : row + 1, :]


def gram_step(step, me, owns, pieces, states, cols, relatives, chunks, groups):
    members = len(relatives)
    features = owns[step].shape[1]
    total = members * owns[step].shape[0]
    counts = [own.shape[0] for own in owns]
    tile = 256
    row_shapes = [(c, lanes) for c in counts]
    stack = pltpu.VMEM((total, features), jnp.bfloat16)
    params = dict(
        compiler_params=pltpu.CompilerParams(vmem_limit_bytes=24 * 2**20),
        cost_estimate=pl.CostEstimate(
            flops=2 * sum(counts) * total * features,
            bytes_accessed=2 * features * (sum(counts) + total),
            transcendentals=0,
        ),
    )
    if step < len(chunks) - 1:
        results = pl.pallas_call(
            functools.partial(gram_kernel, step, tile),
            in_specs=[vmem] * (step + 3 + step),
            out_specs=[vmem] * (step + 2),
            out_shape=[jax.ShapeDtypeStruct(s, jnp.float32) for s in row_shapes]
            + [jax.ShapeDtypeStruct((1, total), jnp.float32)],
            scratch_shapes=[stack],
            name="gram_step",
            **params,
        )(*owns, *pieces, *states)
        return list(results[:-1]), cols + [results[-1]]
    return pl.pallas_call(
        functools.partial(gram_last_kernel, step, relatives, chunks, groups, tile),
        in_specs=[smem] + [vmem] * (step + 3 + 2 * step),
        out_specs=vmem,
        out_shape=jax.ShapeDtypeStruct((groups * members, sum(chunks)), jnp.float32),
        scratch_shapes=[
            stack,
            pltpu.VMEM((1, total), jnp.float32),
            pltpu.VMEM((groups * members, sum(chunks)), jnp.float32),
        ]
        + [pltpu.VMEM(s, jnp.float32) for s in row_shapes],
        name="gram_last",
        **params,
    )(me, *owns, *pieces, *states, *cols)


def tail_kernel(capacity, members, slot_ref, part_ref, out_ref, table):
    groups = part_ref.shape[0] // members
    width = table.shape[1]
    table[...] = jnp.full(table.shape, sentinel, jnp.float32)
    for g in range(groups):
        table[g : g + 1, :capacity] = jnp.max(
            part_ref[g * members : (g + 1) * members, :], axis=0, keepdims=True
        )
    lane = lax.broadcasted_iota(jnp.int32, (lanes, lanes), 1)
    for q in range(out_ref.shape[0]):
        slot = jnp.broadcast_to(slot_ref[q : q + 1, :], (lanes, lanes)).T
        best = jnp.full((lanes, lanes), sentinel, jnp.float32)
        for g in range(groups):
            for c in range(0, width, lanes):
                entry = table[g : g + 1, c : c + lanes]
                best = jnp.maximum(
                    best, jnp.where(slot - (g * capacity + c) == lane, entry, sentinel)
                )
        out_ref[q : q + 1, :] = jnp.max(best.T, axis=0, keepdims=True)


def tail(partials, slots, capacity, members):
    groups = partials.shape[0] // members
    width = -(-capacity // lanes) * lanes
    return pl.pallas_call(
        functools.partial(tail_kernel, capacity, members),
        in_specs=[vmem, vmem],
        out_specs=vmem,
        out_shape=jax.ShapeDtypeStruct(slots.shape, jnp.float32),
        scratch_shapes=[pltpu.VMEM((groups, width), jnp.float32)],
        name="pick_rows",
    )(slots, partials)


def on_device(embeddings, send_slot):
    row_count, features = embeddings.shape
    groups = lax.axis_size("grp")
    members = lax.axis_size("blk")
    slot_count = 2 * row_count
    capacity = slot_count // groups
    chunks = chunk_sizes(capacity)
    me = jnp.stack([lax.axis_index("grp"), lax.axis_index("blk")]).astype(jnp.int32)
    slots = send_slot.reshape(row_count // lanes, lanes)
    placed = head(me, embeddings, slots, capacity, chunks, groups)
    count, high = len(chunks), groups // 2
    last = count - 1

    sent, owns, done, states, cols, pairs = {}, {}, {}, [], [], {}

    def rows(value, index, size):
        return value[index * size : (index + 1) * size]

    def block(step, z):
        size = chunks[step]
        return jnp.concatenate(
            [rows(placed[2 * step], z, size), rows(sent["y", step], z, size)], axis=0
        )

    def send(key, value, axis, size, bit, *earlier):
        held = [sent[name] for name in earlier if name in sent]
        held += [done[name[1]] for name in earlier if name[0] == "gram" and name[1] in done]
        sent[key] = swap(after(value, *held) if held else value, axis, size, bit)

    def send_y(step):
        if step < count:
            send(("y", step), placed[2 * step + 1], "grp", groups, 1, ("y", step - 1))

    def send_z(step, z):
        early = [("z", step - 1, z)]
        if z == high - 1:
            early += [("x", step - 2, 0)]
        send(("z", step, z), block(step, z), "grp", groups, 2 * z, *early)

    def send_x(step):
        parts = [block(step, 0)] + [sent["z", step, z] for z in range(1, high)]
        owns[step] = jnp.concatenate(parts, axis=0)
        cuts = 1 if step == 0 else 2
        half = owns[step].shape[0] // cuts
        for cut in range(cuts):
            early = [("x", step - 1, 0), ("x", step - 1, 1)] if cut == 0 else [("gram", step - 1)]
            value = rows(owns[step], cut, half)
            send(("x", step, cut), value, "blk", members, 2, *early)
            if cut == 0 and step >= 1:
                gram(step - 1)

    def gram(step):
        nonlocal states, cols
        across = [sent[name] for name in sent if name[:2] == ("x", step)]
        pairs[step] = jnp.concatenate([owns[step]] + across, axis=0)
        send(("c", step), pairs[step], "blk", members, 1)
        result = gram_step(
            step,
            me,
            [owns[j] for j in range(step + 1)],
            (pairs[step], sent["c", step]),
            states,
            cols,
            (0, 2, 1, 3),
            chunks,
            groups,
        )
        if step == last:
            return result
        states, cols = result
        done[step] = cols[-1]

    far = [high // 2] + [z for z in reversed(range(1, high)) if z != high // 2]
    send_y(0)
    for z in far[:2]:
        send_z(0, z)
    send_y(1)
    for z in far[2:]:
        send_z(0, z)
    for step in range(1, count):
        for z in far[:2]:
            send_z(step, z)
        send_x(step - 1)
        for z in far[2:]:
            send_z(step, z)
        send_y(step + 1)
    send_x(last)
    result = gram(last)
    homeward = lax.all_to_all(result, ("grp", "blk"), 0, 0, tiled=True)
    return tail(homeward, slots, capacity, members).reshape(row_count)


def solution(mesh):
    in_specs = (P(("grp", "blk"), None), P(("grp", "blk")))
    out_specs = P(("grp", "blk"))
    return jax.shard_map(
        on_device, mesh=mesh, in_specs=in_specs, out_specs=out_specs, check_vma=False
    )
```

```python
import functools

import jax
import jax.numpy as jnp
from jax import lax
from jax.experimental import pallas as pl
from jax.experimental.pallas import tpu as pltpu
from jax.sharding import PartitionSpec as P

sentinel = -3.0
epsilon = 1e-06
dead_mark = 2.0
dead_bias = -8.0
lanes = 128
smem = pl.BlockSpec(memory_space=pltpu.SMEM)
vmem = pl.BlockSpec(memory_space=pltpu.VMEM)


def chunk_sizes(capacity):
    count = 4 if capacity % 64 == 0 else 3
    return (capacity // count,) * count


def after(value, *earlier):
    return lax.optimization_barrier((value,) + earlier)[0]


def swap(value, axis, size, bit):
    return lax.ppermute(value, axis, [(i, i ^ bit) for i in range(size)])


def head_kernel(capacity, chunks, groups, me_ref, slot_ref, x_ref, *out_refs):
    wide = x_ref[...].astype(jnp.float32)
    normed = (
        wide * lax.rsqrt(jnp.sum(wide * wide, axis=-1, keepdims=True) + epsilon)
    ).astype(jnp.bfloat16)
    slots = jnp.concatenate([slot_ref[q : q + 1, :] for q in range(slot_ref.shape[0])], axis=1)
    first, high = 0, groups // 2
    for step, size in enumerate(chunks):
        place = lax.broadcasted_iota(jnp.int32, (groups, size, 1), 1)
        order = lax.broadcasted_iota(jnp.int32, (groups, size, 1), 0)
        group = (order % high * 2 + order // high) ^ me_ref[0]
        wanted = (group * capacity + place + first).reshape(groups * size, 1)
        pick = jnp.where(wanted == slots, 1.0, 0.0)
        live = jnp.max(pick, axis=1, keepdims=True)
        placed = jnp.dot(pick.astype(jnp.bfloat16), normed, preferred_element_type=jnp.float32)
        lane = lax.broadcasted_iota(jnp.int32, (1, placed.shape[1]), 1)
        mark = jnp.where(lane == 0, dead_mark, 0.0)
        placed = (placed + (1.0 - live) * mark).astype(jnp.bfloat16)
        out_refs[2 * step][...] = placed[: high * size, :]
        out_refs[2 * step + 1][...] = placed[high * size :, :]
        first += size


def head(me, embeddings, slots, capacity, chunks, groups):
    rows, features = embeddings.shape
    return pl.pallas_call(
        functools.partial(head_kernel, capacity, chunks, groups),
        in_specs=[smem, vmem, vmem],
        out_specs=[vmem] * (2 * len(chunks)),
        out_shape=[
            jax.ShapeDtypeStruct((groups // 2 * size, features), jnp.bfloat16)
            for size in chunks
            for _ in range(2)
        ],
        compiler_params=pltpu.CompilerParams(vmem_limit_bytes=32 * 2**20),
        name="place_rows",
    )(me, slots, embeddings)


def lane_fold(values):
    best = values[:, :lanes]
    for start in range(lanes, values.shape[1], lanes):
        best = jnp.maximum(best, values[:, start : start + lanes])
    return best


def gram_body(own_refs, piece_refs, row_refs, col_ref, stack, tile):
    step = len(own_refs) - 1
    start = 0
    for piece_ref in piece_refs:
        stack[start : start + piece_ref.shape[0], :] = piece_ref[...]
        start += piece_ref.shape[0]
    row_refs[step][...] = jnp.full(row_refs[step].shape, sentinel, jnp.float32)
    nt = (((1,), (1,)), ((), ()))

    @pl.loop(0, stack.shape[0] // tile)
    def _(n):
        first = pl.multiple_of(n * tile, tile)
        x = stack[pl.ds(first, tile), :]
        marks = x[:, :lanes].astype(jnp.float32).T[0:1, :]
        col_bias = jnp.where(marks > 1.5, dead_bias, 0.0)
        col_best = jnp.full((1, tile), sentinel, jnp.float32)
        for j in range(step + 1):
            own = own_refs[j][...]
            scores = lax.dot_general(own, x, nt, preferred_element_type=jnp.float32)
            usable = scores + col_bias
            if j == step:
                rows = lax.broadcasted_iota(jnp.int32, usable.shape, 0)
                cols = lax.broadcasted_iota(jnp.int32, usable.shape, 1)
                usable = jnp.where(rows - cols == first, dead_bias, usable)
            else:
                row_bias = jnp.where(own[:, 0:1].astype(jnp.float32) > 1.5, dead_bias, 0.0)
                col_best = jnp.maximum(
                    col_best, jnp.max(scores + row_bias, axis=0, keepdims=True)
                )
            row_refs[j][...] = jnp.maximum(row_refs[j][...], lane_fold(usable))
        col_ref[0:1, pl.ds(first, tile)] = col_best


def gram_kernel(first, step, tile, *refs):
    news = step + 1 - first
    owns, refs = refs[: step + 1], refs[step + 1 :]
    pieces, refs = refs[: 2 * news], refs[2 * news :]
    states, refs = refs[:first], refs[first:]
    rows, cols, stack = refs[: step + 1], refs[step + 1 : -1], refs[-1]
    for state, row in zip(states, rows):
        row[...] = state[...]
    for k in range(news):
        now = first + k + 1
        gram_body(owns[:now], pieces[2 * k : 2 * k + 2], rows[:now], cols[k], stack, tile)


def gram_last_kernel(step, relatives, chunks, groups, tile, me_ref, *refs):
    members = len(relatives)
    owns, pieces, refs = refs[: step + 1], refs[step + 1 : step + 3], refs[step + 3 :]
    states, refs = refs[:step], refs[step:]
    cols, refs = refs[:step], refs[step:]
    out_ref, stack, col, table = refs[:4]
    rows = refs[4:]
    for state, row in zip(states, rows):
        row[...] = state[...]
    gram_body(owns, pieces, rows, col, stack, tile)
    first = 0
    for k, size in enumerate(chunks):
        col_k = (cols[k] if k < step else col)[0:1, :]
        row_k = jnp.max(rows[k][...].T, axis=0, keepdims=True)
        count = groups * size
        for p, relative in enumerate(relatives):
            for r in range(groups):
                start = p * count + r * size
                best = col_k[:, start : start + size]
                if p == 0:
                    best = jnp.maximum(best, row_k[:, r * size : (r + 1) * size])
                row = r * members + p
                table[row : row + 1, first : first + size] = best
        first += size
    for r in range(groups):
        for p, relative in enumerate(relatives):
            row = r * members + p
            target = (me_ref[0] ^ r) * members + (me_ref[1] ^ relative)
            out_ref[pl.ds(target, 1), :] = table[row : row + 1, :]


def gram_step(first, me, owns, pieces, states, cols, relatives, chunks, groups):
    step = len(owns) - 1
    members = len(relatives)
    features = owns[0].shape[1]
    counts = [own.shape[0] for own in owns]
    totals = [members * count for count in counts[first:]]
    total = max(totals)
    tile = 256
    row_shapes = [(c, lanes) for c in counts]
    stack = pltpu.VMEM((total, features), jnp.bfloat16)
    params = dict(
        compiler_params=pltpu.CompilerParams(vmem_limit_bytes=24 * 2**20),
        cost_estimate=pl.CostEstimate(
            flops=2 * sum(counts) * total * features,
            bytes_accessed=2 * features * (sum(counts) + total),
            transcendentals=0,
        ),
    )
    if step < len(chunks) - 1:
        results = pl.pallas_call(
            functools.partial(gram_kernel, first, step, tile),
            in_specs=[vmem] * (step + 1 + len(pieces) + first),
            out_specs=[vmem] * (step + 1 + len(totals)),
            out_shape=[jax.ShapeDtypeStruct(s, jnp.float32) for s in row_shapes]
            + [jax.ShapeDtypeStruct((1, count), jnp.float32) for count in totals],
            scratch_shapes=[stack],
            name="gram_step",
            **params,
        )(*owns, *pieces, *states)
        return list(results[: step + 1]), cols + list(results[step + 1 :])
    return pl.pallas_call(
        functools.partial(gram_last_kernel, step, relatives, chunks, groups, tile),
        in_specs=[smem] + [vmem] * (step + 3 + 2 * step),
        out_specs=vmem,
        out_shape=jax.ShapeDtypeStruct((groups * members, sum(chunks)), jnp.float32),
        scratch_shapes=[
            stack,
            pltpu.VMEM((1, total), jnp.float32),
            pltpu.VMEM((groups * members, sum(chunks)), jnp.float32),
        ]
        + [pltpu.VMEM(s, jnp.float32) for s in row_shapes],
        name="gram_last",
        **params,
    )(me, *owns, *pieces, *states, *cols)


def tail_kernel(capacity, members, slot_ref, part_ref, out_ref, table):
    groups = part_ref.shape[0] // members
    width = table.shape[1]
    table[...] = jnp.full(table.shape, sentinel, jnp.float32)
    for g in range(groups):
        table[g : g + 1, :capacity] = jnp.max(
            part_ref[g * members : (g + 1) * members, :], axis=0, keepdims=True
        )
    lane = lax.broadcasted_iota(jnp.int32, (lanes, lanes), 1)
    for q in range(out_ref.shape[0]):
        slot = jnp.broadcast_to(slot_ref[q : q + 1, :], (lanes, lanes)).T
        best = jnp.full((lanes, lanes), sentinel, jnp.float32)
        for g in range(groups):
            for c in range(0, width, lanes):
                entry = table[g : g + 1, c : c + lanes]
                best = jnp.maximum(
                    best, jnp.where(slot - (g * capacity + c) == lane, entry, sentinel)
                )
        out_ref[q : q + 1, :] = jnp.max(best.T, axis=0, keepdims=True)


def tail(partials, slots, capacity, members):
    groups = partials.shape[0] // members
    width = -(-capacity // lanes) * lanes
    return pl.pallas_call(
        functools.partial(tail_kernel, capacity, members),
        in_specs=[vmem, vmem],
        out_specs=vmem,
        out_shape=jax.ShapeDtypeStruct(slots.shape, jnp.float32),
        scratch_shapes=[pltpu.VMEM((groups, width), jnp.float32)],
        name="pick_rows",
    )(slots, partials)


def on_device(embeddings, send_slot):
    row_count, features = embeddings.shape
    groups = lax.axis_size("grp")
    members = lax.axis_size("blk")
    slot_count = 2 * row_count
    capacity = slot_count // groups
    chunks = chunk_sizes(capacity)
    me = jnp.stack([lax.axis_index("grp"), lax.axis_index("blk")]).astype(jnp.int32)
    slots = send_slot.reshape(row_count // lanes, lanes)
    placed = head(me, embeddings, slots, capacity, chunks, groups)
    count, high = len(chunks), groups // 2
    last = count - 1

    sent, owns, done, pairs = {}, {}, {}, {}

    def rows(value, index, size):
        return value[index * size : (index + 1) * size]

    def block(step, z):
        size = chunks[step]
        return jnp.concatenate(
            [rows(placed[2 * step], z, size), rows(sent["y", step], z, size)], axis=0
        )

    def send(key, value, axis, size, bit, *earlier):
        held = [done[name] if name in done else sent[name] for name in earlier]
        sent[key] = swap(after(value, *held) if held else value, axis, size, bit)

    def send_z(step, z):
        early = [("z", step - 1, z)] if step >= 1 else []
        if step >= 2 and z != high // 2:
            early += [("x", step - 2, 0)]
        send(("z", step, z), block(step, z), "grp", groups, 2 * z, *early)

    def collect(step):
        parts = [block(step, 0)] + [sent["z", step, z] for z in range(1, high)]
        owns[step] = jnp.concatenate(parts, axis=0)

    def send_x(step):
        collect(step)
        early = [("x", step - 1, 0)] if step >= 1 else []
        early += [("y", step + 2)] if step + 2 < count else []
        send(("x", step, 0), owns[step], "blk", members, 2, *early)

    def send_c(step):
        across = [sent[name] for name in list(sent) if name[:2] == ("x", step)]
        pairs[step] = jnp.concatenate([owns[step]] + across, axis=0)
        send(("c", step), pairs[step], "blk", members, 1)

    def gram(first, step, states, cols):
        pieces = []
        for k in range(first, step + 1):
            pieces += [pairs[k], sent["c", k]]
        mine = [owns[k] for k in range(step + 1)]
        return gram_step(
            first, me, mine, pieces, states, cols, (0, 2, 1, 3), chunks, groups
        )

    far = [high // 2] + [z for z in reversed(range(1, high)) if z != high // 2]
    for step in range(count):
        send(("y", step), placed[2 * step + 1], "grp", groups, 1)
    for z in far:
        send_z(0, z)
    for step in range(1, count):
        for z in far:
            send_z(step, z)
        send_x(step - 1)
        send_c(step - 1)
    collect(last)
    total = owns[last].shape[0]
    third = total // 48 * 16
    states, cols = gram(0, last - 2, [], [])
    done["gram", 0] = cols[-1]
    states, cols = gram(last - 1, last - 1, states, cols)
    done["gram", 1] = cols[-1]
    early = [("x", last - 1, 0)] + [("c", k) for k in range(last - 1)]
    send(("x", last, 0), owns[last][:third], "blk", members, 2, *early)
    early = [("gram", 0), ("c", last - 1)]
    send(("x", last, 1), owns[last][third : 2 * third], "blk", members, 2, *early)
    send(("x", last, 2), owns[last][2 * third :], "blk", members, 2, ("gram", 1))
    send_c(last)
    result = gram(last, last, states, cols)
    homeward = lax.all_to_all(result, ("grp", "blk"), 0, 0, tiled=True)
    return tail(homeward, slots, capacity, members).reshape(row_count)


def solution(mesh):
    in_specs = (P(("grp", "blk"), None), P(("grp", "blk")))
    out_specs = P(("grp", "blk"))
    return jax.shard_map(
        on_device, mesh=mesh, in_specs=in_specs, out_specs=out_specs, check_vma=False
    )
```

```python
import functools

import jax
import jax.numpy as jnp
from jax import lax
from jax.experimental import pallas as pl
from jax.experimental.pallas import tpu as pltpu
from jax.sharding import PartitionSpec as P

sentinel = -3.0
epsilon = 1e-06
dead_mark = 2.0
dead_bias = -8.0
lanes = 128
smem = pl.BlockSpec(memory_space=pltpu.SMEM)
vmem = pl.BlockSpec(memory_space=pltpu.VMEM)


def chunk_sizes(capacity):
    count = 4 if capacity % 64 == 0 else 3
    return (capacity // count,) * count


def after(value, *earlier):
    return lax.optimization_barrier((value,) + earlier)[0]


def swap(value, axis, size, bit):
    return lax.ppermute(value, axis, [(i, i ^ bit) for i in range(size)])


def head_kernel(capacity, chunks, groups, me_ref, slot_ref, x_ref, *out_refs):
    wide = x_ref[...].astype(jnp.float32)
    normed = (
        wide * lax.rsqrt(jnp.sum(wide * wide, axis=-1, keepdims=True) + epsilon)
    ).astype(jnp.bfloat16)
    slots = jnp.concatenate([slot_ref[q : q + 1, :] for q in range(slot_ref.shape[0])], axis=1)
    first, high = 0, groups // 2
    for step, size in enumerate(chunks):
        place = lax.broadcasted_iota(jnp.int32, (groups, size, 1), 1)
        order = lax.broadcasted_iota(jnp.int32, (groups, size, 1), 0)
        group = (order % high * 2 + order // high) ^ me_ref[0]
        wanted = (group * capacity + place + first).reshape(groups * size, 1)
        pick = jnp.where(wanted == slots, 1.0, 0.0)
        live = jnp.max(pick, axis=1, keepdims=True)
        placed = jnp.dot(pick.astype(jnp.bfloat16), normed, preferred_element_type=jnp.float32)
        lane = lax.broadcasted_iota(jnp.int32, (1, placed.shape[1]), 1)
        mark = jnp.where(lane == 0, dead_mark, 0.0)
        placed = (placed + (1.0 - live) * mark).astype(jnp.bfloat16)
        out_refs[2 * step][...] = placed[: high * size, :]
        out_refs[2 * step + 1][...] = placed[high * size :, :]
        first += size


def head(me, embeddings, slots, capacity, chunks, groups):
    rows, features = embeddings.shape
    return pl.pallas_call(
        functools.partial(head_kernel, capacity, chunks, groups),
        in_specs=[smem, vmem, vmem],
        out_specs=[vmem] * (2 * len(chunks)),
        out_shape=[
            jax.ShapeDtypeStruct((groups // 2 * size, features), jnp.bfloat16)
            for size in chunks
            for _ in range(2)
        ],
        compiler_params=pltpu.CompilerParams(vmem_limit_bytes=32 * 2**20),
        name="place_rows",
    )(me, slots, embeddings)


def lane_fold(values):
    best = values[:, :lanes]
    for start in range(lanes, values.shape[1], lanes):
        best = jnp.maximum(best, values[:, start : start + lanes])
    return best


def gram_body(own_refs, piece_refs, row_refs, col_ref, stack, tile):
    step = len(own_refs) - 1
    start = 0
    for piece_ref in piece_refs:
        stack[start : start + piece_ref.shape[0], :] = piece_ref[...]
        start += piece_ref.shape[0]
    row_refs[step][...] = jnp.full(row_refs[step].shape, sentinel, jnp.float32)
    nt = (((1,), (1,)), ((), ()))

    @pl.loop(0, stack.shape[0] // tile)
    def _(n):
        first = pl.multiple_of(n * tile, tile)
        x = stack[pl.ds(first, tile), :]
        marks = x[:, :lanes].astype(jnp.float32).T[0:1, :]
        col_bias = jnp.where(marks > 1.5, dead_bias, 0.0)
        col_best = jnp.full((1, tile), sentinel, jnp.float32)
        for j in range(step + 1):
            own = own_refs[j][...]
            scores = lax.dot_general(own, x, nt, preferred_element_type=jnp.float32)
            usable = scores + col_bias
            if j == step:
                rows = lax.broadcasted_iota(jnp.int32, usable.shape, 0)
                cols = lax.broadcasted_iota(jnp.int32, usable.shape, 1)
                usable = jnp.where(rows - cols == first, dead_bias, usable)
            else:
                row_bias = jnp.where(own[:, 0:1].astype(jnp.float32) > 1.5, dead_bias, 0.0)
                col_best = jnp.maximum(
                    col_best, jnp.max(scores + row_bias, axis=0, keepdims=True)
                )
            row_refs[j][...] = jnp.maximum(row_refs[j][...], lane_fold(usable))
        col_ref[0:1, pl.ds(first, tile)] = col_best


def gram_kernel(first, step, tile, *refs):
    news = step + 1 - first
    owns, refs = refs[: step + 1], refs[step + 1 :]
    pieces, refs = refs[: 2 * news], refs[2 * news :]
    states, refs = refs[:first], refs[first:]
    rows, cols, stack = refs[: step + 1], refs[step + 1 : -1], refs[-1]
    for state, row in zip(states, rows):
        row[...] = state[...]
    for k in range(news):
        now = first + k + 1
        gram_body(owns[:now], pieces[2 * k : 2 * k + 2], rows[:now], cols[k], stack, tile)


def gram_last_kernel(step, relatives, chunks, groups, tile, me_ref, *refs):
    members = len(relatives)
    owns, pieces, refs = refs[: step + 1], refs[step + 1 : step + 3], refs[step + 3 :]
    states, refs = refs[:step], refs[step:]
    cols, refs = refs[:step], refs[step:]
    out_ref, stack, col, table = refs[:4]
    rows = refs[4:]
    for state, row in zip(states, rows):
        row[...] = state[...]
    gram_body(owns, pieces, rows, col, stack, tile)
    first = 0
    for k, size in enumerate(chunks):
        col_k = (cols[k] if k < step else col)[0:1, :]
        row_k = jnp.max(rows[k][...].T, axis=0, keepdims=True)
        count = groups * size
        for p, relative in enumerate(relatives):
            for r in range(groups):
                start = p * count + r * size
                best = col_k[:, start : start + size]
                if p == 0:
                    best = jnp.maximum(best, row_k[:, r * size : (r + 1) * size])
                row = r * members + p
                table[row : row + 1, first : first + size] = best
        first += size
    for r in range(groups):
        for p, relative in enumerate(relatives):
            row = r * members + p
            target = (me_ref[0] ^ r) * members + (me_ref[1] ^ relative)
            out_ref[pl.ds(target, 1), :] = table[row : row + 1, :]


def gram_step(first, me, owns, pieces, states, cols, relatives, chunks, groups):
    step = len(owns) - 1
    members = len(relatives)
    features = owns[0].shape[1]
    counts = [own.shape[0] for own in owns]
    totals = [members * count for count in counts[first:]]
    total = max(totals)
    tile = 256
    row_shapes = [(c, lanes) for c in counts]
    stack = pltpu.VMEM((total, features), jnp.bfloat16)
    params = dict(
        compiler_params=pltpu.CompilerParams(vmem_limit_bytes=24 * 2**20),
        cost_estimate=pl.CostEstimate(
            flops=2 * sum(counts) * total * features,
            bytes_accessed=2 * features * (sum(counts) + total),
            transcendentals=0,
        ),
    )
    if step < len(chunks) - 1:
        results = pl.pallas_call(
            functools.partial(gram_kernel, first, step, tile),
            in_specs=[vmem] * (step + 1 + len(pieces) + first),
            out_specs=[vmem] * (step + 1 + len(totals)),
            out_shape=[jax.ShapeDtypeStruct(s, jnp.float32) for s in row_shapes]
            + [jax.ShapeDtypeStruct((1, count), jnp.float32) for count in totals],
            scratch_shapes=[stack],
            name="gram_step",
            **params,
        )(*owns, *pieces, *states)
        return list(results[: step + 1]), cols + list(results[step + 1 :])
    return pl.pallas_call(
        functools.partial(gram_last_kernel, step, relatives, chunks, groups, tile),
        in_specs=[smem] + [vmem] * (step + 3 + 2 * step),
        out_specs=vmem,
        out_shape=jax.ShapeDtypeStruct((groups * members, sum(chunks)), jnp.float32),
        scratch_shapes=[
            stack,
            pltpu.VMEM((1, total), jnp.float32),
            pltpu.VMEM((groups * members, sum(chunks)), jnp.float32),
        ]
        + [pltpu.VMEM(s, jnp.float32) for s in row_shapes],
        name="gram_last",
        **params,
    )(me, *owns, *pieces, *states, *cols)


def tail_kernel(capacity, members, slot_ref, part_ref, out_ref, table):
    groups = part_ref.shape[0] // members
    width = table.shape[1]
    table[...] = jnp.full(table.shape, sentinel, jnp.float32)
    for g in range(groups):
        table[g : g + 1, :capacity] = jnp.max(
            part_ref[g * members : (g + 1) * members, :], axis=0, keepdims=True
        )
    lane = lax.broadcasted_iota(jnp.int32, (lanes, lanes), 1)
    for q in range(out_ref.shape[0]):
        slot = jnp.broadcast_to(slot_ref[q : q + 1, :], (lanes, lanes)).T
        best = jnp.full((lanes, lanes), sentinel, jnp.float32)
        for g in range(groups):
            for c in range(0, width, lanes):
                entry = table[g : g + 1, c : c + lanes]
                best = jnp.maximum(
                    best, jnp.where(slot - (g * capacity + c) == lane, entry, sentinel)
                )
        out_ref[q : q + 1, :] = jnp.max(best.T, axis=0, keepdims=True)


def tail(partials, slots, capacity, members):
    groups = partials.shape[0] // members
    width = -(-capacity // lanes) * lanes
    return pl.pallas_call(
        functools.partial(tail_kernel, capacity, members),
        in_specs=[vmem, vmem],
        out_specs=vmem,
        out_shape=jax.ShapeDtypeStruct(slots.shape, jnp.float32),
        scratch_shapes=[pltpu.VMEM((groups, width), jnp.float32)],
        name="pick_rows",
    )(slots, partials)


def on_device(embeddings, send_slot):
    row_count, features = embeddings.shape
    groups = lax.axis_size("grp")
    members = lax.axis_size("blk")
    slot_count = 2 * row_count
    capacity = slot_count // groups
    chunks = chunk_sizes(capacity)
    me = jnp.stack([lax.axis_index("grp"), lax.axis_index("blk")]).astype(jnp.int32)
    slots = send_slot.reshape(row_count // lanes, lanes)
    placed = head(me, embeddings, slots, capacity, chunks, groups)
    count, high = len(chunks), groups // 2
    last = count - 1

    sent, owns, done, pairs = {}, {}, {}, {}

    def rows(value, index, size):
        return value[index * size : (index + 1) * size]

    def block(step, z):
        size = chunks[step]
        return jnp.concatenate(
            [rows(placed[2 * step], z, size), rows(sent["y", step], z, size)], axis=0
        )

    def send(key, value, axis, size, bit, *earlier):
        held = [done[name] if name in done else sent[name] for name in earlier]
        sent[key] = swap(after(value, *held) if held else value, axis, size, bit)

    def send_z(step, z):
        early = [("z", step - 1, z)] if step >= 1 else []
        if step >= 2 and z != high // 2:
            early += [("x", step - 2, 0)]
        send(("z", step, z), block(step, z), "grp", groups, 2 * z, *early)

    def collect(step):
        parts = [block(step, 0)] + [sent["z", step, z] for z in range(1, high)]
        owns[step] = jnp.concatenate(parts, axis=0)

    def send_x(step):
        collect(step)
        early = [("x", step - 1, 0)] if step >= 1 else []
        early += [("y", step + 2)] if step + 2 < count else []
        send(("x", step, 0), owns[step], "blk", members, 2, *early)

    def send_c(step, *early):
        across = [sent[name] for name in list(sent) if name[:2] == ("x", step)]
        pairs[step] = jnp.concatenate([owns[step]] + across, axis=0)
        send(("c", step), pairs[step], "blk", members, 1, *early)

    def gram(first, step, states, cols):
        pieces = []
        for k in range(first, step + 1):
            pieces += [pairs[k], sent["c", k]]
        mine = [owns[k] for k in range(step + 1)]
        return gram_step(
            first, me, mine, pieces, states, cols, (0, 2, 1, 3), chunks, groups
        )

    far = [high // 2] + [z for z in reversed(range(1, high)) if z != high // 2]
    for step in range(count):
        send(("y", step), placed[2 * step + 1], "grp", groups, 1)
    for z in far:
        send_z(0, z)
    for step in range(1, count):
        for z in far:
            send_z(step, z)
        send_x(step - 1)
        send_c(step - 1, *([("z", last, z) for z in far] if step == last else []))
    collect(last)
    total = owns[last].shape[0]
    cut, end = total * 208 // 384 // 16 * 16, total * 352 // 384 // 16 * 16
    states, cols = gram(0, last - 2, [], [])
    done["gram", 0] = cols[-1]
    states, cols = gram(last - 1, last - 1, states, cols)
    done["gram", 1] = cols[-1]
    early = [("x", last - 1, 0)] + [("c", k) for k in range(last - 1)]
    send(("x", last, 0), owns[last][:cut], "blk", members, 2, *early)
    early = [("gram", 0), ("c", last - 1)]
    send(("x", last, 1), owns[last][cut:end], "blk", members, 2, *early)
    send(("x", last, 2), owns[last][end:], "blk", members, 2, ("gram", 1))
    send_c(last)
    result = gram(last, last, states, cols)
    homeward = lax.all_to_all(result, ("grp", "blk"), 0, 0, tiled=True)
    return tail(homeward, slots, capacity, members).reshape(row_count)


def solution(mesh):
    in_specs = (P(("grp", "blk"), None), P(("grp", "blk")))
    out_specs = P(("grp", "blk"))
    return jax.shard_map(
        on_device, mesh=mesh, in_specs=in_specs, out_specs=out_specs, check_vma=False
    )
```

```python
import functools

import jax
import jax.numpy as jnp
from jax import lax
from jax.experimental import pallas as pl
from jax.experimental.pallas import tpu as pltpu
from jax.sharding import PartitionSpec as P

sentinel = -3.0
epsilon = 1e-06
dead_mark = 2.0
dead_bias = -8.0
lanes = 128
smem = pl.BlockSpec(memory_space=pltpu.SMEM)
vmem = pl.BlockSpec(memory_space=pltpu.VMEM)


def chunk_sizes(capacity):
    count = 4 if capacity % 64 == 0 else 3
    return (capacity // count,) * count


def after(value, *earlier):
    return lax.optimization_barrier((value,) + earlier)[0]


def swap(value, axis, size, bit):
    return lax.ppermute(value, axis, [(i, i ^ bit) for i in range(size)])


def place(me, slots, normed, capacity, first, size, groups, low):
    shape = (groups // 2, size, 1)
    spot = lax.broadcasted_iota(jnp.int32, shape, 1) + first
    group = (lax.broadcasted_iota(jnp.int32, shape, 0) * 2 + low) ^ me
    wanted = (group * capacity + spot).reshape(groups // 2 * size, 1)
    pick = jnp.where(wanted == slots, 1.0, 0.0)
    live = jnp.max(pick, axis=1, keepdims=True)
    placed = jnp.dot(pick.astype(jnp.bfloat16), normed, preferred_element_type=jnp.float32)
    lane = lax.broadcasted_iota(jnp.int32, (1, placed.shape[1]), 1)
    mark = jnp.where(lane == 0, dead_mark, 0.0)
    return (placed + (1.0 - live) * mark).astype(jnp.bfloat16)


def flat(slot_ref):
    return jnp.concatenate([slot_ref[q : q + 1, :] for q in range(slot_ref.shape[0])], axis=1)


def first_kernel(capacity, chunks, groups, me_ref, slot_ref, x_ref, normed_ref, send_ref):
    wide = x_ref[...].astype(jnp.float32)
    normed_ref[...] = (
        wide * lax.rsqrt(jnp.sum(wide * wide, axis=-1, keepdims=True) + epsilon)
    ).astype(jnp.bfloat16)
    send_ref[...] = place(
        me_ref[0], flat(slot_ref), normed_ref[...], capacity, 0, chunks[0], groups, 1
    )


def rest_kernel(capacity, chunks, groups, me_ref, slot_ref, normed_ref, *out_refs):
    keeps, send_ref = out_refs[:-1], out_refs[-1]
    slots, normed = flat(slot_ref), normed_ref[...]
    first, row = 0, 0
    for step, size in enumerate(chunks):
        if step > 0:
            count = groups // 2 * size
            send_ref[row : row + count, :] = place(
                me_ref[0], slots, normed, capacity, first, size, groups, 1
            )
            row += count
        first += size
    first = 0
    for step, size in enumerate(chunks):
        keeps[step][...] = place(me_ref[0], slots, normed, capacity, first, size, groups, 0)
        first += size


def head(me, embeddings, slots, capacity, chunks, groups):
    rows, features = embeddings.shape
    half = [groups // 2 * size for size in chunks]

    def shape(count):
        return jax.ShapeDtypeStruct((count, features), jnp.bfloat16)

    def cost(count):
        return pl.CostEstimate(
            flops=2 * count * rows * features,
            bytes_accessed=2 * (rows + count) * features,
            transcendentals=0,
        )

    params = pltpu.CompilerParams(vmem_limit_bytes=24 * 2**20)
    normed, first_send = pl.pallas_call(
        functools.partial(first_kernel, capacity, chunks, groups),
        in_specs=[smem, vmem, vmem],
        out_specs=[vmem, vmem],
        out_shape=[shape(rows), shape(half[0])],
        compiler_params=params,
        cost_estimate=cost(half[0]),
        name="place_first",
    )(me, slots, embeddings)
    *keeps, rest_send = pl.pallas_call(
        functools.partial(rest_kernel, capacity, chunks, groups),
        in_specs=[smem, vmem, vmem],
        out_specs=[vmem] * (len(chunks) + 1),
        out_shape=[shape(count) for count in half] + [shape(sum(half[1:]))],
        compiler_params=params,
        cost_estimate=cost(2 * sum(half) - half[0]),
        name="place_rest",
    )(me, slots, normed)
    return keeps, first_send, rest_send


def lane_fold(values):
    best = values[:, :lanes]
    for start in range(lanes, values.shape[1], lanes):
        best = jnp.maximum(best, values[:, start : start + lanes])
    return best


def gram_body(own_refs, piece_refs, row_refs, col_ref, stack, tile):
    step = len(own_refs) - 1
    start = 0
    for piece_ref in piece_refs:
        stack[start : start + piece_ref.shape[0], :] = piece_ref[...]
        start += piece_ref.shape[0]
    row_refs[step][...] = jnp.full(row_refs[step].shape, sentinel, jnp.float32)
    nt = (((1,), (1,)), ((), ()))

    @pl.loop(0, stack.shape[0] // tile)
    def _(n):
        first = pl.multiple_of(n * tile, tile)
        x = stack[pl.ds(first, tile), :]
        marks = x[:, :lanes].astype(jnp.float32).T[0:1, :]
        col_bias = jnp.where(marks > 1.5, dead_bias, 0.0)
        col_best = jnp.full((1, tile), sentinel, jnp.float32)
        for j in range(step + 1):
            own = own_refs[j][...]
            scores = lax.dot_general(own, x, nt, preferred_element_type=jnp.float32)
            usable = scores + col_bias
            if j == step:
                rows = lax.broadcasted_iota(jnp.int32, usable.shape, 0)
                cols = lax.broadcasted_iota(jnp.int32, usable.shape, 1)
                usable = jnp.where(rows - cols == first, dead_bias, usable)
            else:
                row_bias = jnp.where(own[:, 0:1].astype(jnp.float32) > 1.5, dead_bias, 0.0)
                col_best = jnp.maximum(
                    col_best, jnp.max(scores + row_bias, axis=0, keepdims=True)
                )
            row_refs[j][...] = jnp.maximum(row_refs[j][...], lane_fold(usable))
        col_ref[0:1, pl.ds(first, tile)] = col_best


def gram_kernel(first, step, tile, *refs):
    news = step + 1 - first
    owns, refs = refs[: step + 1], refs[step + 1 :]
    pieces, refs = refs[: 2 * news], refs[2 * news :]
    states, refs = refs[:first], refs[first:]
    rows, cols, stack = refs[: step + 1], refs[step + 1 : -1], refs[-1]
    for state, row in zip(states, rows):
        row[...] = state[...]
    for k in range(news):
        now = first + k + 1
        gram_body(owns[:now], pieces[2 * k : 2 * k + 2], rows[:now], cols[k], stack, tile)


def gram_last_kernel(step, relatives, chunks, groups, tile, me_ref, *refs):
    members = len(relatives)
    owns, pieces, refs = refs[: step + 1], refs[step + 1 : step + 3], refs[step + 3 :]
    states, refs = refs[:step], refs[step:]
    cols, refs = refs[:step], refs[step:]
    out_ref, stack, col, table = refs[:4]
    rows = refs[4:]
    for state, row in zip(states, rows):
        row[...] = state[...]
    gram_body(owns, pieces, rows, col, stack, tile)
    first = 0
    for k, size in enumerate(chunks):
        col_k = (cols[k] if k < step else col)[0:1, :]
        row_k = jnp.max(rows[k][...].T, axis=0, keepdims=True)
        count = groups * size
        for p, relative in enumerate(relatives):
            for r in range(groups):
                start = p * count + r * size
                best = col_k[:, start : start + size]
                if p == 0:
                    best = jnp.maximum(best, row_k[:, r * size : (r + 1) * size])
                row = r * members + p
                table[row : row + 1, first : first + size] = best
        first += size
    for r in range(groups):
        for p, relative in enumerate(relatives):
            row = r * members + p
            target = (me_ref[0] ^ r) * members + (me_ref[1] ^ relative)
            out_ref[pl.ds(target, 1), :] = table[row : row + 1, :]


def gram_step(first, me, owns, pieces, states, cols, relatives, chunks, groups):
    step = len(owns) - 1
    members = len(relatives)
    features = owns[0].shape[1]
    counts = [own.shape[0] for own in owns]
    totals = [members * count for count in counts[first:]]
    total = max(totals)
    tile = 256
    row_shapes = [(c, lanes) for c in counts]
    stack = pltpu.VMEM((total, features), jnp.bfloat16)
    params = dict(
        compiler_params=pltpu.CompilerParams(vmem_limit_bytes=24 * 2**20),
        cost_estimate=pl.CostEstimate(
            flops=2 * sum(counts) * total * features,
            bytes_accessed=2 * features * (sum(counts) + total),
            transcendentals=0,
        ),
    )
    if step < len(chunks) - 1:
        results = pl.pallas_call(
            functools.partial(gram_kernel, first, step, tile),
            in_specs=[vmem] * (step + 1 + len(pieces) + first),
            out_specs=[vmem] * (step + 1 + len(totals)),
            out_shape=[jax.ShapeDtypeStruct(s, jnp.float32) for s in row_shapes]
            + [jax.ShapeDtypeStruct((1, count), jnp.float32) for count in totals],
            scratch_shapes=[stack],
            name="gram_step",
            **params,
        )(*owns, *pieces, *states)
        return list(results[: step + 1]), cols + list(results[step + 1 :])
    return pl.pallas_call(
        functools.partial(gram_last_kernel, step, relatives, chunks, groups, tile),
        in_specs=[smem] + [vmem] * (step + 3 + 2 * step),
        out_specs=vmem,
        out_shape=jax.ShapeDtypeStruct((groups * members, sum(chunks)), jnp.float32),
        scratch_shapes=[
            stack,
            pltpu.VMEM((1, total), jnp.float32),
            pltpu.VMEM((groups * members, sum(chunks)), jnp.float32),
        ]
        + [pltpu.VMEM(s, jnp.float32) for s in row_shapes],
        name="gram_last",
        **params,
    )(me, *owns, *pieces, *states, *cols)


def tail_kernel(capacity, members, slot_ref, part_ref, out_ref, table):
    groups = part_ref.shape[0] // members
    width = table.shape[1]
    table[...] = jnp.full(table.shape, sentinel, jnp.float32)
    for g in range(groups):
        table[g : g + 1, :capacity] = jnp.max(
            part_ref[g * members : (g + 1) * members, :], axis=0, keepdims=True
        )
    lane = lax.broadcasted_iota(jnp.int32, (lanes, lanes), 1)
    for q in range(out_ref.shape[0]):
        slot = jnp.broadcast_to(slot_ref[q : q + 1, :], (lanes, lanes)).T
        best = jnp.full((lanes, lanes), sentinel, jnp.float32)
        for g in range(groups):
            for c in range(0, width, lanes):
                entry = table[g : g + 1, c : c + lanes]
                best = jnp.maximum(
                    best, jnp.where(slot - (g * capacity + c) == lane, entry, sentinel)
                )
        out_ref[q : q + 1, :] = jnp.max(best.T, axis=0, keepdims=True)


def tail(partials, slots, capacity, members):
    groups = partials.shape[0] // members
    width = -(-capacity // lanes) * lanes
    return pl.pallas_call(
        functools.partial(tail_kernel, capacity, members),
        in_specs=[vmem, vmem],
        out_specs=vmem,
        out_shape=jax.ShapeDtypeStruct(slots.shape, jnp.float32),
        scratch_shapes=[pltpu.VMEM((groups, width), jnp.float32)],
        name="pick_rows",
    )(slots, partials)


def on_device(embeddings, send_slot):
    row_count, features = embeddings.shape
    groups = lax.axis_size("grp")
    members = lax.axis_size("blk")
    slot_count = 2 * row_count
    capacity = slot_count // groups
    chunks = chunk_sizes(capacity)
    me = jnp.stack([lax.axis_index("grp"), lax.axis_index("blk")]).astype(jnp.int32)
    slots = send_slot.reshape(row_count // lanes, lanes)
    keeps, first_send, rest_send = head(me, embeddings, slots, capacity, chunks, groups)
    count, high = len(chunks), groups // 2
    last = count - 1

    sent, owns, done, pairs = {}, {}, {}, {}

    def rows(value, index, size):
        return value[index * size : (index + 1) * size]

    def block(step, z):
        size = chunks[step]
        near = sent["y", 0] if step == 0 else sent["y", 1]
        skip = sum(chunks[1:step]) * high
        return jnp.concatenate(
            [rows(keeps[step], z, size), rows(near[skip:], z, size)], axis=0
        )

    def send(key, value, axis, size, bit, *earlier):
        held = [done[name] if name in done else sent[name] for name in earlier]
        sent[key] = swap(after(value, *held) if held else value, axis, size, bit)

    def send_z(step, z):
        early = [("z", step - 1, z)] if step >= 1 else []
        if step >= 2 and z == far[-1]:
            early += [("x", step - 2, 0)]
        if step == last and step >= 3:
            early += [("c", step - 2 if z == far[-1] else step - 3)]
        send(("z", step, z), block(step, z), "grp", groups, 2 * z, *early)

    def collect(step):
        parts = [block(step, 0)] + [sent["z", step, z] for z in range(1, high)]
        owns[step] = jnp.concatenate(parts, axis=0)

    def send_x(step, cuts, between):
        total = owns[step].shape[0]
        cuts = [0] + [total * cut // 384 // 16 * 16 for cut in cuts] + [total]
        parts = [name for name in sent if name[:2] == ("x", step - 1)]
        for part in range(len(cuts) - 1):
            value = owns[step][cuts[part] : cuts[part + 1]]
            early = parts if part == 0 else between
            send(("x", step, part), value, "blk", members, 2, *early)

    def send_c(step, *early):
        across = [sent[name] for name in list(sent) if name[:2] == ("x", step)]
        pairs[step] = jnp.concatenate([owns[step]] + across, axis=0)
        send(("c", step), pairs[step], "blk", members, 1, *early)

    def gram(first, step, states, cols):
        pieces = []
        for k in range(first, step + 1):
            pieces += [pairs[k], sent["c", k]]
        mine = [owns[k] for k in range(step + 1)]
        return gram_step(
            first, me, mine, pieces, states, cols, (0, 2, 1, 3), chunks, groups
        )

    far = [high // 2] + [z for z in range(1, high) if z != high // 2]
    send(("y", 0), first_send, "grp", groups, 1)
    send(("y", 1), rest_send, "grp", groups, 1)
    for z in far:
        send_z(0, z)
    for step in range(1, count):
        collect(step - 1)
        if step < last:
            for z in far:
                send_z(step, z)
            send_x(step - 1, [], [])
            send_c(step - 1)
    for z in far:
        send_z(last, z)
    collect(last)
    states, cols = gram(0, last - 2, [], [])
    done["gram", 0] = cols[-1]
    send_x(last - 1, [256], [("gram", 0)])
    send_c(last - 1, *[("z", last, z) for z in far])
    states, cols = gram(last - 1, last - 1, states, cols)
    done["gram", 1] = cols[-1]
    send_x(last, [256], [("gram", 1)])
    send_c(last)
    result = gram(last, last, states, cols)
    homeward = lax.all_to_all(result, ("grp", "blk"), 0, 0, tiled=True)
    return tail(homeward, slots, capacity, members).reshape(row_count)


def solution(mesh):
    in_specs = (P(("grp", "blk"), None), P(("grp", "blk")))
    out_specs = P(("grp", "blk"))
    return jax.shard_map(
        on_device, mesh=mesh, in_specs=in_specs, out_specs=out_specs, check_vma=False
    )
```

```python
import functools

import jax
import jax.numpy as jnp
from jax import lax
from jax.experimental import pallas as pl
from jax.experimental.pallas import tpu as pltpu
from jax.sharding import PartitionSpec as P

sentinel = -3.0
epsilon = 1e-06
dead_mark = 2.0
dead_bias = -8.0
lanes = 128
smem = pl.BlockSpec(memory_space=pltpu.SMEM)
vmem = pl.BlockSpec(memory_space=pltpu.VMEM)


def chunk_sizes(capacity):
    count = 4 if capacity % 64 == 0 else 3
    return (capacity // count,) * count


def after(value, *earlier):
    return lax.optimization_barrier((value,) + earlier)[0]


def swap(value, axis, size, bit):
    return lax.ppermute(value, axis, [(i, i ^ bit) for i in range(size)])


def place(me, slots, normed, capacity, first, size, groups, low):
    shape = (groups // 2, size, 1)
    spot = lax.broadcasted_iota(jnp.int32, shape, 1) + first
    group = (lax.broadcasted_iota(jnp.int32, shape, 0) * 2 + low) ^ me
    wanted = (group * capacity + spot).reshape(groups // 2 * size, 1)
    pick = jnp.where(wanted == slots, 1.0, 0.0)
    live = jnp.max(pick, axis=1, keepdims=True)
    placed = jnp.dot(pick.astype(jnp.bfloat16), normed, preferred_element_type=jnp.float32)
    lane = lax.broadcasted_iota(jnp.int32, (1, placed.shape[1]), 1)
    mark = jnp.where(lane == 0, dead_mark, 0.0)
    return (placed + (1.0 - live) * mark).astype(jnp.bfloat16)


def flat(slot_ref):
    return jnp.concatenate([slot_ref[q : q + 1, :] for q in range(slot_ref.shape[0])], axis=1)


def first_kernel(capacity, chunks, groups, me_ref, slot_ref, x_ref, normed_ref, send_ref):
    wide = x_ref[...].astype(jnp.float32)
    normed_ref[...] = (
        wide * lax.rsqrt(jnp.sum(wide * wide, axis=-1, keepdims=True) + epsilon)
    ).astype(jnp.bfloat16)
    send_ref[...] = place(
        me_ref[0], flat(slot_ref), normed_ref[...], capacity, 0, chunks[0], groups, 1
    )


def rest_kernel(capacity, chunks, groups, me_ref, slot_ref, normed_ref, *out_refs):
    keeps, send_ref = out_refs[:-1], out_refs[-1]
    slots, normed = flat(slot_ref), normed_ref[...]
    first, row = 0, 0
    for step, size in enumerate(chunks):
        if step > 0:
            count = groups // 2 * size
            send_ref[row : row + count, :] = place(
                me_ref[0], slots, normed, capacity, first, size, groups, 1
            )
            row += count
        first += size
    first = 0
    for step, size in enumerate(chunks):
        keeps[step][...] = place(me_ref[0], slots, normed, capacity, first, size, groups, 0)
        first += size


def head(me, embeddings, slots, capacity, chunks, groups):
    rows, features = embeddings.shape
    half = [groups // 2 * size for size in chunks]

    def shape(count):
        return jax.ShapeDtypeStruct((count, features), jnp.bfloat16)

    def cost(count):
        return pl.CostEstimate(
            flops=2 * count * rows * features,
            bytes_accessed=2 * (rows + count) * features,
            transcendentals=0,
        )

    params = pltpu.CompilerParams(vmem_limit_bytes=24 * 2**20)
    normed, first_send = pl.pallas_call(
        functools.partial(first_kernel, capacity, chunks, groups),
        in_specs=[smem, vmem, vmem],
        out_specs=[vmem, vmem],
        out_shape=[shape(rows), shape(half[0])],
        compiler_params=params,
        cost_estimate=cost(half[0]),
        name="place_first",
    )(me, slots, embeddings)
    *keeps, rest_send = pl.pallas_call(
        functools.partial(rest_kernel, capacity, chunks, groups),
        in_specs=[smem, vmem, vmem],
        out_specs=[vmem] * (len(chunks) + 1),
        out_shape=[shape(count) for count in half] + [shape(sum(half[1:]))],
        compiler_params=params,
        cost_estimate=cost(2 * sum(half) - half[0]),
        name="place_rest",
    )(me, slots, normed)
    return keeps, first_send, rest_send


def lane_fold(values):
    best = values[:, :lanes]
    for start in range(lanes, values.shape[1], lanes):
        best = jnp.maximum(best, values[:, start : start + lanes])
    return best


def gram_body(own_refs, piece_refs, row_refs, col_ref, stack, tile):
    step = len(own_refs) - 1
    start = 0
    for piece_ref in piece_refs:
        stack[start : start + piece_ref.shape[0], :] = piece_ref[...]
        start += piece_ref.shape[0]
    row_refs[step][...] = jnp.full(row_refs[step].shape, sentinel, jnp.float32)
    nt = (((1,), (1,)), ((), ()))

    @pl.loop(0, stack.shape[0] // tile)
    def _(n):
        first = pl.multiple_of(n * tile, tile)
        x = stack[pl.ds(first, tile), :]
        marks = x[:, :lanes].astype(jnp.float32).T[0:1, :]
        col_bias = jnp.where(marks > 1.5, dead_bias, 0.0)
        col_best = jnp.full((1, tile), sentinel, jnp.float32)
        for j in range(step + 1):
            own = own_refs[j][...]
            scores = lax.dot_general(own, x, nt, preferred_element_type=jnp.float32)
            usable = scores + col_bias
            if j == step:
                rows = lax.broadcasted_iota(jnp.int32, usable.shape, 0)
                cols = lax.broadcasted_iota(jnp.int32, usable.shape, 1)
                usable = jnp.where(rows - cols == first, dead_bias, usable)
            else:
                row_bias = jnp.where(own[:, 0:1].astype(jnp.float32) > 1.5, dead_bias, 0.0)
                col_best = jnp.maximum(
                    col_best, jnp.max(scores + row_bias, axis=0, keepdims=True)
                )
            row_refs[j][...] = jnp.maximum(row_refs[j][...], lane_fold(usable))
        col_ref[0:1, pl.ds(first, tile)] = col_best


def gram_kernel(first, step, tile, *refs):
    news = step + 1 - first
    owns, refs = refs[: step + 1], refs[step + 1 :]
    pieces, refs = refs[: 2 * news], refs[2 * news :]
    states, refs = refs[:first], refs[first:]
    rows, cols, stack = refs[: step + 1], refs[step + 1 : -1], refs[-1]
    for state, row in zip(states, rows):
        row[...] = state[...]
    for k in range(news):
        now = first + k + 1
        gram_body(owns[:now], pieces[2 * k : 2 * k + 2], rows[:now], cols[k], stack, tile)


def gram_last_kernel(step, relatives, chunks, groups, tile, me_ref, *refs):
    members = len(relatives)
    owns, pieces, refs = refs[: step + 1], refs[step + 1 : step + 3], refs[step + 3 :]
    states, refs = refs[:step], refs[step:]
    cols, refs = refs[:step], refs[step:]
    out_ref, stack, col, table = refs[:4]
    rows = refs[4:]
    for state, row in zip(states, rows):
        row[...] = state[...]
    gram_body(owns, pieces, rows, col, stack, tile)
    first = 0
    for k, size in enumerate(chunks):
        col_k = (cols[k] if k < step else col)[0:1, :]
        row_k = jnp.max(rows[k][...].T, axis=0, keepdims=True)
        count = groups * size
        for p, relative in enumerate(relatives):
            for r in range(groups):
                start = p * count + r * size
                best = col_k[:, start : start + size]
                if p == 0:
                    best = jnp.maximum(best, row_k[:, r * size : (r + 1) * size])
                row = r * members + p
                table[row : row + 1, first : first + size] = best
        first += size
    for r in range(groups):
        for p, relative in enumerate(relatives):
            row = r * members + p
            target = (me_ref[0] ^ r) * members + (me_ref[1] ^ relative)
            out_ref[pl.ds(target, 1), :] = table[row : row + 1, :]


def gram_step(first, me, owns, pieces, states, cols, relatives, chunks, groups):
    step = len(owns) - 1
    members = len(relatives)
    features = owns[0].shape[1]
    counts = [own.shape[0] for own in owns]
    totals = [members * count for count in counts[first:]]
    total = max(totals)
    tile = 256
    row_shapes = [(c, lanes) for c in counts]
    stack = pltpu.VMEM((total, features), jnp.bfloat16)
    params = dict(
        compiler_params=pltpu.CompilerParams(vmem_limit_bytes=24 * 2**20),
        cost_estimate=pl.CostEstimate(
            flops=2 * sum(counts) * total * features,
            bytes_accessed=2 * features * (sum(counts) + total),
            transcendentals=0,
        ),
    )
    if step < len(chunks) - 1:
        results = pl.pallas_call(
            functools.partial(gram_kernel, first, step, tile),
            in_specs=[vmem] * (step + 1 + len(pieces) + first),
            out_specs=[vmem] * (step + 1 + len(totals)),
            out_shape=[jax.ShapeDtypeStruct(s, jnp.float32) for s in row_shapes]
            + [jax.ShapeDtypeStruct((1, count), jnp.float32) for count in totals],
            scratch_shapes=[stack],
            name="gram_step",
            **params,
        )(*owns, *pieces, *states)
        return list(results[: step + 1]), cols + list(results[step + 1 :])
    return pl.pallas_call(
        functools.partial(gram_last_kernel, step, relatives, chunks, groups, tile),
        in_specs=[smem] + [vmem] * (step + 3 + 2 * step),
        out_specs=vmem,
        out_shape=jax.ShapeDtypeStruct((groups * members, sum(chunks)), jnp.float32),
        scratch_shapes=[
            stack,
            pltpu.VMEM((1, total), jnp.float32),
            pltpu.VMEM((groups * members, sum(chunks)), jnp.float32),
        ]
        + [pltpu.VMEM(s, jnp.float32) for s in row_shapes],
        name="gram_last",
        **params,
    )(me, *owns, *pieces, *states, *cols)


def tail_kernel(capacity, members, slot_ref, part_ref, out_ref, table):
    groups = part_ref.shape[0] // members
    width = table.shape[1]
    table[...] = jnp.full(table.shape, sentinel, jnp.float32)
    for g in range(groups):
        table[g : g + 1, :capacity] = jnp.max(
            part_ref[g * members : (g + 1) * members, :], axis=0, keepdims=True
        )
    lane = lax.broadcasted_iota(jnp.int32, (lanes, lanes), 1)
    for q in range(out_ref.shape[0]):
        slot = jnp.broadcast_to(slot_ref[q : q + 1, :], (lanes, lanes)).T
        best = jnp.full((lanes, lanes), sentinel, jnp.float32)
        for g in range(groups):
            for c in range(0, width, lanes):
                entry = table[g : g + 1, c : c + lanes]
                best = jnp.maximum(
                    best, jnp.where(slot - (g * capacity + c) == lane, entry, sentinel)
                )
        out_ref[q : q + 1, :] = jnp.max(best.T, axis=0, keepdims=True)


def tail(partials, slots, capacity, members):
    groups = partials.shape[0] // members
    width = -(-capacity // lanes) * lanes
    return pl.pallas_call(
        functools.partial(tail_kernel, capacity, members),
        in_specs=[vmem, vmem],
        out_specs=vmem,
        out_shape=jax.ShapeDtypeStruct(slots.shape, jnp.float32),
        scratch_shapes=[pltpu.VMEM((groups, width), jnp.float32)],
        name="pick_rows",
    )(slots, partials)


def on_device(embeddings, send_slot):
    row_count, features = embeddings.shape
    groups = lax.axis_size("grp")
    members = lax.axis_size("blk")
    slot_count = 2 * row_count
    capacity = slot_count // groups
    chunks = chunk_sizes(capacity)
    me = jnp.stack([lax.axis_index("grp"), lax.axis_index("blk")]).astype(jnp.int32)
    slots = send_slot.reshape(row_count // lanes, lanes)
    keeps, first_send, rest_send = head(me, embeddings, slots, capacity, chunks, groups)
    count, high = len(chunks), groups // 2
    last = count - 1

    sent, owns, done, pairs = {}, {}, {}, {}

    def rows(value, index, size):
        return value[index * size : (index + 1) * size]

    def block(step, z):
        size = chunks[step]
        near = first_near if step == 0 else sent["y", 2]
        skip = sum(chunks[1:step]) * high
        return jnp.concatenate(
            [rows(keeps[step], z, size), rows(near[skip:], z, size)], axis=0
        )

    def send(key, value, axis, size, bit, *earlier):
        held = [done[name] if name in done else sent[name] for name in earlier]
        sent[key] = swap(after(value, *held) if held else value, axis, size, bit)

    def send_z(step, z):
        early = [("z", step - 1, z)] if step >= 1 else []
        if step >= 2 and z == far[-1]:
            early += [("x", step - 2, 0)]
        if step == last and step >= 3:
            early += [("c", step - 2 if z == far[-1] else step - 3)]
        send(("z", step, z), block(step, z), "grp", groups, 2 * z, *early)

    def collect(step):
        parts = [block(step, 0)] + [sent["z", step, z] for z in range(1, high)]
        owns[step] = jnp.concatenate(parts, axis=0)

    def send_x(step, cuts, between):
        total = owns[step].shape[0]
        cuts = [0] + [total * cut // 384 // 16 * 16 for cut in cuts] + [total]
        parts = [name for name in sent if name[:2] == ("x", step - 1)]
        for part in range(len(cuts) - 1):
            value = owns[step][cuts[part] : cuts[part + 1]]
            early = parts if part == 0 else between[part - 1]
            send(("x", step, part), value, "blk", members, 2, *early)

    def send_c(step, *early):
        across = [sent[name] for name in list(sent) if name[:2] == ("x", step)]
        pairs[step] = jnp.concatenate([owns[step]] + across, axis=0)
        send(("c", step), pairs[step], "blk", members, 1, *early)

    def gram(first, step, states, cols):
        pieces = []
        for k in range(first, step + 1):
            pieces += [pairs[k], sent["c", k]]
        mine = [owns[k] for k in range(step + 1)]
        return gram_step(
            first, me, mine, pieces, states, cols, (0, 2, 1, 3), chunks, groups
        )

    far = [high // 2] + [z for z in range(1, high) if z != high // 2]
    cut = first_send.shape[0] // 32 * 16
    done["rest"] = rest_send
    send(("y", 0), first_send[:cut], "grp", groups, 1)
    send(("y", 1), first_send[cut:], "grp", groups, 1, "rest")
    send(("y", 2), rest_send, "grp", groups, 1, ("y", 0))
    first_near = jnp.concatenate([sent["y", 0], sent["y", 1]], axis=0)
    for z in far:
        send_z(0, z)
    for step in range(1, count):
        collect(step - 1)
        for z in far:
            send_z(step, z)
        send_x(step - 1, [], [])
        send_c(step - 1, *[("z", step, z) for z in far])
    collect(last)
    states, cols = gram(0, last - 2, [], [])
    done["gram", 0] = cols[-1]
    states, cols = gram(last - 1, last - 1, states, cols)
    done["gram", 1] = cols[-1]
    send_x(last, [208, 352], [[("gram", 0), ("c", last - 1)], [("gram", 1)]])
    send_c(last)
    result = gram(last, last, states, cols)
    homeward = lax.all_to_all(result, ("grp", "blk"), 0, 0, tiled=True)
    return tail(homeward, slots, capacity, members).reshape(row_count)


def solution(mesh):
    in_specs = (P(("grp", "blk"), None), P(("grp", "blk")))
    out_specs = P(("grp", "blk"))
    return jax.shard_map(
        on_device, mesh=mesh, in_specs=in_specs, out_specs=out_specs, check_vma=False
    )
```

```python
import functools

import jax
import jax.numpy as jnp
from jax import lax
from jax.experimental import pallas as pl
from jax.experimental.pallas import tpu as pltpu
from jax.sharding import PartitionSpec as P

sentinel = -3.0
epsilon = 1e-06
dead_mark = 2.0
dead_bias = -8.0
lanes = 128
smem = pl.BlockSpec(memory_space=pltpu.SMEM)
vmem = pl.BlockSpec(memory_space=pltpu.VMEM)


def chunk_sizes(capacity):
    count = 4 if capacity % 64 == 0 else 3
    return (capacity // count,) * count


def after(value, *earlier):
    return lax.optimization_barrier((value,) + earlier)[0]


def swap(value, axis, size, bit):
    return lax.ppermute(value, axis, [(i, i ^ bit) for i in range(size)])


def place(me, slots, normed, capacity, first, size, groups, low):
    shape = (groups // 2, size, 1)
    spot = lax.broadcasted_iota(jnp.int32, shape, 1) + first
    group = (lax.broadcasted_iota(jnp.int32, shape, 0) * 2 + low) ^ me
    wanted = (group * capacity + spot).reshape(groups // 2 * size, 1)
    pick = jnp.where(wanted == slots, 1.0, 0.0)
    live = jnp.max(pick, axis=1, keepdims=True)
    placed = jnp.dot(pick.astype(jnp.bfloat16), normed, preferred_element_type=jnp.float32)
    lane = lax.broadcasted_iota(jnp.int32, (1, placed.shape[1]), 1)
    mark = jnp.where(lane == 0, dead_mark, 0.0)
    return (placed + (1.0 - live) * mark).astype(jnp.bfloat16)


def flat(slot_ref):
    return jnp.concatenate([slot_ref[q : q + 1, :] for q in range(slot_ref.shape[0])], axis=1)


def first_kernel(capacity, chunks, groups, me_ref, slot_ref, x_ref, normed_ref, send_ref):
    wide = x_ref[...].astype(jnp.float32)
    normed_ref[...] = (
        wide * lax.rsqrt(jnp.sum(wide * wide, axis=-1, keepdims=True) + epsilon)
    ).astype(jnp.bfloat16)
    send_ref[...] = place(
        me_ref[0], flat(slot_ref), normed_ref[...], capacity, 0, chunks[0], groups, 1
    )


def rest_kernel(capacity, chunks, groups, me_ref, slot_ref, normed_ref, *out_refs):
    keeps, send_refs = out_refs[:-2], out_refs[-2:]
    slots, normed = flat(slot_ref), normed_ref[...]
    first, row = 0, 0
    for step, size in enumerate(chunks):
        placed = place(me_ref[0], slots, normed, capacity, first, size, groups, 1) if step else None
        if step == 1:
            send_refs[0][...] = placed
        elif step > 1:
            send_refs[1][row : row + placed.shape[0], :] = placed
            row += placed.shape[0]
        first += size
    first = 0
    for step, size in enumerate(chunks):
        keeps[step][...] = place(me_ref[0], slots, normed, capacity, first, size, groups, 0)
        first += size


def head(me, embeddings, slots, capacity, chunks, groups):
    rows, features = embeddings.shape
    half = [groups // 2 * size for size in chunks]

    def shape(count):
        return jax.ShapeDtypeStruct((count, features), jnp.bfloat16)

    def cost(count):
        return pl.CostEstimate(
            flops=2 * count * rows * features,
            bytes_accessed=2 * (rows + count) * features,
            transcendentals=0,
        )

    params = pltpu.CompilerParams(vmem_limit_bytes=24 * 2**20)
    normed, first_send = pl.pallas_call(
        functools.partial(first_kernel, capacity, chunks, groups),
        in_specs=[smem, vmem, vmem],
        out_specs=[vmem, vmem],
        out_shape=[shape(rows), shape(half[0])],
        compiler_params=params,
        cost_estimate=cost(half[0]),
        name="place_first",
    )(me, slots, embeddings)
    *keeps, next_send, rest_send = pl.pallas_call(
        functools.partial(rest_kernel, capacity, chunks, groups),
        in_specs=[smem, vmem, vmem],
        out_specs=[vmem] * (len(chunks) + 2),
        out_shape=[shape(count) for count in half + [half[1], sum(half[2:])]],
        compiler_params=params,
        cost_estimate=cost(2 * sum(half) - half[0]),
        name="place_rest",
    )(me, slots, normed)
    return keeps, first_send, next_send, rest_send


def lane_fold(values):
    best = values[:, :lanes]
    for start in range(lanes, values.shape[1], lanes):
        best = jnp.maximum(best, values[:, start : start + lanes])
    return best


def gram_body(own_refs, piece_ref, row_refs, col_ref, col_start, holds_own):
    step = len(own_refs) - 1
    tile = 256
    nt = (((1,), (1,)), ((), ()))
    if holds_own:
        row_refs[step][...] = jnp.full(row_refs[step].shape, sentinel, jnp.float32)
    for first in range(0, piece_ref.shape[0], tile):
        x = piece_ref[first : first + tile, :]
        marks = x[:, :lanes].astype(jnp.float32).T[0:1, :]
        col_bias = jnp.where(marks > 1.5, dead_bias, 0.0)
        col_best = jnp.full((1, tile), sentinel, jnp.float32)
        for j in range(step + 1):
            own = own_refs[j][...]
            scores = lax.dot_general(own, x, nt, preferred_element_type=jnp.float32)
            usable = scores + col_bias
            if j == step:
                if holds_own and first < own.shape[0]:
                    rows = lax.broadcasted_iota(jnp.int32, usable.shape, 0)
                    cols = lax.broadcasted_iota(jnp.int32, usable.shape, 1)
                    usable = jnp.where(rows - cols == first, dead_bias, usable)
            else:
                row_bias = jnp.where(own[:, 0:1].astype(jnp.float32) > 1.5, dead_bias, 0.0)
                col_best = jnp.maximum(
                    col_best, jnp.max(scores + row_bias, axis=0, keepdims=True)
                )
            row_refs[j][...] = jnp.maximum(row_refs[j][...], lane_fold(usable))
        col_ref[0:1, col_start + first : col_start + first + tile] = col_best


def gram_kernel(first, step, pieces, *refs):
    news = step + 1 - first
    owns, refs = refs[: step + 1], refs[step + 1 :]
    blocks, refs = refs[: pieces * news], refs[pieces * news :]
    states, refs = refs[:first], refs[first:]
    rows, cols = refs[: step + 1], refs[step + 1 :]
    for state, row in zip(states, rows):
        row[...] = state[...]
    for k in range(news):
        now = first + k + 1
        for p in range(pieces):
            block = blocks[pieces * k + p]
            start = p * block.shape[0]
            gram_body(owns[:now], block, rows[:now], cols[k], start, p == 0)


def gram_last_kernel(step, relatives, chunks, groups, me_ref, *refs):
    members = len(relatives)
    owns, block, refs = refs[: step + 1], refs[step + 1], refs[step + 2 :]
    states, refs = refs[: step + 1], refs[step + 1 :]
    cols, refs = refs[: step + 1], refs[step + 1 :]
    out_ref, col, table = refs[:3]
    rows = refs[3:]
    for state, row in zip(states, rows):
        row[...] = state[...]
    gram_body(owns, block, rows, col, 0, False)
    first = 0
    for k, size in enumerate(chunks):
        row_k = jnp.max(rows[k][...].T, axis=0, keepdims=True)
        count = groups * size
        for p, relative in enumerate(relatives):
            source, shift = (col, 2 * count) if k == step and p >= 2 else (cols[k], 0)
            for r in range(groups):
                start = p * count + r * size - shift
                best = source[0:1, start : start + size]
                if p == 0:
                    best = jnp.maximum(best, row_k[:, r * size : (r + 1) * size])
                row = r * members + p
                table[row : row + 1, first : first + size] = best
        first += size
    for r in range(groups):
        for p, relative in enumerate(relatives):
            row = r * members + p
            target = (me_ref[0] ^ r) * members + (me_ref[1] ^ relative)
            out_ref[pl.ds(target, 1), :] = table[row : row + 1, :]


def gram_params(owns, blocks):
    features = owns[0].shape[1]
    mine, others = sum(own.shape[0] for own in owns), sum(block.shape[0] for block in blocks)
    return dict(
        compiler_params=pltpu.CompilerParams(vmem_limit_bytes=24 * 2**20),
        cost_estimate=pl.CostEstimate(
            flops=2 * mine * others * features,
            bytes_accessed=2 * features * (mine + others),
            transcendentals=0,
        ),
    )


def gram_step(first, owns, blocks, states, pieces):
    step = len(owns) - 1
    row_shapes = [(own.shape[0], lanes) for own in owns]
    col_shapes = [(1, pieces * 2 * own.shape[0]) for own in owns[first:]]
    results = pl.pallas_call(
        functools.partial(gram_kernel, first, step, pieces),
        in_specs=[vmem] * (step + 1 + len(blocks) + first),
        out_specs=[vmem] * len(row_shapes + col_shapes),
        out_shape=[jax.ShapeDtypeStruct(s, jnp.float32) for s in row_shapes + col_shapes],
        name="gram_step",
        **gram_params(owns, blocks),
    )(*owns, *blocks, *states)
    return list(results[: step + 1]), list(results[step + 1 :])


def gram_last(me, owns, block, states, cols, relatives, chunks, groups):
    step = len(owns) - 1
    members = len(relatives)
    shape = (groups * members, sum(chunks))
    return pl.pallas_call(
        functools.partial(gram_last_kernel, step, relatives, chunks, groups),
        in_specs=[smem] + [vmem] * (3 * step + 4),
        out_specs=vmem,
        out_shape=jax.ShapeDtypeStruct(shape, jnp.float32),
        scratch_shapes=[pltpu.VMEM((1, block.shape[0]), jnp.float32), pltpu.VMEM(shape, jnp.float32)]
        + [pltpu.VMEM((own.shape[0], lanes), jnp.float32) for own in owns],
        name="gram_last",
        **gram_params(owns, [block]),
    )(me, *owns, block, *states, *cols)


def tail_kernel(capacity, members, slot_ref, part_ref, out_ref, table):
    groups = part_ref.shape[0] // members
    width = table.shape[1]
    table[...] = jnp.full(table.shape, sentinel, jnp.float32)
    for g in range(groups):
        table[g : g + 1, :capacity] = jnp.max(
            part_ref[g * members : (g + 1) * members, :], axis=0, keepdims=True
        )
    lane = lax.broadcasted_iota(jnp.int32, (lanes, lanes), 1)
    for q in range(out_ref.shape[0]):
        slot = jnp.broadcast_to(slot_ref[q : q + 1, :], (lanes, lanes)).T
        best = jnp.full((lanes, lanes), sentinel, jnp.float32)
        for g in range(groups):
            for c in range(0, width, lanes):
                entry = table[g : g + 1, c : c + lanes]
                best = jnp.maximum(
                    best, jnp.where(slot - (g * capacity + c) == lane, entry, sentinel)
                )
        out_ref[q : q + 1, :] = jnp.max(best.T, axis=0, keepdims=True)


def tail(partials, slots, capacity, members):
    groups = partials.shape[0] // members
    width = -(-capacity // lanes) * lanes
    return pl.pallas_call(
        functools.partial(tail_kernel, capacity, members),
        in_specs=[vmem, vmem],
        out_specs=vmem,
        out_shape=jax.ShapeDtypeStruct(slots.shape, jnp.float32),
        scratch_shapes=[pltpu.VMEM((groups, width), jnp.float32)],
        name="pick_rows",
    )(slots, partials)


def on_device(embeddings, send_slot):
    row_count, features = embeddings.shape
    groups = lax.axis_size("grp")
    members = lax.axis_size("blk")
    slot_count = 2 * row_count
    capacity = slot_count // groups
    chunks = chunk_sizes(capacity)
    me = jnp.stack([lax.axis_index("grp"), lax.axis_index("blk")]).astype(jnp.int32)
    slots = send_slot.reshape(row_count // lanes, lanes)
    keeps, first_send, next_send, rest_send = head(me, embeddings, slots, capacity, chunks, groups)
    count, high = len(chunks), groups // 2
    last = count - 1

    sent, owns, done, pairs = {}, {}, {}, {}

    def rows(value, index, size):
        return value[index * size : (index + 1) * size]

    def block(step, z):
        size = chunks[step]
        near = first_near if step == 0 else sent["y", min(step, 2) + 1]
        skip = sum(chunks[2:step]) * high
        return jnp.concatenate(
            [rows(keeps[step], z, size), rows(near[skip:], z, size)], axis=0
        )

    def send(key, value, axis, size, bit, *earlier):
        held = [done[name] if name in done else sent[name] for name in earlier]
        sent[key] = swap(after(value, *held) if held else value, axis, size, bit)

    def send_z(step, z):
        early = [("z", step - 1, z)] if step >= 1 else []
        if step >= 2 and z == far[-1]:
            early += [("x", step - 2, 0)]
        if step == last and step >= 3:
            early += [("c", step - 2 if z == far[-1] else step - 3)]
        send(("z", step, z), block(step, z), "grp", groups, 2 * z, *early)

    def send_near_z():
        blocks = jnp.concatenate([block(step, 1) for step in range(1, count)], axis=0)
        send(("n",), blocks, "grp", groups, 2, ("z", 0, 1))

    def collect(step):
        parts = [block(step, 0)]
        for z in range(1, high):
            if z == 1 and step >= 1:
                start = 2 * sum(chunks[1:step])
                parts.append(sent["n",][start : start + 2 * chunks[step]])
            else:
                parts.append(sent["z", step, z])
        owns[step] = jnp.concatenate(parts, axis=0)

    def send_x(step, cuts, between):
        total = owns[step].shape[0]
        cuts = [0] + [total * cut // 384 // 16 * 16 for cut in cuts] + [total]
        parts = [name for name in sent if name[:2] == ("x", step - 1)]
        for part in range(len(cuts) - 1):
            value = owns[step][cuts[part] : cuts[part + 1]]
            early = parts if part == 0 else between[part - 1]
            send(("x", step, part), value, "blk", members, 2, *early)

    def send_c(step, *early):
        across = [sent[name] for name in list(sent) if name[:2] == ("x", step)]
        pairs[step] = jnp.concatenate([owns[step]] + across, axis=0)
        send(("c", step), pairs[step], "blk", members, 1, *early)

    far = [high // 2] + [z for z in range(1, high) if z != high // 2]
    cut = first_send.shape[0] // 32 * 16
    done["rest"] = rest_send
    send(("y", 0), first_send[:cut], "grp", groups, 1)
    send(("y", 1), first_send[cut:], "grp", groups, 1, "rest")
    send(("y", 2), next_send, "grp", groups, 1, ("y", 0))
    send(("y", 3), rest_send, "grp", groups, 1, ("y", 0))
    first_near = jnp.concatenate([sent["y", 0], sent["y", 1]], axis=0)
    for z in far:
        send_z(0, z)
    far.remove(1)
    for step in range(1, count):
        collect(step - 1)
        for z in far:
            send_z(step, z)
        if step == 1:
            send_near_z()
        send_x(step - 1, [], [])
        send_c(step - 1, *[("z", step, z) for z in far])
    collect(last)
    mine = [owns[k] for k in range(count)]
    blocks = [block for k in range(last) for block in (pairs[k], sent["c", k])]
    states, cols = gram_step(0, mine[:last], blocks, [], 2)
    done["gram"] = cols[-1]
    send_x(last, [304], [["gram"]])
    send_c(last)
    states, half = gram_step(last, mine, [pairs[last]], states, 1)
    result = gram_last(
        me, mine, sent["c", last], states, cols + half, (0, 2, 1, 3), chunks, groups
    )
    homeward = lax.all_to_all(result, ("grp", "blk"), 0, 0, tiled=True)
    return tail(homeward, slots, capacity, members).reshape(row_count)


def solution(mesh):
    in_specs = (P(("grp", "blk"), None), P(("grp", "blk")))
    out_specs = P(("grp", "blk"))
    return jax.shard_map(
        on_device, mesh=mesh, in_specs=in_specs, out_specs=out_specs, check_vma=False
    )
```

```python
import functools

import jax
import jax.numpy as jnp
from jax import lax
from jax.experimental import pallas as pl
from jax.experimental.pallas import tpu as pltpu
from jax.sharding import PartitionSpec as P

sentinel = -3.0
epsilon = 1e-06
dead_mark = 2.0
dead_bias = -8.0
lanes = 128
smem = pl.BlockSpec(memory_space=pltpu.SMEM)
vmem = pl.BlockSpec(memory_space=pltpu.VMEM)
hbm = pl.BlockSpec(memory_space=pltpu.HBM)


def chunk_sizes(capacity):
    count = 4 if capacity % 64 == 0 else 3
    return (capacity // count,) * count


def after(value, *earlier):
    return lax.optimization_barrier((value,) + earlier)[0]


def swap(value, axis, size, bit):
    return lax.ppermute(value, axis, [(i, i ^ bit) for i in range(size)])


def place(me, slots, normed, capacity, first, size, groups, low):
    shape = (groups // 2, size, 1)
    spot = lax.broadcasted_iota(jnp.int32, shape, 1) + first
    group = (lax.broadcasted_iota(jnp.int32, shape, 0) * 2 + low) ^ me
    wanted = (group * capacity + spot).reshape(groups // 2 * size, 1)
    pick = jnp.where(wanted == slots, 1.0, 0.0)
    live = jnp.max(pick, axis=1, keepdims=True)
    placed = jnp.dot(pick.astype(jnp.bfloat16), normed, preferred_element_type=jnp.float32)
    lane = lax.broadcasted_iota(jnp.int32, (1, placed.shape[1]), 1)
    mark = jnp.where(lane == 0, dead_mark, 0.0)
    return (placed + (1.0 - live) * mark).astype(jnp.bfloat16)


def flat(slot_ref):
    return jnp.concatenate([slot_ref[q : q + 1, :] for q in range(slot_ref.shape[0])], axis=1)


def first_kernel(
    capacity, chunks, groups, me_ref, slots_hbm, x_hbm, normed_ref, send_ref, slot_ref, x_ref, sems
):
    copies = [pltpu.make_async_copy(slots_hbm, slot_ref, sems.at[0])]
    part = x_ref.shape[0] // 3
    for k in range(3):
        span = pl.ds(k * part, part)
        copies.append(pltpu.make_async_copy(x_hbm.at[span], x_ref.at[span], sems.at[k + 1]))
    for copy in copies:
        copy.start()
    for k in range(3):
        copies[k + 1].wait()
        wide = x_ref[k * part : (k + 1) * part, :].astype(jnp.float32)
        normed_ref[k * part : (k + 1) * part, :] = (
            wide * lax.rsqrt(jnp.sum(wide * wide, axis=-1, keepdims=True) + epsilon)
        ).astype(jnp.bfloat16)
    copies[0].wait()
    send_ref[...] = place(
        me_ref[0], flat(slot_ref), normed_ref[...], capacity, 0, chunks[0], groups, 1
    )


def rest_kernel(capacity, chunks, groups, me_ref, slot_ref, normed_ref, *out_refs):
    keeps, send_refs = out_refs[:-2], out_refs[-2:]
    slots, normed = flat(slot_ref), normed_ref[...]
    first, row = 0, 0
    for step, size in enumerate(chunks):
        placed = place(me_ref[0], slots, normed, capacity, first, size, groups, 1) if step else None
        if step == 1:
            send_refs[0][...] = placed
        elif step > 1:
            send_refs[1][row : row + placed.shape[0], :] = placed
            row += placed.shape[0]
        first += size
    first = 0
    for step, size in enumerate(chunks):
        keeps[step][...] = place(me_ref[0], slots, normed, capacity, first, size, groups, 0)
        first += size


def head(me, embeddings, slots, capacity, chunks, groups):
    rows, features = embeddings.shape
    half = [groups // 2 * size for size in chunks]

    def shape(count):
        return jax.ShapeDtypeStruct((count, features), jnp.bfloat16)

    def cost(count):
        return pl.CostEstimate(
            flops=2 * count * rows * features,
            bytes_accessed=2 * (rows + count) * features,
            transcendentals=0,
        )

    params = pltpu.CompilerParams(vmem_limit_bytes=24 * 2**20)
    normed, first_send = pl.pallas_call(
        functools.partial(first_kernel, capacity, chunks, groups),
        in_specs=[smem, hbm, hbm],
        out_specs=[vmem, vmem],
        out_shape=[shape(rows), shape(half[0])],
        scratch_shapes=[
            pltpu.VMEM(slots.shape, jnp.int32),
            pltpu.VMEM(embeddings.shape, embeddings.dtype),
            pltpu.SemaphoreType.DMA((4,)),
        ],
        compiler_params=params,
        cost_estimate=cost(half[0]),
        name="place_first",
    )(me, slots, embeddings)
    *keeps, next_send, rest_send = pl.pallas_call(
        functools.partial(rest_kernel, capacity, chunks, groups),
        in_specs=[smem, vmem, vmem],
        out_specs=[vmem] * (len(chunks) + 2),
        out_shape=[shape(count) for count in half + [half[1], sum(half[2:])]],
        compiler_params=params,
        cost_estimate=cost(2 * sum(half) - half[0]),
        name="place_rest",
    )(me, slots, normed)
    return keeps, first_send, next_send, rest_send


def lane_fold(values):
    best = values[:, :lanes]
    for start in range(lanes, values.shape[1], lanes):
        best = jnp.maximum(best, values[:, start : start + lanes])
    return best


def gram_body(own_refs, piece_ref, row_refs, col_ref, col_start, holds_own):
    step = len(own_refs) - 1
    tile = 256
    nt = (((1,), (1,)), ((), ()))
    if holds_own:
        row_refs[step][...] = jnp.full(row_refs[step].shape, sentinel, jnp.float32)
    for first in range(0, piece_ref.shape[0], tile):
        x = piece_ref[first : first + tile, :]
        marks = x[:, :lanes].astype(jnp.float32).T[0:1, :]
        col_bias = jnp.where(marks > 1.5, dead_bias, 0.0)
        col_best = jnp.full((1, tile), sentinel, jnp.float32)
        for j in range(step + 1):
            own = own_refs[j][...]
            scores = lax.dot_general(own, x, nt, preferred_element_type=jnp.float32)
            usable = scores + col_bias
            if j == step:
                if holds_own and first < own.shape[0]:
                    rows = lax.broadcasted_iota(jnp.int32, usable.shape, 0)
                    cols = lax.broadcasted_iota(jnp.int32, usable.shape, 1)
                    usable = jnp.where(rows - cols == first, dead_bias, usable)
            else:
                row_bias = jnp.where(own[:, 0:1].astype(jnp.float32) > 1.5, dead_bias, 0.0)
                col_best = jnp.maximum(
                    col_best, jnp.max(scores + row_bias, axis=0, keepdims=True)
                )
            row_refs[j][...] = jnp.maximum(row_refs[j][...], lane_fold(usable))
        col_ref[0:1, col_start + first : col_start + first + tile] = col_best


def gram_kernel(first, step, pieces, *refs):
    news = step + 1 - first
    owns, refs = refs[: step + 1], refs[step + 1 :]
    blocks, refs = refs[: pieces * news], refs[pieces * news :]
    states, refs = refs[:first], refs[first:]
    rows, cols = refs[: step + 1], refs[step + 1 :]
    for state, row in zip(states, rows):
        row[...] = state[...]
    for k in range(news):
        now = first + k + 1
        for p in range(pieces):
            block = blocks[pieces * k + p]
            start = p * block.shape[0]
            gram_body(owns[:now], block, rows[:now], cols[k], start, p == 0)


def gram_last_kernel(step, relatives, chunks, groups, me_ref, *refs):
    members = len(relatives)
    owns, block, refs = refs[: step + 1], refs[step + 1], refs[step + 2 :]
    states, refs = refs[: step + 1], refs[step + 1 :]
    cols, refs = refs[: step + 1], refs[step + 1 :]
    out_ref, col, table = refs[:3]
    rows = refs[3:]
    for state, row in zip(states, rows):
        row[...] = state[...]
    gram_body(owns, block, rows, col, 0, False)
    first = 0
    for k, size in enumerate(chunks):
        row_k = jnp.max(rows[k][...].T, axis=0, keepdims=True)
        count = groups * size
        for p, relative in enumerate(relatives):
            source, shift = (col, 2 * count) if k == step and p >= 2 else (cols[k], 0)
            for r in range(groups):
                start = p * count + r * size - shift
                best = source[0:1, start : start + size]
                if p == 0:
                    best = jnp.maximum(best, row_k[:, r * size : (r + 1) * size])
                row = r * members + p
                table[row : row + 1, first : first + size] = best
        first += size
    for r in range(groups):
        for p, relative in enumerate(relatives):
            row = r * members + p
            target = (me_ref[0] ^ r) * members + (me_ref[1] ^ relative)
            out_ref[pl.ds(target, 1), :] = table[row : row + 1, :]


def gram_params(owns, blocks):
    features = owns[0].shape[1]
    mine, others = sum(own.shape[0] for own in owns), sum(block.shape[0] for block in blocks)
    return dict(
        compiler_params=pltpu.CompilerParams(vmem_limit_bytes=24 * 2**20),
        cost_estimate=pl.CostEstimate(
            flops=2 * mine * others * features,
            bytes_accessed=2 * features * (mine + others),
            transcendentals=0,
        ),
    )


def gram_step(first, owns, blocks, states, pieces):
    step = len(owns) - 1
    row_shapes = [(own.shape[0], lanes) for own in owns]
    col_shapes = [(1, pieces * 2 * own.shape[0]) for own in owns[first:]]
    results = pl.pallas_call(
        functools.partial(gram_kernel, first, step, pieces),
        in_specs=[vmem] * (step + 1 + len(blocks) + first),
        out_specs=[vmem] * len(row_shapes + col_shapes),
        out_shape=[jax.ShapeDtypeStruct(s, jnp.float32) for s in row_shapes + col_shapes],
        name="gram_step",
        **gram_params(owns, blocks),
    )(*owns, *blocks, *states)
    return list(results[: step + 1]), list(results[step + 1 :])


def gram_last(me, owns, block, states, cols, relatives, chunks, groups):
    step = len(owns) - 1
    members = len(relatives)
    shape = (groups * members, sum(chunks))
    return pl.pallas_call(
        functools.partial(gram_last_kernel, step, relatives, chunks, groups),
        in_specs=[smem] + [vmem] * (3 * step + 4),
        out_specs=vmem,
        out_shape=jax.ShapeDtypeStruct(shape, jnp.float32),
        scratch_shapes=[pltpu.VMEM((1, block.shape[0]), jnp.float32), pltpu.VMEM(shape, jnp.float32)]
        + [pltpu.VMEM((own.shape[0], lanes), jnp.float32) for own in owns],
        name="gram_last",
        **gram_params(owns, [block]),
    )(me, *owns, block, *states, *cols)


def tail_kernel(capacity, members, slot_ref, part_ref, out_ref, table):
    groups = part_ref.shape[0] // members
    width = table.shape[1]
    table[...] = jnp.full(table.shape, sentinel, jnp.float32)
    for g in range(groups):
        table[g : g + 1, :capacity] = jnp.max(
            part_ref[g * members : (g + 1) * members, :], axis=0, keepdims=True
        )
    lane = lax.broadcasted_iota(jnp.int32, (lanes, lanes), 1)
    for q in range(out_ref.shape[0]):
        slot = jnp.broadcast_to(slot_ref[q : q + 1, :], (lanes, lanes)).T
        best = jnp.full((lanes, lanes), sentinel, jnp.float32)
        for g in range(groups):
            for c in range(0, width, lanes):
                entry = table[g : g + 1, c : c + lanes]
                best = jnp.maximum(
                    best, jnp.where(slot - (g * capacity + c) == lane, entry, sentinel)
                )
        out_ref[q : q + 1, :] = jnp.max(best.T, axis=0, keepdims=True)


def tail(partials, slots, capacity, members):
    groups = partials.shape[0] // members
    width = -(-capacity // lanes) * lanes
    return pl.pallas_call(
        functools.partial(tail_kernel, capacity, members),
        in_specs=[vmem, vmem],
        out_specs=vmem,
        out_shape=jax.ShapeDtypeStruct(slots.shape, jnp.float32),
        scratch_shapes=[pltpu.VMEM((groups, width), jnp.float32)],
        name="pick_rows",
    )(slots, partials)


def on_device(embeddings, send_slot):
    row_count, features = embeddings.shape
    groups = lax.axis_size("grp")
    members = lax.axis_size("blk")
    slot_count = 2 * row_count
    capacity = slot_count // groups
    chunks = chunk_sizes(capacity)
    me = jnp.stack([lax.axis_index("grp"), lax.axis_index("blk")]).astype(jnp.int32)
    slots = send_slot.reshape(row_count // lanes, lanes)
    keeps, first_send, next_send, rest_send = head(me, embeddings, slots, capacity, chunks, groups)
    count, high = len(chunks), groups // 2
    last = count - 1

    sent, owns, done, pairs = {}, {}, {}, {}

    def rows(value, index, size):
        return value[index * size : (index + 1) * size]

    def block(step, z):
        size = chunks[step]
        near = sent["y", min(step, 2) + 1] if step else sent["y", int(z < high // 2)]
        skip = sum(chunks[2:step]) * high if step else 0
        index = z if step else z % (high // 2)
        return jnp.concatenate(
            [rows(keeps[step], z, size), rows(near[skip:], index, size)], axis=0
        )

    def send(key, value, axis, size, bit, *earlier):
        held = [done[name] if name in done else sent[name] for name in earlier]
        sent[key] = swap(after(value, *held) if held else value, axis, size, bit)

    def send_z(step, z):
        early = [("z", step - 1, z)] if step >= 1 else []
        if step >= 2 and z == far[-1]:
            early += [("x", step - 2, 0)]
        if step == last and step >= 3:
            early += [("c", step - 3)]
        send(("z", step, z), block(step, z), "grp", groups, 2 * z, *early)

    def send_near_z():
        blocks = jnp.concatenate([block(step, 1) for step in range(2, count)], axis=0)
        send(("n",), blocks, "grp", groups, 2, ("z", 1, 1), ("x", 0, 0))

    def collect(step):
        parts = [block(step, 0)]
        for z in range(1, high):
            if z == 1 and step >= 2:
                start = 2 * sum(chunks[2:step])
                parts.append(sent["n",][start : start + 2 * chunks[step]])
            else:
                parts.append(sent["z", step, z])
        owns[step] = jnp.concatenate(parts, axis=0)

    def send_x(step, cuts, between, *earlier):
        total = owns[step].shape[0]
        cuts = [0] + [total * cut // 384 // 16 * 16 for cut in cuts] + [total]
        parts = [name for name in sent if name[:2] == ("x", step - 1)]
        for part in range(len(cuts) - 1):
            value = owns[step][cuts[part] : cuts[part + 1]]
            early = parts + list(earlier) if part == 0 else between[part - 1]
            send(("x", step, part), value, "blk", members, 2, *early)

    def send_c(step, *early):
        across = [sent[name] for name in list(sent) if name[:2] == ("x", step)]
        pairs[step] = jnp.concatenate([owns[step]] + across, axis=0)
        send(("c", step), pairs[step], "blk", members, 1, *early)

    far = [high // 2] + [z for z in range(1, high) if z != high // 2]
    cut = first_send.shape[0] // 2
    done["rest"] = rest_send
    send(("y", 0), first_send[cut:], "grp", groups, 1)
    send(("y", 1), first_send[:cut], "grp", groups, 1, "rest")
    send(("y", 2), next_send, "grp", groups, 1, ("y", 0))
    send(("y", 3), rest_send, "grp", groups, 1, ("y", 0))
    for z in far:
        send_z(0, z)
    for step in range(1, count):
        collect(step - 1)
        if step == 2:
            far.remove(1)
            send_near_z()
        for z in far:
            send_z(step, z)
        send_x(step - 1, [], [])
        if step == last:
            send(("o",), owns[step - 1], "blk", members, 1)
            pairs[step - 1] = jnp.concatenate([owns[step - 1], sent["x", step - 1, 0]], axis=0)
            early = [("z", step, z) for z in far] + [("c", step - 2)]
            send(("p",), sent["x", step - 1, 0], "blk", members, 1, *early)
            sent["c", step - 1] = jnp.concatenate([sent["o",], sent["p",]], axis=0)
        else:
            send_c(step - 1, *[("z", step, z) for z in far])
    collect(last)
    mine = [owns[k] for k in range(count)]
    blocks = [block for k in range(last) for block in (pairs[k], sent["c", k])]
    states, cols = gram_step(0, mine[:last], blocks, [], 2)
    done["gram"] = cols[-1]
    send_x(last, [304], [["gram"]], ("o",))
    send_c(last)
    states, half = gram_step(last, mine, [pairs[last]], states, 1)
    result = gram_last(
        me, mine, sent["c", last], states, cols + half, (0, 2, 1, 3), chunks, groups
    )
    homeward = lax.all_to_all(result, ("grp", "blk"), 0, 0, tiled=True)
    return tail(homeward, slots, capacity, members).reshape(row_count)


def solution(mesh):
    in_specs = (P(("grp", "blk"), None), P(("grp", "blk")))
    out_specs = P(("grp", "blk"))
    return jax.shard_map(
        on_device, mesh=mesh, in_specs=in_specs, out_specs=out_specs, check_vma=False
    )
```

```python
import functools

import jax
import jax.numpy as jnp
from jax import lax
from jax.experimental import pallas as pl
from jax.experimental.pallas import tpu as pltpu
from jax.sharding import PartitionSpec as P

sentinel = -3.0
epsilon = 1e-06
dead_mark = 2.0
dead_bias = -8.0
lanes = 128
smem = pl.BlockSpec(memory_space=pltpu.SMEM)
vmem = pl.BlockSpec(memory_space=pltpu.VMEM)


def chunk_sizes(capacity):
    count = 4 if capacity % 64 == 0 else 3
    return (capacity // count,) * count


def after(value, *earlier):
    return lax.optimization_barrier((value,) + earlier)[0]


def swap(value, axis, size, bit):
    return lax.ppermute(value, axis, [(i, i ^ bit) for i in range(size)])


def place(me, slots, normed, capacity, first, size, groups, low, turn=0):
    high = groups // 2
    shape = (high, size, 1)
    spot = lax.broadcasted_iota(jnp.int32, shape, 1) + first
    group = ((lax.broadcasted_iota(jnp.int32, shape, 0) + turn) % high * 2 + low) ^ me
    wanted = (group * capacity + spot).reshape(groups // 2 * size, 1)
    pick = jnp.where(wanted == slots, 1.0, 0.0)
    live = jnp.max(pick, axis=1, keepdims=True)
    placed = jnp.dot(pick.astype(jnp.bfloat16), normed, preferred_element_type=jnp.float32)
    lane = lax.broadcasted_iota(jnp.int32, (1, placed.shape[1]), 1)
    mark = jnp.where(lane == 0, dead_mark, 0.0)
    return (placed + (1.0 - live) * mark).astype(jnp.bfloat16)


def flat(slot_ref):
    return jnp.concatenate([slot_ref[q : q + 1, :] for q in range(slot_ref.shape[0])], axis=1)


def first_kernel(capacity, chunks, groups, me_ref, slot_ref, x_ref, normed_ref, send_ref):
    wide = x_ref[...].astype(jnp.float32)
    normed_ref[...] = (
        wide * lax.rsqrt(jnp.sum(wide * wide, axis=-1, keepdims=True) + epsilon)
    ).astype(jnp.bfloat16)
    send_ref[...] = place(
        me_ref[0], flat(slot_ref), normed_ref[...], capacity, 0, chunks[0], groups, 1, groups // 4
    )


def rest_kernel(capacity, chunks, groups, me_ref, slot_ref, normed_ref, *out_refs):
    keeps, send_refs = out_refs[:-2], out_refs[-2:]
    slots, normed = flat(slot_ref), normed_ref[...]
    first, row = 0, 0
    for step, size in enumerate(chunks):
        placed = place(me_ref[0], slots, normed, capacity, first, size, groups, 1) if step else None
        if step == 1:
            send_refs[0][...] = placed
        elif step > 1:
            send_refs[1][row : row + placed.shape[0], :] = placed
            row += placed.shape[0]
        first += size
    first = 0
    for step, size in enumerate(chunks):
        keeps[step][...] = place(me_ref[0], slots, normed, capacity, first, size, groups, 0)
        first += size


def head(me, embeddings, slots, capacity, chunks, groups):
    rows, features = embeddings.shape
    half = [groups // 2 * size for size in chunks]

    def shape(count):
        return jax.ShapeDtypeStruct((count, features), jnp.bfloat16)

    def cost(count):
        return pl.CostEstimate(
            flops=2 * count * rows * features,
            bytes_accessed=2 * (rows + count) * features,
            transcendentals=0,
        )

    params = pltpu.CompilerParams(vmem_limit_bytes=24 * 2**20)
    normed, first_send = pl.pallas_call(
        functools.partial(first_kernel, capacity, chunks, groups),
        in_specs=[smem, vmem, vmem],
        out_specs=[vmem, vmem],
        out_shape=[shape(rows), shape(half[0])],
        compiler_params=params,
        cost_estimate=cost(half[0]),
        name="place_first",
    )(me, slots, embeddings)
    *keeps, next_send, rest_send = pl.pallas_call(
        functools.partial(rest_kernel, capacity, chunks, groups),
        in_specs=[smem, vmem, vmem],
        out_specs=[vmem] * (len(chunks) + 2),
        out_shape=[shape(count) for count in half + [half[1], sum(half[2:])]],
        compiler_params=params,
        cost_estimate=cost(2 * sum(half) - half[0]),
        name="place_rest",
    )(me, slots, normed)
    return keeps, first_send, next_send, rest_send


def lane_fold(values):
    best = values[:, :lanes]
    for start in range(lanes, values.shape[1], lanes):
        best = jnp.maximum(best, values[:, start : start + lanes])
    return best


def gram_body(own_refs, piece_ref, row_refs, col_ref, col_start, holds_own):
    step = len(own_refs) - 1
    tile = 256
    nt = (((1,), (1,)), ((), ()))
    if holds_own:
        row_refs[step][...] = jnp.full(row_refs[step].shape, sentinel, jnp.float32)
    for first in range(0, piece_ref.shape[0], tile):
        x = piece_ref[first : first + tile, :]
        marks = x[:, :lanes].astype(jnp.float32).T[0:1, :]
        col_bias = jnp.where(marks > 1.5, dead_bias, 0.0)
        col_best = jnp.full((1, tile), sentinel, jnp.float32)
        for j in range(step + 1):
            own = own_refs[j][...]
            scores = lax.dot_general(own, x, nt, preferred_element_type=jnp.float32)
            usable = scores + col_bias
            if j == step:
                if holds_own and first < own.shape[0]:
                    rows = lax.broadcasted_iota(jnp.int32, usable.shape, 0)
                    cols = lax.broadcasted_iota(jnp.int32, usable.shape, 1)
                    usable = jnp.where(rows - cols == first, dead_bias, usable)
            else:
                row_bias = jnp.where(own[:, 0:1].astype(jnp.float32) > 1.5, dead_bias, 0.0)
                col_best = jnp.maximum(
                    col_best, jnp.max(scores + row_bias, axis=0, keepdims=True)
                )
            row_refs[j][...] = jnp.maximum(row_refs[j][...], lane_fold(usable))
        col_ref[0:1, col_start + first : col_start + first + tile] = col_best


def gram_kernel(first, step, pieces, *refs):
    news = step + 1 - first
    owns, refs = refs[: step + 1], refs[step + 1 :]
    blocks, refs = refs[: pieces * news], refs[pieces * news :]
    states, refs = refs[:first], refs[first:]
    rows, cols = refs[: step + 1], refs[step + 1 :]
    for state, row in zip(states, rows):
        row[...] = state[...]
    for k in range(news):
        now = first + k + 1
        for p in range(pieces):
            block = blocks[pieces * k + p]
            start = p * block.shape[0]
            gram_body(owns[:now], block, rows[:now], cols[k], start, p == 0)


def gram_last_kernel(step, relatives, chunks, groups, me_ref, *refs):
    members = len(relatives)
    owns, block, refs = refs[: step + 1], refs[step + 1], refs[step + 2 :]
    states, refs = refs[: step + 1], refs[step + 1 :]
    cols, refs = refs[: step + 1], refs[step + 1 :]
    out_ref, col, table = refs[:3]
    rows = refs[3:]
    for state, row in zip(states, rows):
        row[...] = state[...]
    gram_body(owns, block, rows, col, 0, False)
    first = 0
    for k, size in enumerate(chunks):
        row_k = jnp.max(rows[k][...].T, axis=0, keepdims=True)
        count = groups * size
        for p, relative in enumerate(relatives):
            source, shift = (col, 2 * count) if k == step and p >= 2 else (cols[k], 0)
            for r in range(groups):
                start = p * count + r * size - shift
                best = source[0:1, start : start + size]
                if p == 0:
                    best = jnp.maximum(best, row_k[:, r * size : (r + 1) * size])
                row = r * members + p
                table[row : row + 1, first : first + size] = best
        first += size
    for r in range(groups):
        for p, relative in enumerate(relatives):
            row = r * members + p
            target = (me_ref[0] ^ r) * members + (me_ref[1] ^ relative)
            out_ref[target] = table[row : row + 1, :]


def gram_params(owns, blocks):
    features = owns[0].shape[1]
    mine, others = sum(own.shape[0] for own in owns), sum(block.shape[0] for block in blocks)
    return dict(
        compiler_params=pltpu.CompilerParams(vmem_limit_bytes=24 * 2**20),
        cost_estimate=pl.CostEstimate(
            flops=2 * mine * others * features,
            bytes_accessed=2 * features * (mine + others),
            transcendentals=0,
        ),
    )


def gram_step(first, owns, blocks, states, pieces):
    step = len(owns) - 1
    row_shapes = [(own.shape[0], lanes) for own in owns]
    col_shapes = [(1, pieces * 2 * own.shape[0]) for own in owns[first:]]
    results = pl.pallas_call(
        functools.partial(gram_kernel, first, step, pieces),
        in_specs=[vmem] * (step + 1 + len(blocks) + first),
        out_specs=[vmem] * len(row_shapes + col_shapes),
        out_shape=[jax.ShapeDtypeStruct(s, jnp.float32) for s in row_shapes + col_shapes],
        name="gram_step",
        **gram_params(owns, blocks),
    )(*owns, *blocks, *states)
    return list(results[: step + 1]), list(results[step + 1 :])


def gram_last(me, owns, block, states, cols, relatives, chunks, groups):
    step = len(owns) - 1
    members = len(relatives)
    shape = (groups * members, 1, sum(chunks))
    return pl.pallas_call(
        functools.partial(gram_last_kernel, step, relatives, chunks, groups),
        in_specs=[smem] + [vmem] * (3 * step + 4),
        out_specs=vmem,
        out_shape=jax.ShapeDtypeStruct(shape, jnp.float32),
        scratch_shapes=[pltpu.VMEM((1, block.shape[0]), jnp.float32), pltpu.VMEM(shape[::2], jnp.float32)]
        + [pltpu.VMEM((own.shape[0], lanes), jnp.float32) for own in owns],
        name="gram_last",
        **gram_params(owns, [block]),
    )(me, *owns, block, *states, *cols)


def tail_kernel(capacity, members, slot_ref, part_ref, out_ref, table):
    groups = part_ref.shape[0] // members
    width = table.shape[1]
    table[...] = jnp.full(table.shape, sentinel, jnp.float32)
    for g in range(groups):
        table[g : g + 1, :capacity] = jnp.max(
            part_ref[g * members : (g + 1) * members], axis=0
        )
    lane = lax.broadcasted_iota(jnp.int32, (lanes, lanes), 1)
    for q in range(out_ref.shape[0]):
        slot = jnp.broadcast_to(slot_ref[q : q + 1, :], (lanes, lanes)).T
        best = jnp.full((lanes, lanes), sentinel, jnp.float32)
        for g in range(groups):
            for c in range(0, width, lanes):
                entry = table[g : g + 1, c : c + lanes]
                best = jnp.maximum(
                    best, jnp.where(slot - (g * capacity + c) == lane, entry, sentinel)
                )
        out_ref[q : q + 1, :] = jnp.max(best.T, axis=0, keepdims=True)


def tail(partials, slots, capacity, members):
    groups = partials.shape[0] // members
    width = -(-capacity // lanes) * lanes
    return pl.pallas_call(
        functools.partial(tail_kernel, capacity, members),
        in_specs=[vmem, vmem],
        out_specs=vmem,
        out_shape=jax.ShapeDtypeStruct(slots.shape, jnp.float32),
        scratch_shapes=[pltpu.VMEM((groups, width), jnp.float32)],
        name="pick_rows",
    )(slots, partials)


def on_device(embeddings, send_slot):
    row_count, features = embeddings.shape
    groups = lax.axis_size("grp")
    members = lax.axis_size("blk")
    slot_count = 2 * row_count
    capacity = slot_count // groups
    chunks = chunk_sizes(capacity)
    me = jnp.stack([lax.axis_index("grp"), lax.axis_index("blk")]).astype(jnp.int32)
    slots = send_slot.reshape(row_count // lanes, lanes)
    keeps, first_send, next_send, rest_send = head(me, embeddings, slots, capacity, chunks, groups)
    count, high = len(chunks), groups // 2
    last = count - 1

    sent, owns, done, pairs = {}, {}, {}, {}

    def rows(value, index, size):
        return value[index * size : (index + 1) * size]

    def block(step, z):
        size = chunks[step]
        near = sent["y", min(step, 2) + 1] if step else sent["y", int(z < high // 2)]
        skip = sum(chunks[2:step]) * high if step else 0
        index = z if step else z % (high // 2)
        return jnp.concatenate(
            [rows(keeps[step], z, size), rows(near[skip:], index, size)], axis=0
        )

    def send(key, value, axis, size, bit, *earlier):
        held = [done[name] if name in done else sent[name] for name in earlier]
        sent[key] = swap(after(value, *held) if held else value, axis, size, bit)

    def send_z(step, z):
        early = [("z", step - 1, z)] if step >= 1 else []
        if step >= 2 and z == far[-1]:
            early += [("x", step - 2, 0)]
        if step == last and step >= 3:
            early += [("c", step - 2 if z == far[-1] else step - 3)]
        send(("z", step, z), block(step, z), "grp", groups, 2 * z, *early)

    def send_near_z():
        blocks = jnp.concatenate([block(step, 1) for step in range(2, count)], axis=0)
        send(("n",), blocks, "grp", groups, 2, ("z", 1, 1))

    def collect(step):
        parts = [block(step, 0)]
        for z in range(1, high):
            if z == 1 and step >= 2:
                start = 2 * sum(chunks[2:step])
                parts.append(sent["n",][start : start + 2 * chunks[step]])
            else:
                parts.append(sent["z", step, z])
        owns[step] = jnp.concatenate(parts, axis=0)

    def send_x(step, cuts, between):
        total = owns[step].shape[0]
        cuts = [0] + [total * cut // 384 // 16 * 16 for cut in cuts] + [total]
        parts = [name for name in sent if name[:2] == ("x", step - 1)]
        for part in range(len(cuts) - 1):
            value = owns[step][cuts[part] : cuts[part + 1]]
            early = parts if part == 0 else between[part - 1]
            send(("x", step, part), value, "blk", members, 2, *early)

    def send_c(step, *early):
        across = [sent[name] for name in list(sent) if name[:2] == ("x", step)]
        pairs[step] = jnp.concatenate([owns[step]] + across, axis=0)
        send(("c", step), pairs[step], "blk", members, 1, *early)

    far = [high // 2] + [z for z in range(1, high) if z != high // 2]
    cut = first_send.shape[0] // 2
    done["rest"] = rest_send
    send(("y", 0), first_send[:cut], "grp", groups, 1)
    send(("y", 1), first_send[cut:], "grp", groups, 1, "rest")
    send(("y", 2), next_send, "grp", groups, 1, ("y", 0))
    send(("y", 3), rest_send, "grp", groups, 1, ("y", 0))
    for z in far:
        send_z(0, z)
    for step in range(1, count):
        collect(step - 1)
        for z in far:
            send_z(step, z)
        if step == 1:
            far.remove(1)
            send_near_z()
        send_x(step - 1, [], [])
        send_c(step - 1, *[("z", step, z) for z in far])
    collect(last)
    mine = [owns[k] for k in range(count)]
    blocks = [block for k in range(last) for block in (pairs[k], sent["c", k])]
    states, cols = gram_step(0, mine[:last], blocks, [], 2)
    done["gram"] = cols[-1]
    send_x(last, [304], [["gram"]])
    send_c(last)
    states, half = gram_step(last, mine, [pairs[last]], states, 1)
    result = gram_last(
        me, mine, sent["c", last], states, cols + half, (0, 2, 1, 3), chunks, groups
    )
    homeward = lax.all_to_all(result, ("grp", "blk"), 0, 0, tiled=True)
    return tail(homeward, slots, capacity, members).reshape(row_count)


def solution(mesh):
    in_specs = (P(("grp", "blk"), None), P(("grp", "blk")))
    out_specs = P(("grp", "blk"))
    return jax.shard_map(
        on_device, mesh=mesh, in_specs=in_specs, out_specs=out_specs, check_vma=False
    )
```

```python
import functools

import jax
import jax.numpy as jnp
from jax import lax
from jax.experimental import pallas as pl
from jax.experimental.pallas import tpu as pltpu
from jax.sharding import PartitionSpec as P

sentinel = -3.0
epsilon = 1e-06
dead_mark = 2.0
dead_bias = -8.0
lanes = 128
smem = pl.BlockSpec(memory_space=pltpu.SMEM)
vmem = pl.BlockSpec(memory_space=pltpu.VMEM)


def chunk_sizes(capacity):
    count = 4 if capacity % 64 == 0 else 3
    return (capacity // count,) * count


def after(value, *earlier):
    return lax.optimization_barrier((value,) + earlier)[0]


def swap(value, axis, size, bit):
    return lax.ppermute(value, axis, [(i, i ^ bit) for i in range(size)])


def place(me, slots, normed, capacity, first, size, groups, low, turn=0):
    high = groups // 2
    shape = (high, size, 1)
    spot = lax.broadcasted_iota(jnp.int32, shape, 1) + first
    group = ((lax.broadcasted_iota(jnp.int32, shape, 0) + turn) % high * 2 + low) ^ me
    wanted = (group * capacity + spot).reshape(groups // 2 * size, 1)
    pick = jnp.where(wanted == slots, 1.0, 0.0)
    live = jnp.max(pick, axis=1, keepdims=True)
    placed = jnp.dot(pick.astype(jnp.bfloat16), normed, preferred_element_type=jnp.float32)
    lane = lax.broadcasted_iota(jnp.int32, (1, placed.shape[1]), 1)
    mark = jnp.where(lane == 0, dead_mark, 0.0)
    return (placed + (1.0 - live) * mark).astype(jnp.bfloat16)


def flat(slot_ref):
    return jnp.concatenate([slot_ref[q : q + 1, :] for q in range(slot_ref.shape[0])], axis=1)


def first_kernel(capacity, chunks, groups, me_ref, slot_ref, x_ref, normed_ref, send_ref):
    wide = x_ref[...].astype(jnp.float32)
    normed_ref[...] = (
        wide * lax.rsqrt(jnp.sum(wide * wide, axis=-1, keepdims=True) + epsilon)
    ).astype(jnp.bfloat16)
    send_ref[...] = place(
        me_ref[0], flat(slot_ref), normed_ref[...], capacity, 0, chunks[0], groups, 1, groups // 4
    )


def rest_kernel(capacity, chunks, groups, me_ref, slot_ref, normed_ref, *out_refs):
    keeps, send_refs = out_refs[:-2], out_refs[-2:]
    slots, normed = flat(slot_ref), normed_ref[...]
    first, row = 0, 0
    for step, size in enumerate(chunks):
        placed = place(me_ref[0], slots, normed, capacity, first, size, groups, 1) if step else None
        if step == 1:
            send_refs[0][...] = placed
        elif step > 1:
            send_refs[1][row : row + placed.shape[0], :] = placed
            row += placed.shape[0]
        first += size
    first = 0
    for step, size in enumerate(chunks):
        keeps[step][...] = place(me_ref[0], slots, normed, capacity, first, size, groups, 0)
        first += size


def head(me, embeddings, slots, capacity, chunks, groups):
    rows, features = embeddings.shape
    half = [groups // 2 * size for size in chunks]

    def shape(count):
        return jax.ShapeDtypeStruct((count, features), jnp.bfloat16)

    def cost(count):
        return pl.CostEstimate(
            flops=2 * count * rows * features,
            bytes_accessed=2 * (rows + count) * features,
            transcendentals=0,
        )

    params = pltpu.CompilerParams(vmem_limit_bytes=24 * 2**20)
    normed, first_send = pl.pallas_call(
        functools.partial(first_kernel, capacity, chunks, groups),
        in_specs=[smem, vmem, vmem],
        out_specs=[vmem, vmem],
        out_shape=[shape(rows), shape(half[0])],
        compiler_params=params,
        cost_estimate=cost(half[0]),
        name="place_first",
    )(me, slots, embeddings)
    *keeps, next_send, rest_send = pl.pallas_call(
        functools.partial(rest_kernel, capacity, chunks, groups),
        in_specs=[smem, vmem, vmem],
        out_specs=[vmem] * (len(chunks) + 2),
        out_shape=[shape(count) for count in half + [half[1], sum(half[2:])]],
        compiler_params=params,
        cost_estimate=cost(2 * sum(half) - half[0]),
        name="place_rest",
    )(me, slots, normed)
    return keeps, first_send, next_send, rest_send


def lane_fold(values):
    best = values[:, :lanes]
    for start in range(lanes, values.shape[1], lanes):
        best = jnp.maximum(best, values[:, start : start + lanes])
    return best


def gram_body(own_refs, piece_ref, row_refs, col_ref, col_start, holds_own):
    step = len(own_refs) - 1
    tile = 256
    nt = (((1,), (1,)), ((), ()))
    if holds_own:
        row_refs[step][...] = jnp.full(row_refs[step].shape, sentinel, jnp.float32)
    for first in range(0, piece_ref.shape[0], tile):
        x = piece_ref[first : first + tile, :]
        marks = x[:, :lanes].astype(jnp.float32).T[0:1, :]
        col_bias = jnp.where(marks > 1.5, dead_bias, 0.0)
        col_best = jnp.full((1, tile), sentinel, jnp.float32)
        for j in range(step + 1):
            own = own_refs[j][...]
            scores = lax.dot_general(own, x, nt, preferred_element_type=jnp.float32)
            usable = scores + col_bias
            if j == step:
                if holds_own and first < own.shape[0]:
                    rows = lax.broadcasted_iota(jnp.int32, usable.shape, 0)
                    cols = lax.broadcasted_iota(jnp.int32, usable.shape, 1)
                    usable = jnp.where(rows - cols == first, dead_bias, usable)
            else:
                row_bias = jnp.where(own[:, 0:1].astype(jnp.float32) > 1.5, dead_bias, 0.0)
                col_best = jnp.maximum(
                    col_best, jnp.max(scores + row_bias, axis=0, keepdims=True)
                )
            row_refs[j][...] = jnp.maximum(row_refs[j][...], lane_fold(usable))
        col_ref[0:1, col_start + first : col_start + first + tile] = col_best


def gram_kernel(first, step, pieces, *refs):
    news = step + 1 - first
    owns, refs = refs[: step + 1], refs[step + 1 :]
    blocks, refs = refs[: pieces * news], refs[pieces * news :]
    states, refs = refs[:first], refs[first:]
    rows, cols = refs[: step + 1], refs[step + 1 :]
    for state, row in zip(states, rows):
        row[...] = state[...]
    for k in range(news):
        now = first + k + 1
        for p in range(pieces):
            block = blocks[pieces * k + p]
            start = p * block.shape[0]
            gram_body(owns[:now], block, rows[:now], cols[k], start, p == 0)


def gram_last_kernel(step, relatives, chunks, groups, me_ref, *refs):
    members = len(relatives)
    owns, block, refs = refs[: step + 1], refs[step + 1], refs[step + 2 :]
    states, refs = refs[: step + 1], refs[step + 1 :]
    cols, refs = refs[: step + 1], refs[step + 1 :]
    out_ref, col, table = refs[:3]
    rows = refs[3:]
    for state, row in zip(states, rows):
        row[...] = state[...]
    gram_body(owns, block, rows, col, 0, False)
    first = 0
    for k, size in enumerate(chunks):
        row_k = jnp.max(rows[k][...].T, axis=0, keepdims=True)
        count = groups * size
        for p, relative in enumerate(relatives):
            source, shift = (col, 2 * count) if k == step and p >= 2 else (cols[k], 0)
            for r in range(groups):
                start = p * count + r * size - shift
                best = source[0:1, start : start + size]
                if p == 0:
                    best = jnp.maximum(best, row_k[:, r * size : (r + 1) * size])
                row = r * members + p
                table[row : row + 1, first : first + size] = best
        first += size
    for r in range(groups):
        for p, relative in enumerate(relatives):
            row = r * members + p
            target = (me_ref[0] ^ r) * members + (me_ref[1] ^ relative)
            out_ref[target] = table[row : row + 1, :]


def gram_params(owns, blocks):
    features = owns[0].shape[1]
    mine, others = sum(own.shape[0] for own in owns), sum(block.shape[0] for block in blocks)
    return dict(
        compiler_params=pltpu.CompilerParams(vmem_limit_bytes=24 * 2**20),
        cost_estimate=pl.CostEstimate(
            flops=2 * mine * others * features,
            bytes_accessed=2 * features * (mine + others),
            transcendentals=0,
        ),
    )


def gram_step(first, owns, blocks, states, pieces):
    step = len(owns) - 1
    row_shapes = [(own.shape[0], lanes) for own in owns]
    col_shapes = [(1, pieces * 2 * own.shape[0]) for own in owns[first:]]
    results = pl.pallas_call(
        functools.partial(gram_kernel, first, step, pieces),
        in_specs=[vmem] * (step + 1 + len(blocks) + first),
        out_specs=[vmem] * len(row_shapes + col_shapes),
        out_shape=[jax.ShapeDtypeStruct(s, jnp.float32) for s in row_shapes + col_shapes],
        name="gram_step",
        **gram_params(owns, blocks),
    )(*owns, *blocks, *states)
    return list(results[: step + 1]), list(results[step + 1 :])


def gram_last(me, owns, block, states, cols, relatives, chunks, groups):
    step = len(owns) - 1
    members = len(relatives)
    shape = (groups * members, 1, sum(chunks))
    return pl.pallas_call(
        functools.partial(gram_last_kernel, step, relatives, chunks, groups),
        in_specs=[smem] + [vmem] * (3 * step + 4),
        out_specs=vmem,
        out_shape=jax.ShapeDtypeStruct(shape, jnp.float32),
        scratch_shapes=[pltpu.VMEM((1, block.shape[0]), jnp.float32), pltpu.VMEM(shape[::2], jnp.float32)]
        + [pltpu.VMEM((own.shape[0], lanes), jnp.float32) for own in owns],
        name="gram_last",
        **gram_params(owns, [block]),
    )(me, *owns, block, *states, *cols)


def tail_kernel(capacity, members, slot_ref, part_ref, out_ref, table):
    groups = part_ref.shape[0] // members
    width = table.shape[1]
    table[...] = jnp.full(table.shape, sentinel, jnp.float32)
    for g in range(groups):
        table[g : g + 1, :capacity] = jnp.max(
            part_ref[g * members : (g + 1) * members], axis=0
        )
    lane = lax.broadcasted_iota(jnp.int32, (lanes, lanes), 1)
    for q in range(out_ref.shape[0]):
        slot = jnp.broadcast_to(slot_ref[q : q + 1, :], (lanes, lanes)).T
        best = jnp.full((lanes, lanes), sentinel, jnp.float32)
        for g in range(groups):
            for c in range(0, width, lanes):
                entry = table[g : g + 1, c : c + lanes]
                best = jnp.maximum(
                    best, jnp.where(slot - (g * capacity + c) == lane, entry, sentinel)
                )
        out_ref[q : q + 1, :] = jnp.max(best.T, axis=0, keepdims=True)


def tail(partials, slots, capacity, members):
    groups = partials.shape[0] // members
    width = -(-capacity // lanes) * lanes
    return pl.pallas_call(
        functools.partial(tail_kernel, capacity, members),
        in_specs=[vmem, vmem],
        out_specs=vmem,
        out_shape=jax.ShapeDtypeStruct(slots.shape, jnp.float32),
        scratch_shapes=[pltpu.VMEM((groups, width), jnp.float32)],
        name="pick_rows",
    )(slots, partials)


def on_device(embeddings, send_slot):
    row_count, features = embeddings.shape
    groups = lax.axis_size("grp")
    members = lax.axis_size("blk")
    slot_count = 2 * row_count
    capacity = slot_count // groups
    chunks = chunk_sizes(capacity)
    me = jnp.stack([lax.axis_index("grp"), lax.axis_index("blk")]).astype(jnp.int32)
    slots = send_slot.reshape(row_count // lanes, lanes)
    keeps, first_send, next_send, rest_send = head(me, embeddings, slots, capacity, chunks, groups)
    count, high = len(chunks), groups // 2
    last = count - 1

    sent, owns, done, pairs = {}, {}, {}, {}

    def rows(value, index, size):
        return value[index * size : (index + 1) * size]

    def block(step, z):
        size = chunks[step]
        near = sent["y", min(step, 2) + 1] if step else sent["y", int(z < high // 2)]
        skip = sum(chunks[2:step]) * high if step else 0
        index = z if step else z % (high // 2)
        return jnp.concatenate(
            [rows(keeps[step], z, size), rows(near[skip:], index, size)], axis=0
        )

    def send(key, value, axis, size, bit, *earlier):
        held = [done[name] if name in done else sent[name] for name in earlier]
        sent[key] = swap(after(value, *held) if held else value, axis, size, bit)

    def send_z(step, z):
        early = [("z", step - 1, z)] if step >= 1 else []
        if step >= 2 and z == high - 1:
            early += [("x", step - 2, 0)]
        if z == 1:
            early += [("c", step - 2)] if step >= 2 else [("y", step + 2)]
        send(("z", step, z), block(step, z), "grp", groups, 2 * z, *early)

    def collect(step):
        parts = [block(step, 0)]
        for z in range(1, high):
            parts.append(sent["z", step, z])
        owns[step] = jnp.concatenate(parts, axis=0)

    def send_x(step, cuts, between):
        total = owns[step].shape[0]
        cuts = [0] + [total * cut // 384 // 16 * 16 for cut in cuts] + [total]
        parts = [name for name in sent if name[:2] == ("x", step - 1)]
        for part in range(len(cuts) - 1):
            value = owns[step][cuts[part] : cuts[part + 1]]
            early = parts if part == 0 else between[part - 1]
            send(("x", step, part), value, "blk", members, 2, *early)

    def send_c(step, *early):
        across = [sent[name] for name in list(sent) if name[:2] == ("x", step)]
        pairs[step] = jnp.concatenate([owns[step]] + across, axis=0)
        send(("c", step), pairs[step], "blk", members, 1, *early)

    far = [high // 2] + [z for z in reversed(range(1, high)) if z != high // 2]
    cut = first_send.shape[0] // 2
    done["rest"] = rest_send
    send(("y", 0), first_send[:cut], "grp", groups, 1)
    send(("y", 1), first_send[cut:], "grp", groups, 1, "rest")
    send(("y", 2), next_send, "grp", groups, 1, ("y", 0))
    send(("y", 3), rest_send, "grp", groups, 1, ("y", 0))
    for z in far:
        send_z(0, z)
    for step in range(1, count):
        collect(step - 1)
        for z in far:
            send_z(step, z)
        send_x(step - 1, [], [])
        send_c(step - 1, *[("z", step, z) for z in far])
    collect(last)
    mine = [owns[k] for k in range(count)]
    blocks = [block for k in range(last) for block in (pairs[k], sent["c", k])]
    states, cols = gram_step(0, mine[:last], blocks, [], 2)
    done["gram"] = cols[-1]
    send_x(last, [304], [["gram"]])
    send_c(last)
    states, half = gram_step(last, mine, [pairs[last]], states, 1)
    result = gram_last(
        me, mine, sent["c", last], states, cols + half, (0, 2, 1, 3), chunks, groups
    )
    homeward = lax.all_to_all(result, ("grp", "blk"), 0, 0, tiled=True)
    return tail(homeward, slots, capacity, members).reshape(row_count)


def solution(mesh):
    in_specs = (P(("grp", "blk"), None), P(("grp", "blk")))
    out_specs = P(("grp", "blk"))
    return jax.shard_map(
        on_device, mesh=mesh, in_specs=in_specs, out_specs=out_specs, check_vma=False
    )
```

```python
import functools

import jax
import jax.numpy as jnp
from jax import lax
from jax.experimental import pallas as pl
from jax.experimental.pallas import tpu as pltpu
from jax.sharding import PartitionSpec as P

sentinel = -3.0
epsilon = 1e-06
dead_mark = 2.0
dead_bias = -8.0
lanes = 128
smem = pl.BlockSpec(memory_space=pltpu.SMEM)
vmem = pl.BlockSpec(memory_space=pltpu.VMEM)


def chunk_sizes(capacity):
    count = 4 if capacity % 64 == 0 else 3
    return (capacity // count,) * count


def after(value, *earlier):
    return lax.optimization_barrier((value,) + earlier)[0]


def swap(value, axis, size, bit):
    return lax.ppermute(value, axis, [(i, i ^ bit) for i in range(size)])


def place(me, slots, normed, capacity, first, size, groups, low):
    high = groups // 2
    shape = (high, size, 1)
    spot = lax.broadcasted_iota(jnp.int32, shape, 1) + first
    group = (lax.broadcasted_iota(jnp.int32, shape, 0) * 2 + low) ^ me
    wanted = (group * capacity + spot).reshape(groups // 2 * size, 1)
    pick = jnp.where(wanted == slots, 1.0, 0.0)
    live = jnp.max(pick, axis=1, keepdims=True)
    placed = jnp.dot(pick.astype(jnp.bfloat16), normed, preferred_element_type=jnp.float32)
    lane = lax.broadcasted_iota(jnp.int32, (1, placed.shape[1]), 1)
    mark = jnp.where(lane == 0, dead_mark, 0.0)
    return (placed + (1.0 - live) * mark).astype(jnp.bfloat16)


def flat(slot_ref):
    return jnp.concatenate([slot_ref[q : q + 1, :] for q in range(slot_ref.shape[0])], axis=1)


def first_kernel(capacity, chunks, groups, me_ref, slot_ref, x_ref, normed_ref, send_ref):
    wide = x_ref[...].astype(jnp.float32)
    normed_ref[...] = (
        wide * lax.rsqrt(jnp.sum(wide * wide, axis=-1, keepdims=True) + epsilon)
    ).astype(jnp.bfloat16)
    send_ref[...] = place(
        me_ref[0], flat(slot_ref), normed_ref[...], capacity, 0, chunks[0], groups, 1
    )


def rest_kernel(capacity, chunks, groups, me_ref, slot_ref, normed_ref, *out_refs):
    keeps, send_refs = out_refs[:-2], out_refs[-2:]
    slots, normed = flat(slot_ref), normed_ref[...]
    first, row = 0, 0
    for step, size in enumerate(chunks):
        placed = place(me_ref[0], slots, normed, capacity, first, size, groups, 1) if step else None
        if step == 1:
            send_refs[0][...] = placed
        elif step > 1:
            send_refs[1][row : row + placed.shape[0], :] = placed
            row += placed.shape[0]
        first += size
    first = 0
    for step, size in enumerate(chunks):
        keeps[step][...] = place(me_ref[0], slots, normed, capacity, first, size, groups, 0)
        first += size


def head(me, embeddings, slots, capacity, chunks, groups):
    rows, features = embeddings.shape
    half = [groups // 2 * size for size in chunks]

    def shape(count):
        return jax.ShapeDtypeStruct((count, features), jnp.bfloat16)

    def cost(count):
        return pl.CostEstimate(
            flops=2 * count * rows * features,
            bytes_accessed=2 * (rows + count) * features,
            transcendentals=0,
        )

    params = pltpu.CompilerParams(vmem_limit_bytes=24 * 2**20)
    normed, first_send = pl.pallas_call(
        functools.partial(first_kernel, capacity, chunks, groups),
        in_specs=[smem, vmem, vmem],
        out_specs=[vmem, vmem],
        out_shape=[shape(rows), shape(half[0])],
        compiler_params=params,
        cost_estimate=cost(half[0]),
        name="place_first",
    )(me, slots, embeddings)
    *keeps, next_send, rest_send = pl.pallas_call(
        functools.partial(rest_kernel, capacity, chunks, groups),
        in_specs=[smem, vmem, vmem],
        out_specs=[vmem] * (len(chunks) + 2),
        out_shape=[shape(count) for count in half + [half[1], sum(half[2:])]],
        compiler_params=params,
        cost_estimate=cost(2 * sum(half) - half[0]),
        name="place_rest",
    )(me, slots, normed)
    return keeps, first_send, next_send, rest_send


def lane_fold(values):
    best = values[:, :lanes]
    for start in range(lanes, values.shape[1], lanes):
        best = jnp.maximum(best, values[:, start : start + lanes])
    return best


def gram_body(own_refs, piece_ref, row_refs, col_ref, col_start, holds_own):
    step = len(own_refs) - 1
    tile = 256
    nt = (((1,), (1,)), ((), ()))
    if holds_own:
        row_refs[step][...] = jnp.full(row_refs[step].shape, sentinel, jnp.float32)
    for first in range(0, piece_ref.shape[0], tile):
        x = piece_ref[first : first + tile, :]
        marks = x[:, :lanes].astype(jnp.float32).T[0:1, :]
        col_bias = jnp.where(marks > 1.5, dead_bias, 0.0)
        col_best = jnp.full((1, tile), sentinel, jnp.float32)
        for j in range(step + 1):
            own = own_refs[j][...]
            scores = lax.dot_general(own, x, nt, preferred_element_type=jnp.float32)
            usable = scores + col_bias
            if j == step:
                if holds_own and first < own.shape[0]:
                    rows = lax.broadcasted_iota(jnp.int32, usable.shape, 0)
                    cols = lax.broadcasted_iota(jnp.int32, usable.shape, 1)
                    usable = jnp.where(rows - cols == first, dead_bias, usable)
            else:
                row_bias = jnp.where(own[:, 0:1].astype(jnp.float32) > 1.5, dead_bias, 0.0)
                col_best = jnp.maximum(
                    col_best, jnp.max(scores + row_bias, axis=0, keepdims=True)
                )
            row_refs[j][...] = jnp.maximum(row_refs[j][...], lane_fold(usable))
        col_ref[0:1, col_start + first : col_start + first + tile] = col_best


def gram_kernel(first, step, pieces, *refs):
    news = step + 1 - first
    owns, refs = refs[: step + 1], refs[step + 1 :]
    blocks, refs = refs[: pieces * news], refs[pieces * news :]
    states, refs = refs[:first], refs[first:]
    rows, cols = refs[: step + 1], refs[step + 1 :]
    for state, row in zip(states, rows):
        row[...] = state[...]
    for k in range(news):
        now = first + k + 1
        for p in range(pieces):
            block = blocks[pieces * k + p]
            start = p * block.shape[0]
            gram_body(owns[:now], block, rows[:now], cols[k], start, p == 0)


def gram_last_kernel(step, relatives, chunks, groups, me_ref, *refs):
    members = len(relatives)
    owns, block, refs = refs[: step + 1], refs[step + 1], refs[step + 2 :]
    states, refs = refs[: step + 1], refs[step + 1 :]
    cols, refs = refs[: step + 1], refs[step + 1 :]
    out_ref, col, table = refs[:3]
    rows = refs[3:]
    for state, row in zip(states, rows):
        row[...] = state[...]
    gram_body(owns, block, rows, col, 0, False)
    first = 0
    for k, size in enumerate(chunks):
        row_k = jnp.max(rows[k][...].T, axis=0, keepdims=True)
        count = groups * size
        for p, relative in enumerate(relatives):
            source, shift = (col, 2 * count) if k == step and p >= 2 else (cols[k], 0)
            for r in range(groups):
                start = p * count + r * size - shift
                best = source[0:1, start : start + size]
                if p == 0:
                    best = jnp.maximum(best, row_k[:, r * size : (r + 1) * size])
                row = r * members + p
                table[row : row + 1, first : first + size] = best
        first += size
    for r in range(groups):
        for p, relative in enumerate(relatives):
            row = r * members + p
            target = (me_ref[0] ^ r) * members + (me_ref[1] ^ relative)
            out_ref[target] = table[row : row + 1, :]


def gram_params(owns, blocks):
    features = owns[0].shape[1]
    mine, others = sum(own.shape[0] for own in owns), sum(block.shape[0] for block in blocks)
    return dict(
        compiler_params=pltpu.CompilerParams(vmem_limit_bytes=24 * 2**20),
        cost_estimate=pl.CostEstimate(
            flops=2 * mine * others * features,
            bytes_accessed=2 * features * (mine + others),
            transcendentals=0,
        ),
    )


def gram_step(first, owns, blocks, states, pieces):
    step = len(owns) - 1
    row_shapes = [(own.shape[0], lanes) for own in owns]
    col_shapes = [(1, pieces * 2 * own.shape[0]) for own in owns[first:]]
    results = pl.pallas_call(
        functools.partial(gram_kernel, first, step, pieces),
        in_specs=[vmem] * (step + 1 + len(blocks) + first),
        out_specs=[vmem] * len(row_shapes + col_shapes),
        out_shape=[jax.ShapeDtypeStruct(s, jnp.float32) for s in row_shapes + col_shapes],
        name="gram_step",
        **gram_params(owns, blocks),
    )(*owns, *blocks, *states)
    return list(results[: step + 1]), list(results[step + 1 :])


def gram_last(me, owns, block, states, cols, relatives, chunks, groups):
    step = len(owns) - 1
    members = len(relatives)
    shape = (groups * members, 1, sum(chunks))
    return pl.pallas_call(
        functools.partial(gram_last_kernel, step, relatives, chunks, groups),
        in_specs=[smem] + [vmem] * (3 * step + 4),
        out_specs=vmem,
        out_shape=jax.ShapeDtypeStruct(shape, jnp.float32),
        scratch_shapes=[pltpu.VMEM((1, block.shape[0]), jnp.float32), pltpu.VMEM(shape[::2], jnp.float32)]
        + [pltpu.VMEM((own.shape[0], lanes), jnp.float32) for own in owns],
        name="gram_last",
        **gram_params(owns, [block]),
    )(me, *owns, block, *states, *cols)


def tail_kernel(capacity, members, slot_ref, part_ref, out_ref, table):
    groups = part_ref.shape[0] // members
    width = table.shape[1]
    table[...] = jnp.full(table.shape, sentinel, jnp.float32)
    for g in range(groups):
        table[g : g + 1, :capacity] = jnp.max(
            part_ref[g * members : (g + 1) * members], axis=0
        )
    lane = lax.broadcasted_iota(jnp.int32, (lanes, lanes), 1)
    for q in range(out_ref.shape[0]):
        slot = jnp.broadcast_to(slot_ref[q : q + 1, :], (lanes, lanes)).T
        best = jnp.full((lanes, lanes), sentinel, jnp.float32)
        for g in range(groups):
            for c in range(0, width, lanes):
                entry = table[g : g + 1, c : c + lanes]
                best = jnp.maximum(
                    best, jnp.where(slot - (g * capacity + c) == lane, entry, sentinel)
                )
        out_ref[q : q + 1, :] = jnp.max(best.T, axis=0, keepdims=True)


def tail(partials, slots, capacity, members):
    groups = partials.shape[0] // members
    width = -(-capacity // lanes) * lanes
    return pl.pallas_call(
        functools.partial(tail_kernel, capacity, members),
        in_specs=[vmem, vmem],
        out_specs=vmem,
        out_shape=jax.ShapeDtypeStruct(slots.shape, jnp.float32),
        scratch_shapes=[pltpu.VMEM((groups, width), jnp.float32)],
        name="pick_rows",
    )(slots, partials)


def on_device(embeddings, send_slot):
    row_count, features = embeddings.shape
    groups = lax.axis_size("grp")
    members = lax.axis_size("blk")
    slot_count = 2 * row_count
    capacity = slot_count // groups
    chunks = chunk_sizes(capacity)
    me = jnp.stack([lax.axis_index("grp"), lax.axis_index("blk")]).astype(jnp.int32)
    slots = send_slot.reshape(row_count // lanes, lanes)
    keeps, first_send, next_send, rest_send = head(me, embeddings, slots, capacity, chunks, groups)
    count, high = len(chunks), groups // 2
    last = count - 1

    sent, owns, done, pairs = {}, {}, {}, {}

    def rows(value, index, size):
        return value[index * size : (index + 1) * size]

    def block(step, z):
        size = chunks[step]
        near = sent["y", min(step, 2) + 1] if step else sent["y", int(z >= high // 2)]
        skip = sum(chunks[2:step]) * high if step else 0
        index = z if step else z % (high // 2)
        return jnp.concatenate(
            [rows(keeps[step], z, size), rows(near[skip:], index, size)], axis=0
        )

    def send(key, value, axis, size, bit, *earlier):
        held = [done[name] if name in done else sent[name] for name in earlier]
        sent[key] = swap(after(value, *held) if held else value, axis, size, bit)

    def send_z(step, z):
        early = [("z", step - 1, z)] if step >= 1 else []
        if step >= 2 and z == high - 1:
            early += [("x", step - 2, 0)]
        if z == 1:
            early += [("c", step - 2)] if step >= 2 else [("y", 3)] if step else []
        send(("z", step, z), block(step, z), "grp", groups, 2 * z, *early)

    def collect(step):
        parts = [block(step, 0)]
        for z in range(1, high):
            parts.append(sent["z", step, z])
        owns[step] = jnp.concatenate(parts, axis=0)

    def send_x(step, cuts, between):
        total = owns[step].shape[0]
        cuts = [0] + [total * cut // 384 // 16 * 16 for cut in cuts] + [total]
        parts = [name for name in sent if name[:2] == ("x", step - 1)]
        for part in range(len(cuts) - 1):
            value = owns[step][cuts[part] : cuts[part + 1]]
            early = parts if part == 0 else between[part - 1]
            send(("x", step, part), value, "blk", members, 2, *early)

    def send_c(step, *early):
        across = [sent[name] for name in list(sent) if name[:2] == ("x", step)]
        pairs[step] = jnp.concatenate([owns[step]] + across, axis=0)
        send(("c", step), pairs[step], "blk", members, 1, *early)

    far = [high // 2] + [z for z in reversed(range(1, high)) if z != high // 2]
    cut = first_send.shape[0] // 2
    done["rest"] = rest_send
    send(("y", 0), first_send[:cut], "grp", groups, 1)
    send(("y", 1), first_send[cut:], "grp", groups, 1, "rest")
    send(("y", 2), next_send, "grp", groups, 1, ("y", 0))
    send(("y", 3), rest_send, "grp", groups, 1, ("y", 1))
    for z in far:
        send_z(0, z)
    for step in range(1, count):
        collect(step - 1)
        for z in far:
            send_z(step, z)
        send_x(step - 1, [], [])
        send_c(step - 1, *[("z", step, z) for z in far])
    collect(last)
    mine = [owns[k] for k in range(count)]
    blocks = [block for k in range(last) for block in (pairs[k], sent["c", k])]
    states, cols = gram_step(0, mine[:last], blocks, [], 2)
    done["gram"] = cols[-1]
    send_x(last, [304], [["gram"]])
    send_c(last)
    states, half = gram_step(last, mine, [pairs[last]], states, 1)
    result = gram_last(
        me, mine, sent["c", last], states, cols + half, (0, 2, 1, 3), chunks, groups
    )
    homeward = lax.all_to_all(result, ("grp", "blk"), 0, 0, tiled=True)
    return tail(homeward, slots, capacity, members).reshape(row_count)


def solution(mesh):
    in_specs = (P(("grp", "blk"), None), P(("grp", "blk")))
    out_specs = P(("grp", "blk"))
    return jax.shard_map(
        on_device, mesh=mesh, in_specs=in_specs, out_specs=out_specs, check_vma=False
    )
```

```python
import functools

import jax
import jax.numpy as jnp
from jax import lax
from jax.experimental import pallas as pl
from jax.experimental.pallas import tpu as pltpu
from jax.sharding import PartitionSpec as P

sentinel = -3.0
epsilon = 1e-06
dead_mark = 2.0
dead_bias = -8.0
lanes = 128
smem = pl.BlockSpec(memory_space=pltpu.SMEM)
vmem = pl.BlockSpec(memory_space=pltpu.VMEM)


def chunk_sizes(capacity):
    count = 4 if capacity % 64 == 0 else 3
    return (capacity // count,) * count


def after(value, *earlier):
    return lax.optimization_barrier((value,) + earlier)[0]


def swap(value, axis, size, bit):
    return lax.ppermute(value, axis, [(i, i ^ bit) for i in range(size)])


def place(me, slots, normed, capacity, first, size, groups, low):
    shape = (groups // 2, size, 1)
    spot = lax.broadcasted_iota(jnp.int32, shape, 1) + first
    group = (lax.broadcasted_iota(jnp.int32, shape, 0) * 2 + low) ^ me
    wanted = (group * capacity + spot).reshape(groups // 2 * size, 1)
    pick = jnp.where(wanted == slots, 1.0, 0.0)
    live = jnp.max(pick, axis=1, keepdims=True)
    placed = jnp.dot(pick.astype(jnp.bfloat16), normed, preferred_element_type=jnp.float32)
    lane = lax.broadcasted_iota(jnp.int32, (1, placed.shape[1]), 1)
    mark = jnp.where(lane == 0, dead_mark, 0.0)
    return (placed + (1.0 - live) * mark).astype(jnp.bfloat16)


def flat(slot_ref):
    return jnp.concatenate([slot_ref[q : q + 1, :] for q in range(slot_ref.shape[0])], axis=1)


def first_kernel(capacity, chunks, groups, me_ref, slot_ref, x_ref, normed_ref, send_ref):
    wide = x_ref[...].astype(jnp.float32)
    normed_ref[...] = (
        wide * lax.rsqrt(jnp.sum(wide * wide, axis=-1, keepdims=True) + epsilon)
    ).astype(jnp.bfloat16)
    send_ref[...] = place(
        me_ref[0], flat(slot_ref), normed_ref[...], capacity, 0, chunks[0], groups, 1
    )


def rest_kernel(capacity, chunks, groups, me_ref, slot_ref, normed_ref, *out_refs):
    keeps, send_refs = out_refs[:-2], out_refs[-2:]
    slots, normed = flat(slot_ref), normed_ref[...]
    first, row = 0, 0
    for step, size in enumerate(chunks):
        placed = place(me_ref[0], slots, normed, capacity, first, size, groups, 1) if step else None
        if step == 1:
            send_refs[0][...] = placed
        elif step > 1:
            send_refs[1][row : row + placed.shape[0], :] = placed
            row += placed.shape[0]
        first += size
    first = 0
    for step, size in enumerate(chunks):
        keeps[step][...] = place(me_ref[0], slots, normed, capacity, first, size, groups, 0)
        first += size


def head(me, embeddings, slots, capacity, chunks, groups):
    rows, features = embeddings.shape
    half = [groups // 2 * size for size in chunks]

    def shape(count):
        return jax.ShapeDtypeStruct((count, features), jnp.bfloat16)

    def cost(count):
        return pl.CostEstimate(
            flops=2 * count * rows * features,
            bytes_accessed=2 * (rows + count) * features,
            transcendentals=0,
        )

    params = pltpu.CompilerParams(vmem_limit_bytes=24 * 2**20)
    normed, first_send = pl.pallas_call(
        functools.partial(first_kernel, capacity, chunks, groups),
        in_specs=[smem, vmem, vmem],
        out_specs=[vmem, vmem],
        out_shape=[shape(rows), shape(half[0])],
        compiler_params=params,
        cost_estimate=cost(half[0]),
        name="place_first",
    )(me, slots, embeddings)
    *keeps, next_send, rest_send = pl.pallas_call(
        functools.partial(rest_kernel, capacity, chunks, groups),
        in_specs=[smem, vmem, vmem],
        out_specs=[vmem] * (len(chunks) + 2),
        out_shape=[shape(count) for count in half + [half[1], sum(half[2:])]],
        compiler_params=params,
        cost_estimate=cost(2 * sum(half) - half[0]),
        name="place_rest",
    )(me, slots, normed)
    return keeps, first_send, next_send, rest_send


def lane_fold(values):
    best = values[:, :lanes]
    for start in range(lanes, values.shape[1], lanes):
        best = jnp.maximum(best, values[:, start : start + lanes])
    return best


def gram_body(own_refs, piece_ref, row_refs, col_ref, col_start, holds_own):
    step = len(own_refs) - 1
    tile = 256
    nt = (((1,), (1,)), ((), ()))
    if holds_own:
        row_refs[step][...] = jnp.full(row_refs[step].shape, sentinel, jnp.float32)
    for first in range(0, piece_ref.shape[0], tile):
        x = piece_ref[first : first + tile, :]
        marks = x[:, :lanes].astype(jnp.float32).T[0:1, :]
        col_bias = jnp.where(marks > 1.5, dead_bias, 0.0)
        col_best = jnp.full((1, tile), sentinel, jnp.float32)
        for j in range(step + 1):
            own = own_refs[j][...]
            scores = lax.dot_general(own, x, nt, preferred_element_type=jnp.float32)
            usable = scores + col_bias
            if j == step:
                if holds_own and first < own.shape[0]:
                    rows = lax.broadcasted_iota(jnp.int32, usable.shape, 0)
                    cols = lax.broadcasted_iota(jnp.int32, usable.shape, 1)
                    usable = jnp.where(rows - cols == first, dead_bias, usable)
            else:
                row_bias = jnp.where(own[:, 0:1].astype(jnp.float32) > 1.5, dead_bias, 0.0)
                col_best = jnp.maximum(
                    col_best, jnp.max(scores + row_bias, axis=0, keepdims=True)
                )
            row_refs[j][...] = jnp.maximum(row_refs[j][...], lane_fold(usable))
        col_ref[0:1, col_start + first : col_start + first + tile] = col_best


def gram_kernel(first, step, pieces, *refs):
    news = step + 1 - first
    owns, refs = refs[: step + 1], refs[step + 1 :]
    blocks, refs = refs[: pieces * news], refs[pieces * news :]
    states, refs = refs[:first], refs[first:]
    rows, cols = refs[: step + 1], refs[step + 1 :]
    for state, row in zip(states, rows):
        row[...] = state[...]
    for k in range(news):
        now = first + k + 1
        for p in range(pieces):
            block = blocks[pieces * k + p]
            start = p * block.shape[0]
            gram_body(owns[:now], block, rows[:now], cols[k], start, p == 0)


def gram_last_kernel(step, relatives, chunks, groups, me_ref, *refs):
    members = len(relatives)
    owns, block, refs = refs[: step + 1], refs[step + 1], refs[step + 2 :]
    states, refs = refs[: step + 1], refs[step + 1 :]
    cols, refs = refs[: step + 1], refs[step + 1 :]
    out_ref, col, table = refs[:3]
    rows = refs[3:]
    for state, row in zip(states, rows):
        row[...] = state[...]
    gram_body(owns, block, rows, col, 0, False)
    first = 0
    for k, size in enumerate(chunks):
        row_k = jnp.max(rows[k][...].T, axis=0, keepdims=True)
        count = groups * size
        for p, relative in enumerate(relatives):
            source, shift = (col, 2 * count) if k == step and p >= 2 else (cols[k], 0)
            for r in range(groups):
                start = p * count + r * size - shift
                best = source[0:1, start : start + size]
                if p == 0:
                    best = jnp.maximum(best, row_k[:, r * size : (r + 1) * size])
                row = r * members + p
                table[row : row + 1, first : first + size] = best
        first += size
    for r in range(groups):
        for p, relative in enumerate(relatives):
            row = r * members + p
            target = (me_ref[0] ^ r) * members + (me_ref[1] ^ relative)
            out_ref[target] = table[row : row + 1, :]


def gram_params(owns, blocks):
    features = owns[0].shape[1]
    mine, others = sum(own.shape[0] for own in owns), sum(block.shape[0] for block in blocks)
    return dict(
        compiler_params=pltpu.CompilerParams(vmem_limit_bytes=24 * 2**20),
        cost_estimate=pl.CostEstimate(
            flops=2 * mine * others * features,
            bytes_accessed=2 * features * (mine + others),
            transcendentals=0,
        ),
    )


def gram_step(first, owns, blocks, states, pieces):
    step = len(owns) - 1
    row_shapes = [(own.shape[0], lanes) for own in owns]
    col_shapes = [(1, pieces * 2 * own.shape[0]) for own in owns[first:]]
    results = pl.pallas_call(
        functools.partial(gram_kernel, first, step, pieces),
        in_specs=[vmem] * (step + 1 + len(blocks) + first),
        out_specs=[vmem] * len(row_shapes + col_shapes),
        out_shape=[jax.ShapeDtypeStruct(s, jnp.float32) for s in row_shapes + col_shapes],
        name="gram_step",
        **gram_params(owns, blocks),
    )(*owns, *blocks, *states)
    return list(results[: step + 1]), list(results[step + 1 :])


def gram_last(me, owns, block, states, cols, relatives, chunks, groups):
    step = len(owns) - 1
    members = len(relatives)
    shape = (groups * members, 1, sum(chunks))
    return pl.pallas_call(
        functools.partial(gram_last_kernel, step, relatives, chunks, groups),
        in_specs=[smem] + [vmem] * (3 * step + 4),
        out_specs=vmem,
        out_shape=jax.ShapeDtypeStruct(shape, jnp.float32),
        scratch_shapes=[pltpu.VMEM((1, block.shape[0]), jnp.float32), pltpu.VMEM(shape[::2], jnp.float32)]
        + [pltpu.VMEM((own.shape[0], lanes), jnp.float32) for own in owns],
        name="gram_last",
        **gram_params(owns, [block]),
    )(me, *owns, block, *states, *cols)


def tail_kernel(capacity, members, slot_ref, part_ref, out_ref, table):
    groups = part_ref.shape[0] // members
    width = table.shape[1]
    table[...] = jnp.full(table.shape, sentinel, jnp.float32)
    for g in range(groups):
        table[g : g + 1, :capacity] = jnp.max(
            part_ref[g * members : (g + 1) * members], axis=0
        )
    lane = lax.broadcasted_iota(jnp.int32, (lanes, lanes), 1)
    for q in range(out_ref.shape[0]):
        slot = jnp.broadcast_to(slot_ref[q : q + 1, :], (lanes, lanes)).T
        best = jnp.full((lanes, lanes), sentinel, jnp.float32)
        for g in range(groups):
            for c in range(0, width, lanes):
                entry = table[g : g + 1, c : c + lanes]
                best = jnp.maximum(
                    best, jnp.where(slot - (g * capacity + c) == lane, entry, sentinel)
                )
        out_ref[q : q + 1, :] = jnp.max(best.T, axis=0, keepdims=True)


def tail(partials, slots, capacity, members):
    groups = partials.shape[0] // members
    width = -(-capacity // lanes) * lanes
    return pl.pallas_call(
        functools.partial(tail_kernel, capacity, members),
        in_specs=[vmem, vmem],
        out_specs=vmem,
        out_shape=jax.ShapeDtypeStruct(slots.shape, jnp.float32),
        scratch_shapes=[pltpu.VMEM((groups, width), jnp.float32)],
        name="pick_rows",
    )(slots, partials)


def on_device(embeddings, send_slot):
    row_count, features = embeddings.shape
    groups = lax.axis_size("grp")
    members = lax.axis_size("blk")
    slot_count = 2 * row_count
    capacity = slot_count // groups
    chunks = chunk_sizes(capacity)
    me = jnp.stack([lax.axis_index("grp"), lax.axis_index("blk")]).astype(jnp.int32)
    slots = send_slot.reshape(row_count // lanes, lanes)
    keeps, first_send, next_send, rest_send = head(me, embeddings, slots, capacity, chunks, groups)
    count, high = len(chunks), groups // 2
    last = count - 1

    sent, owns, done, pairs = {}, {}, {}, {}

    def rows(value, index, size):
        return value[index * size : (index + 1) * size]

    def block(step, z):
        size = chunks[step]
        near = first_near if step == 0 else sent["y", min(step, 2) + 1]
        skip = sum(chunks[2:step]) * high
        return jnp.concatenate(
            [rows(keeps[step], z, size), rows(near[skip:], z, size)], axis=0
        )

    def send(key, value, axis, size, bit, *earlier):
        held = [done[name] if name in done else sent[name] for name in earlier]
        sent[key] = swap(after(value, *held) if held else value, axis, size, bit)

    def send_z(step, z):
        early = [("z", step - 1, z)] if step >= 1 else []
        if step >= 2 and z == far[-1]:
            early += [("x", step - 2, 0)]
        if step == last and step >= 3:
            early += [("c", step - 2 if z == far[-1] else step - 3)]
        send(("z", step, z), block(step, z), "grp", groups, 2 * z, *early)

    def collect(step):
        parts = [block(step, 0)]
        for z in range(1, high):
            parts.append(sent["z", step, z])
        owns[step] = jnp.concatenate(parts, axis=0)

    def send_x(step, cuts, between):
        total = owns[step].shape[0]
        cuts = [0] + [total * cut // 384 // 16 * 16 for cut in cuts] + [total]
        parts = [name for name in sent if name[:2] == ("x", step - 1)]
        for part in range(len(cuts) - 1):
            value = owns[step][cuts[part] : cuts[part + 1]]
            early = parts if part == 0 else between[part - 1]
            send(("x", step, part), value, "blk", members, 2, *early)

    def send_c(step, *early):
        across = [sent[name] for name in list(sent) if name[:2] == ("x", step)]
        pairs[step] = jnp.concatenate([owns[step]] + across, axis=0)
        send(("c", step), pairs[step], "blk", members, 1, *early)

    far = [high // 2] + [z for z in range(1, high) if z != high // 2]
    cut = first_send.shape[0] // 32 * 16
    done["rest"] = rest_send
    send(("y", 0), first_send[:cut], "grp", groups, 1)
    send(("y", 1), first_send[cut:], "grp", groups, 1, "rest")
    send(("y", 2), next_send, "grp", groups, 1, ("y", 0))
    send(("y", 3), rest_send, "grp", groups, 1, ("y", 0))
    first_near = jnp.concatenate([sent["y", 0], sent["y", 1]], axis=0)
    for z in far:
        send_z(0, z)
    for step in range(1, count):
        collect(step - 1)
        for z in far:
            send_z(step, z)
        send_x(step - 1, [], [])
        send_c(step - 1, *[("z", step, z) for z in far])
    collect(last)
    mine = [owns[k] for k in range(count)]
    blocks = [block for k in range(last) for block in (pairs[k], sent["c", k])]
    states, cols = gram_step(0, mine[:last], blocks, [], 2)
    done["gram"] = cols[-1]
    send_x(last, [304], [["gram"]])
    send_c(last)
    states, half = gram_step(last, mine, [pairs[last]], states, 1)
    result = gram_last(
        me, mine, sent["c", last], states, cols + half, (0, 2, 1, 3), chunks, groups
    )
    homeward = lax.all_to_all(result, ("grp", "blk"), 0, 0, tiled=True)
    return tail(homeward, slots, capacity, members).reshape(row_count)


def solution(mesh):
    in_specs = (P(("grp", "blk"), None), P(("grp", "blk")))
    out_specs = P(("grp", "blk"))
    return jax.shard_map(
        on_device, mesh=mesh, in_specs=in_specs, out_specs=out_specs, check_vma=False
    )
```

```python
import functools

import jax
import jax.numpy as jnp
from jax import lax
from jax.experimental import pallas as pl
from jax.experimental.pallas import tpu as pltpu
from jax.sharding import PartitionSpec as P

sentinel = -3.0
epsilon = 1e-06
dead_mark = 2.0
dead_bias = -8.0
lanes = 128
smem = pl.BlockSpec(memory_space=pltpu.SMEM)
vmem = pl.BlockSpec(memory_space=pltpu.VMEM)


def chunk_sizes(capacity):
    count = 4 if capacity % 64 == 0 else 3
    return (capacity // count,) * count


def after(value, *earlier):
    return lax.optimization_barrier((value,) + earlier)[0]


def swap(value, axis, size, bit):
    return lax.ppermute(value, axis, [(i, i ^ bit) for i in range(size)])


def place(me, slots, normed, capacity, first, size, groups, low):
    shape = (groups // 2, size, 1)
    spot = lax.broadcasted_iota(jnp.int32, shape, 1) + first
    group = (lax.broadcasted_iota(jnp.int32, shape, 0) * 2 + low) ^ me
    wanted = (group * capacity + spot).reshape(groups // 2 * size, 1)
    pick = jnp.where(wanted == slots, 1.0, 0.0)
    live = jnp.max(pick, axis=1, keepdims=True)
    placed = jnp.dot(pick.astype(jnp.bfloat16), normed, preferred_element_type=jnp.float32)
    lane = lax.broadcasted_iota(jnp.int32, (1, placed.shape[1]), 1)
    mark = jnp.where(lane == 0, dead_mark, 0.0)
    return (placed + (1.0 - live) * mark).astype(jnp.bfloat16)


def flat(slot_ref):
    return jnp.concatenate([slot_ref[q : q + 1, :] for q in range(slot_ref.shape[0])], axis=1)


def first_kernel(capacity, chunks, groups, me_ref, slot_ref, x_ref, normed_ref, send_ref):
    wide = x_ref[...].astype(jnp.float32)
    normed_ref[...] = (
        wide * lax.rsqrt(jnp.sum(wide * wide, axis=-1, keepdims=True) + epsilon)
    ).astype(jnp.bfloat16)
    send_ref[...] = place(
        me_ref[0], flat(slot_ref), normed_ref[...], capacity, 0, chunks[0], groups, 1
    )


def rest_kernel(capacity, chunks, groups, me_ref, slot_ref, normed_ref, *out_refs):
    keeps, send_refs = out_refs[:-2], out_refs[-2:]
    slots, normed = flat(slot_ref), normed_ref[...]
    first, row = 0, 0
    for step, size in enumerate(chunks):
        placed = place(me_ref[0], slots, normed, capacity, first, size, groups, 1) if step else None
        if step == 1:
            send_refs[0][...] = placed
        elif step > 1:
            send_refs[1][row : row + placed.shape[0], :] = placed
            row += placed.shape[0]
        first += size
    first = 0
    for step, size in enumerate(chunks):
        keeps[step][...] = place(me_ref[0], slots, normed, capacity, first, size, groups, 0)
        first += size


def head(me, embeddings, slots, capacity, chunks, groups):
    rows, features = embeddings.shape
    half = [groups // 2 * size for size in chunks]

    def shape(count):
        return jax.ShapeDtypeStruct((count, features), jnp.bfloat16)

    def cost(count):
        return pl.CostEstimate(
            flops=2 * count * rows * features,
            bytes_accessed=2 * (rows + count) * features,
            transcendentals=0,
        )

    params = pltpu.CompilerParams(vmem_limit_bytes=24 * 2**20)
    normed, first_send = pl.pallas_call(
        functools.partial(first_kernel, capacity, chunks, groups),
        in_specs=[smem, vmem, vmem],
        out_specs=[vmem, vmem],
        out_shape=[shape(rows), shape(half[0])],
        compiler_params=params,
        cost_estimate=cost(half[0]),
        name="place_first",
    )(me, slots, embeddings)
    *keeps, next_send, rest_send = pl.pallas_call(
        functools.partial(rest_kernel, capacity, chunks, groups),
        in_specs=[smem, vmem, vmem],
        out_specs=[vmem] * (len(chunks) + 2),
        out_shape=[shape(count) for count in half + [half[1], sum(half[2:])]],
        compiler_params=params,
        cost_estimate=cost(2 * sum(half) - half[0]),
        name="place_rest",
    )(me, slots, normed)
    return keeps, first_send, next_send, rest_send


def lane_fold(values):
    best = values[:, :lanes]
    for start in range(lanes, values.shape[1], lanes):
        best = jnp.maximum(best, values[:, start : start + lanes])
    return best


def gram_body(own_refs, piece_ref, row_refs, col_ref, col_start, holds_own):
    step = len(own_refs) - 1
    tile = 256
    nt = (((1,), (1,)), ((), ()))
    if holds_own:
        row_refs[step][...] = jnp.full(row_refs[step].shape, sentinel, jnp.float32)
    for first in range(0, piece_ref.shape[0], tile):
        x = piece_ref[first : first + tile, :]
        marks = x[:, :lanes].astype(jnp.float32).T[0:1, :]
        col_bias = jnp.where(marks > 1.5, dead_bias, 0.0)
        col_best = jnp.full((1, tile), sentinel, jnp.float32)
        for j in range(step + 1):
            own = own_refs[j][...]
            scores = lax.dot_general(own, x, nt, preferred_element_type=jnp.float32)
            usable = scores + col_bias
            if j == step:
                if holds_own and first < own.shape[0]:
                    rows = lax.broadcasted_iota(jnp.int32, usable.shape, 0)
                    cols = lax.broadcasted_iota(jnp.int32, usable.shape, 1)
                    usable = jnp.where(rows - cols == first, dead_bias, usable)
            else:
                row_bias = jnp.where(own[:, 0:1].astype(jnp.float32) > 1.5, dead_bias, 0.0)
                col_best = jnp.maximum(
                    col_best, jnp.max(scores + row_bias, axis=0, keepdims=True)
                )
            row_refs[j][...] = jnp.maximum(row_refs[j][...], lane_fold(usable))
        col_ref[0:1, col_start + first : col_start + first + tile] = col_best


def gram_kernel(first, step, pieces, *refs):
    news = step + 1 - first
    owns, refs = refs[: step + 1], refs[step + 1 :]
    blocks, refs = refs[: pieces * news], refs[pieces * news :]
    states, refs = refs[:first], refs[first:]
    rows, cols = refs[: step + 1], refs[step + 1 :]
    for state, row in zip(states, rows):
        row[...] = state[...]
    for k in range(news):
        now = first + k + 1
        for p in range(pieces):
            block = blocks[pieces * k + p]
            start = p * block.shape[0]
            gram_body(owns[:now], block, rows[:now], cols[k], start, p == 0)


def gram_last_kernel(step, relatives, chunks, groups, me_ref, *refs):
    members = len(relatives)
    owns, block, refs = refs[: step + 1], refs[step + 1], refs[step + 2 :]
    states, refs = refs[: step + 1], refs[step + 1 :]
    cols, refs = refs[: step + 1], refs[step + 1 :]
    out_ref, col, table = refs[:3]
    rows = refs[3:]
    for state, row in zip(states, rows):
        row[...] = state[...]
    gram_body(owns, block, rows, col, 0, False)
    first = 0
    for k, size in enumerate(chunks):
        row_k = jnp.max(rows[k][...].T, axis=0, keepdims=True)
        count = groups * size
        for p, relative in enumerate(relatives):
            source, shift = (col, 2 * count) if k == step and p >= 2 else (cols[k], 0)
            for r in range(groups):
                start = p * count + r * size - shift
                best = source[0:1, start : start + size]
                if p == 0:
                    best = jnp.maximum(best, row_k[:, r * size : (r + 1) * size])
                row = r * members + p
                table[row : row + 1, first : first + size] = best
        first += size
    for r in range(groups):
        for p, relative in enumerate(relatives):
            row = r * members + p
            target = (me_ref[0] ^ r) * members + (me_ref[1] ^ relative)
            out_ref[target] = table[row : row + 1, :]


def gram_params(owns, blocks):
    features = owns[0].shape[1]
    mine, others = sum(own.shape[0] for own in owns), sum(block.shape[0] for block in blocks)
    return dict(
        compiler_params=pltpu.CompilerParams(vmem_limit_bytes=24 * 2**20),
        cost_estimate=pl.CostEstimate(
            flops=2 * mine * others * features,
            bytes_accessed=2 * features * (mine + others),
            transcendentals=0,
        ),
    )


def gram_step(first, owns, blocks, states, pieces):
    step = len(owns) - 1
    row_shapes = [(own.shape[0], lanes) for own in owns]
    col_shapes = [(1, pieces * 2 * own.shape[0]) for own in owns[first:]]
    results = pl.pallas_call(
        functools.partial(gram_kernel, first, step, pieces),
        in_specs=[vmem] * (step + 1 + len(blocks) + first),
        out_specs=[vmem] * len(row_shapes + col_shapes),
        out_shape=[jax.ShapeDtypeStruct(s, jnp.float32) for s in row_shapes + col_shapes],
        name="gram_step",
        **gram_params(owns, blocks),
    )(*owns, *blocks, *states)
    return list(results[: step + 1]), list(results[step + 1 :])


def gram_last(me, owns, block, states, cols, relatives, chunks, groups):
    step = len(owns) - 1
    members = len(relatives)
    shape = (groups * members, 1, sum(chunks))
    return pl.pallas_call(
        functools.partial(gram_last_kernel, step, relatives, chunks, groups),
        in_specs=[smem] + [vmem] * (3 * step + 4),
        out_specs=vmem,
        out_shape=jax.ShapeDtypeStruct(shape, jnp.float32),
        scratch_shapes=[pltpu.VMEM((1, block.shape[0]), jnp.float32), pltpu.VMEM(shape[::2], jnp.float32)]
        + [pltpu.VMEM((own.shape[0], lanes), jnp.float32) for own in owns],
        name="gram_last",
        **gram_params(owns, [block]),
    )(me, *owns, block, *states, *cols)


def tail_kernel(capacity, members, slot_ref, part_ref, out_ref, table):
    groups = part_ref.shape[0] // members
    width = table.shape[1]
    table[...] = jnp.full(table.shape, sentinel, jnp.float32)
    for g in range(groups):
        table[g : g + 1, :capacity] = jnp.max(
            part_ref[g * members : (g + 1) * members], axis=0
        )
    lane = lax.broadcasted_iota(jnp.int32, (lanes, lanes), 1)
    for q in range(out_ref.shape[0]):
        slot = jnp.broadcast_to(slot_ref[q : q + 1, :], (lanes, lanes)).T
        best = jnp.full((lanes, lanes), sentinel, jnp.float32)
        for g in range(groups):
            for c in range(0, width, lanes):
                entry = table[g : g + 1, c : c + lanes]
                best = jnp.maximum(
                    best, jnp.where(slot - (g * capacity + c) == lane, entry, sentinel)
                )
        out_ref[q : q + 1, :] = jnp.max(best.T, axis=0, keepdims=True)


def tail(partials, slots, capacity, members):
    groups = partials.shape[0] // members
    width = -(-capacity // lanes) * lanes
    return pl.pallas_call(
        functools.partial(tail_kernel, capacity, members),
        in_specs=[vmem, vmem],
        out_specs=vmem,
        out_shape=jax.ShapeDtypeStruct(slots.shape, jnp.float32),
        scratch_shapes=[pltpu.VMEM((groups, width), jnp.float32)],
        name="pick_rows",
    )(slots, partials)


def on_device(embeddings, send_slot):
    row_count, features = embeddings.shape
    groups = lax.axis_size("grp")
    members = lax.axis_size("blk")
    slot_count = 2 * row_count
    capacity = slot_count // groups
    chunks = chunk_sizes(capacity)
    me = jnp.stack([lax.axis_index("grp"), lax.axis_index("blk")]).astype(jnp.int32)
    slots = send_slot.reshape(row_count // lanes, lanes)
    keeps, first_send, next_send, rest_send = head(me, embeddings, slots, capacity, chunks, groups)
    count, high = len(chunks), groups // 2
    last = count - 1

    sent, owns, done, pairs = {}, {}, {}, {}

    def rows(value, index, size):
        return value[index * size : (index + 1) * size]

    def block(step, z):
        size = chunks[step]
        near = first_near if step == 0 else sent["y", min(step, 2) + 1]
        skip = sum(chunks[2:step]) * high
        return jnp.concatenate(
            [rows(keeps[step], z, size), rows(near[skip:], z, size)], axis=0
        )

    def send(key, value, axis, size, bit, *earlier):
        held = [done[name] if name in done else sent[name] for name in earlier]
        sent[key] = swap(after(value, *held) if held else value, axis, size, bit)

    def send_z(step, z):
        early = [("z", step - 1, z)] if step >= 1 else []
        if step >= 2 and z == far[-1]:
            early += [("x", step - 2, 0)]
        if step >= 2 and z == 1:
            early += [("c", step - 2)]
        send(("z", step, z), block(step, z), "grp", groups, 2 * z, *early)

    def collect(step):
        parts = [block(step, 0)]
        for z in range(1, high):
            parts.append(sent["z", step, z])
        owns[step] = jnp.concatenate(parts, axis=0)

    def send_x(step, cuts, between):
        total = owns[step].shape[0]
        cuts = [0] + [total * cut // 384 // 16 * 16 for cut in cuts] + [total]
        parts = [name for name in sent if name[:2] == ("x", step - 1)]
        for part in range(len(cuts) - 1):
            value = owns[step][cuts[part] : cuts[part + 1]]
            early = parts if part == 0 else between[part - 1]
            send(("x", step, part), value, "blk", members, 2, *early)

    def send_c(step, *early):
        across = [sent[name] for name in list(sent) if name[:2] == ("x", step)]
        pairs[step] = jnp.concatenate([owns[step]] + across, axis=0)
        send(("c", step), pairs[step], "blk", members, 1, *early)

    far = [high // 2] + [z for z in range(1, high) if z != high // 2]
    cut = first_send.shape[0] // 32 * 16
    done["rest"] = rest_send
    send(("y", 0), first_send[:cut], "grp", groups, 1)
    send(("y", 1), first_send[cut:], "grp", groups, 1, "rest")
    send(("y", 2), next_send, "grp", groups, 1, ("y", 0))
    send(("y", 3), rest_send, "grp", groups, 1, ("y", 0))
    first_near = jnp.concatenate([sent["y", 0], sent["y", 1]], axis=0)
    for z in far:
        send_z(0, z)
    for step in range(1, count):
        collect(step - 1)
        for z in far:
            send_z(step, z)
        send_x(step - 1, [], [])
        send_c(step - 1, *[("z", step, z) for z in far])
    collect(last)
    mine = [owns[k] for k in range(count)]
    blocks = [block for k in range(last) for block in (pairs[k], sent["c", k])]
    states, cols = gram_step(0, mine[:last], blocks, [], 2)
    done["gram"] = cols[-1]
    send_x(last, [304], [["gram"]])
    send_c(last)
    states, half = gram_step(last, mine, [pairs[last]], states, 1)
    result = gram_last(
        me, mine, sent["c", last], states, cols + half, (0, 2, 1, 3), chunks, groups
    )
    homeward = lax.all_to_all(result, ("grp", "blk"), 0, 0, tiled=True)
    return tail(homeward, slots, capacity, members).reshape(row_count)


def solution(mesh):
    in_specs = (P(("grp", "blk"), None), P(("grp", "blk")))
    out_specs = P(("grp", "blk"))
    return jax.shard_map(
        on_device, mesh=mesh, in_specs=in_specs, out_specs=out_specs, check_vma=False
    )
```

```python
import functools

import jax
import jax.numpy as jnp
from jax import lax
from jax.experimental import pallas as pl
from jax.experimental.pallas import tpu as pltpu
from jax.sharding import PartitionSpec as P

sentinel = -3.0
epsilon = 1e-06
dead_mark = 2.0
dead_bias = -8.0
lanes = 128
smem = pl.BlockSpec(memory_space=pltpu.SMEM)
vmem = pl.BlockSpec(memory_space=pltpu.VMEM)


def chunk_sizes(capacity):
    count = 4 if capacity % 64 == 0 else 3
    return (capacity // count,) * count


def after(value, *earlier):
    return lax.optimization_barrier((value,) + earlier)[0]


def swap(value, axis, size, bit):
    return lax.ppermute(value, axis, [(i, i ^ bit) for i in range(size)])


def place(me, slots, normed, capacity, first, size, groups, low):
    shape = (groups // 2, size, 1)
    spot = lax.broadcasted_iota(jnp.int32, shape, 1) + first
    group = (lax.broadcasted_iota(jnp.int32, shape, 0) * 2 + low) ^ me
    wanted = (group * capacity + spot).reshape(groups // 2 * size, 1)
    pick = jnp.where(wanted == slots, 1.0, 0.0)
    live = jnp.max(pick, axis=1, keepdims=True)
    placed = jnp.dot(pick.astype(jnp.bfloat16), normed, preferred_element_type=jnp.float32)
    lane = lax.broadcasted_iota(jnp.int32, (1, placed.shape[1]), 1)
    mark = jnp.where(lane == 0, dead_mark, 0.0)
    return (placed + (1.0 - live) * mark).astype(jnp.bfloat16)


def flat(slot_ref):
    return jnp.concatenate([slot_ref[q : q + 1, :] for q in range(slot_ref.shape[0])], axis=1)


def first_kernel(capacity, chunks, groups, me_ref, slot_ref, x_ref, normed_ref, send_ref):
    wide = x_ref[...].astype(jnp.float32)
    normed_ref[...] = (
        wide * lax.rsqrt(jnp.sum(wide * wide, axis=-1, keepdims=True) + epsilon)
    ).astype(jnp.bfloat16)
    send_ref[...] = place(
        me_ref[0], flat(slot_ref), normed_ref[...], capacity, 0, chunks[0], groups, 1
    )


def rest_kernel(capacity, chunks, groups, me_ref, slot_ref, normed_ref, *out_refs):
    keeps, send_refs = out_refs[: len(chunks)], out_refs[len(chunks) :]
    slots, normed = flat(slot_ref), normed_ref[...]
    first = 0
    for step, size in enumerate(chunks):
        if step > 0:
            send_refs[step - 1][...] = place(
                me_ref[0], slots, normed, capacity, first, size, groups, 1
            )
        first += size
    first = 0
    for step, size in enumerate(chunks):
        keeps[step][...] = place(me_ref[0], slots, normed, capacity, first, size, groups, 0)
        first += size


def head(me, embeddings, slots, capacity, chunks, groups):
    rows, features = embeddings.shape
    half = [groups // 2 * size for size in chunks]

    def shape(count):
        return jax.ShapeDtypeStruct((count, features), jnp.bfloat16)

    def cost(count):
        return pl.CostEstimate(
            flops=2 * count * rows * features,
            bytes_accessed=2 * (rows + count) * features,
            transcendentals=0,
        )

    params = pltpu.CompilerParams(vmem_limit_bytes=24 * 2**20)
    normed, first_send = pl.pallas_call(
        functools.partial(first_kernel, capacity, chunks, groups),
        in_specs=[smem, vmem, vmem],
        out_specs=[vmem, vmem],
        out_shape=[shape(rows), shape(half[0])],
        compiler_params=params,
        cost_estimate=cost(half[0]),
        name="place_first",
    )(me, slots, embeddings)
    *placed, = pl.pallas_call(
        functools.partial(rest_kernel, capacity, chunks, groups),
        in_specs=[smem, vmem, vmem],
        out_specs=[vmem] * (2 * len(chunks) - 1),
        out_shape=[shape(count) for count in half + half[1:]],
        compiler_params=params,
        cost_estimate=cost(2 * sum(half) - half[0]),
        name="place_rest",
    )(me, slots, normed)
    return placed[: len(chunks)], [first_send] + placed[len(chunks) :]


def lane_fold(values):
    best = values[:, :lanes]
    for start in range(lanes, values.shape[1], lanes):
        best = jnp.maximum(best, values[:, start : start + lanes])
    return best


def gram_body(own_refs, piece_ref, row_refs, col_ref, col_start, holds_own):
    step = len(own_refs) - 1
    tile = 256
    nt = (((1,), (1,)), ((), ()))
    if holds_own:
        row_refs[step][...] = jnp.full(row_refs[step].shape, sentinel, jnp.float32)
    for first in range(0, piece_ref.shape[0], tile):
        x = piece_ref[first : first + tile, :]
        marks = x[:, :lanes].astype(jnp.float32).T[0:1, :]
        col_bias = jnp.where(marks > 1.5, dead_bias, 0.0)
        col_best = jnp.full((1, tile), sentinel, jnp.float32)
        for j in range(step + 1):
            own = own_refs[j][...]
            scores = lax.dot_general(own, x, nt, preferred_element_type=jnp.float32)
            usable = scores + col_bias
            if j == step:
                if holds_own and first < own.shape[0]:
                    rows = lax.broadcasted_iota(jnp.int32, usable.shape, 0)
                    cols = lax.broadcasted_iota(jnp.int32, usable.shape, 1)
                    usable = jnp.where(rows - cols == first, dead_bias, usable)
            else:
                row_bias = jnp.where(own[:, 0:1].astype(jnp.float32) > 1.5, dead_bias, 0.0)
                col_best = jnp.maximum(
                    col_best, jnp.max(scores + row_bias, axis=0, keepdims=True)
                )
            row_refs[j][...] = jnp.maximum(row_refs[j][...], lane_fold(usable))
        col_ref[0:1, col_start + first : col_start + first + tile] = col_best


def gram_kernel(first, step, pieces, *refs):
    news = step + 1 - first
    owns, refs = refs[: step + 1], refs[step + 1 :]
    blocks, refs = refs[: pieces * news], refs[pieces * news :]
    states, refs = refs[:first], refs[first:]
    rows, cols = refs[: step + 1], refs[step + 1 :]
    for state, row in zip(states, rows):
        row[...] = state[...]
    for k in range(news):
        now = first + k + 1
        for p in range(pieces):
            block = blocks[pieces * k + p]
            start = p * block.shape[0]
            gram_body(owns[:now], block, rows[:now], cols[k], start, p == 0)


def gram_last_kernel(step, relatives, chunks, groups, me_ref, *refs):
    members = len(relatives)
    owns, block, refs = refs[: step + 1], refs[step + 1], refs[step + 2 :]
    states, refs = refs[: step + 1], refs[step + 1 :]
    cols, refs = refs[: step + 1], refs[step + 1 :]
    out_ref, col, table = refs[:3]
    rows = refs[3:]
    for state, row in zip(states, rows):
        row[...] = state[...]
    gram_body(owns, block, rows, col, 0, False)
    first = 0
    for k, size in enumerate(chunks):
        row_k = jnp.max(rows[k][...].T, axis=0, keepdims=True)
        count = groups * size
        for p, relative in enumerate(relatives):
            source, shift = (col, 2 * count) if k == step and p >= 2 else (cols[k], 0)
            for r in range(groups):
                start = p * count + r * size - shift
                best = source[0:1, start : start + size]
                if p == 0:
                    best = jnp.maximum(best, row_k[:, r * size : (r + 1) * size])
                row = r * members + p
                table[row : row + 1, first : first + size] = best
        first += size
    for r in range(groups):
        for p, relative in enumerate(relatives):
            row = r * members + p
            target = (me_ref[0] ^ r) * members + (me_ref[1] ^ relative)
            out_ref[target] = table[row : row + 1, :]


def gram_params(owns, blocks):
    features = owns[0].shape[1]
    mine, others = sum(own.shape[0] for own in owns), sum(block.shape[0] for block in blocks)
    return dict(
        compiler_params=pltpu.CompilerParams(vmem_limit_bytes=24 * 2**20),
        cost_estimate=pl.CostEstimate(
            flops=2 * mine * others * features,
            bytes_accessed=2 * features * (mine + others),
            transcendentals=0,
        ),
    )


def gram_step(first, owns, blocks, states, pieces):
    step = len(owns) - 1
    row_shapes = [(own.shape[0], lanes) for own in owns]
    col_shapes = [(1, pieces * 2 * own.shape[0]) for own in owns[first:]]
    results = pl.pallas_call(
        functools.partial(gram_kernel, first, step, pieces),
        in_specs=[vmem] * (step + 1 + len(blocks) + first),
        out_specs=[vmem] * len(row_shapes + col_shapes),
        out_shape=[jax.ShapeDtypeStruct(s, jnp.float32) for s in row_shapes + col_shapes],
        name="gram_step",
        **gram_params(owns, blocks),
    )(*owns, *blocks, *states)
    return list(results[: step + 1]), list(results[step + 1 :])


def gram_last(me, owns, block, states, cols, relatives, chunks, groups):
    step = len(owns) - 1
    members = len(relatives)
    shape = (groups * members, 1, sum(chunks))
    return pl.pallas_call(
        functools.partial(gram_last_kernel, step, relatives, chunks, groups),
        in_specs=[smem] + [vmem] * (3 * step + 4),
        out_specs=vmem,
        out_shape=jax.ShapeDtypeStruct(shape, jnp.float32),
        scratch_shapes=[pltpu.VMEM((1, block.shape[0]), jnp.float32), pltpu.VMEM(shape[::2], jnp.float32)]
        + [pltpu.VMEM((own.shape[0], lanes), jnp.float32) for own in owns],
        name="gram_last",
        **gram_params(owns, [block]),
    )(me, *owns, block, *states, *cols)


def tail_kernel(capacity, members, slot_ref, part_ref, out_ref, table):
    groups = part_ref.shape[0] // members
    width = table.shape[1]
    table[...] = jnp.full(table.shape, sentinel, jnp.float32)
    for g in range(groups):
        table[g : g + 1, :capacity] = jnp.max(
            part_ref[g * members : (g + 1) * members], axis=0
        )
    lane = lax.broadcasted_iota(jnp.int32, (lanes, lanes), 1)
    for q in range(out_ref.shape[0]):
        slot = jnp.broadcast_to(slot_ref[q : q + 1, :], (lanes, lanes)).T
        best = jnp.full((lanes, lanes), sentinel, jnp.float32)
        for g in range(groups):
            for c in range(0, width, lanes):
                entry = table[g : g + 1, c : c + lanes]
                best = jnp.maximum(
                    best, jnp.where(slot - (g * capacity + c) == lane, entry, sentinel)
                )
        out_ref[q : q + 1, :] = jnp.max(best.T, axis=0, keepdims=True)


def tail(partials, slots, capacity, members):
    groups = partials.shape[0] // members
    width = -(-capacity // lanes) * lanes
    return pl.pallas_call(
        functools.partial(tail_kernel, capacity, members),
        in_specs=[vmem, vmem],
        out_specs=vmem,
        out_shape=jax.ShapeDtypeStruct(slots.shape, jnp.float32),
        scratch_shapes=[pltpu.VMEM((groups, width), jnp.float32)],
        name="pick_rows",
    )(slots, partials)


def on_device(embeddings, send_slot):
    row_count, features = embeddings.shape
    groups = lax.axis_size("grp")
    members = lax.axis_size("blk")
    slot_count = 2 * row_count
    capacity = slot_count // groups
    chunks = chunk_sizes(capacity)
    me = jnp.stack([lax.axis_index("grp"), lax.axis_index("blk")]).astype(jnp.int32)
    slots = send_slot.reshape(row_count // lanes, lanes)
    keeps, sends = head(me, embeddings, slots, capacity, chunks, groups)
    count, high = len(chunks), groups // 2
    last = count - 1

    sent, owns, done, pairs = {}, {}, {}, {}

    def rows(value, index, size):
        return value[index * size : (index + 1) * size]

    def block(step, z):
        size = chunks[step]
        near = first_near if step == 0 else sent["y", step + 1]
        return jnp.concatenate([rows(keeps[step], z, size), rows(near, z, size)], axis=0)

    def send(key, value, axis, size, bit, *earlier):
        held = [done[name] if name in done else sent[name] for name in earlier]
        sent[key] = swap(after(value, *held) if held else value, axis, size, bit)

    def send_z(step, z):
        early = [("z", step - 1, z)] if step >= 1 else []
        if step >= 2 and z == far[-1]:
            early += [("x", step - 2, 0)]
        if step >= 2 and z == 1:
            early += [("c", step - 2)]
        send(("z", step, z), block(step, z), "grp", groups, 2 * z, *early)

    def collect(step):
        parts = [block(step, 0)]
        for z in range(1, high):
            parts.append(sent["z", step, z])
        owns[step] = jnp.concatenate(parts, axis=0)

    def send_x(step, cuts, between):
        total = owns[step].shape[0]
        cuts = [0] + [total * cut // 384 // 16 * 16 for cut in cuts] + [total]
        parts = [name for name in sent if name[:2] == ("x", step - 1)]
        for part in range(len(cuts) - 1):
            value = owns[step][cuts[part] : cuts[part + 1]]
            early = parts if part == 0 else between[part - 1]
            send(("x", step, part), value, "blk", members, 2, *early)

    def send_c(step, *early):
        across = [sent[name] for name in list(sent) if name[:2] == ("x", step)]
        pairs[step] = jnp.concatenate([owns[step]] + across, axis=0)
        send(("c", step), pairs[step], "blk", members, 1, *early)

    far = [high // 2] + [z for z in range(1, high) if z != high // 2]
    cut = sends[0].shape[0] // 32 * 16
    done["rest"] = sends[1]
    send(("y", 0), sends[0][:cut], "grp", groups, 1)
    send(("y", 1), sends[0][cut:], "grp", groups, 1, "rest")
    send(("y", 2), sends[1], "grp", groups, 1, ("y", 0))
    for step in range(2, count):
        early = ("y", 0) if step == 2 else ("y", step)
        send(("y", step + 1), sends[step], "grp", groups, 1, early)
    first_near = jnp.concatenate([sent["y", 0], sent["y", 1]], axis=0)
    for z in far:
        send_z(0, z)
    for step in range(1, count):
        collect(step - 1)
        for z in far:
            send_z(step, z)
        send_x(step - 1, [], [])
        send_c(step - 1, *[("z", step, z) for z in far])
    collect(last)
    mine = [owns[k] for k in range(count)]
    blocks = [block for k in range(last) for block in (pairs[k], sent["c", k])]
    states, cols = gram_step(0, mine[:last], blocks, [], 2)
    done["gram"] = cols[-1]
    send_x(last, [304], [["gram"]])
    send_c(last)
    states, half = gram_step(last, mine, [pairs[last]], states, 1)
    result = gram_last(
        me, mine, sent["c", last], states, cols + half, (0, 2, 1, 3), chunks, groups
    )
    homeward = lax.all_to_all(result, ("grp", "blk"), 0, 0, tiled=True)
    return tail(homeward, slots, capacity, members).reshape(row_count)


def solution(mesh):
    in_specs = (P(("grp", "blk"), None), P(("grp", "blk")))
    out_specs = P(("grp", "blk"))
    return jax.shard_map(
        on_device, mesh=mesh, in_specs=in_specs, out_specs=out_specs, check_vma=False
    )
```

```python
import functools

import jax
import jax.numpy as jnp
from jax import lax
from jax.experimental import pallas as pl
from jax.experimental.pallas import tpu as pltpu
from jax.sharding import PartitionSpec as P

sentinel = -3.0
epsilon = 1e-06
dead_mark = 2.0
dead_bias = -8.0
lanes = 128
smem = pl.BlockSpec(memory_space=pltpu.SMEM)
vmem = pl.BlockSpec(memory_space=pltpu.VMEM)


def chunk_sizes(capacity):
    count = 4 if capacity % 64 == 0 else 3
    return (capacity // count,) * count


def after(value, *earlier):
    return lax.optimization_barrier((value,) + earlier)[0]


def swap(value, axis, size, bit):
    return lax.ppermute(value, axis, [(i, i ^ bit) for i in range(size)])


def place(me, slots, normed, capacity, first, size, groups, low):
    shape = (groups // 2, size, 1)
    spot = lax.broadcasted_iota(jnp.int32, shape, 1) + first
    group = (lax.broadcasted_iota(jnp.int32, shape, 0) * 2 + low) ^ me
    wanted = (group * capacity + spot).reshape(groups // 2 * size, 1)
    pick = jnp.where(wanted == slots, 1.0, 0.0)
    live = jnp.max(pick, axis=1, keepdims=True)
    placed = jnp.dot(pick.astype(jnp.bfloat16), normed, preferred_element_type=jnp.float32)
    lane = lax.broadcasted_iota(jnp.int32, (1, placed.shape[1]), 1)
    mark = jnp.where(lane == 0, dead_mark, 0.0)
    return (placed + (1.0 - live) * mark).astype(jnp.bfloat16)


def flat(slot_ref):
    return jnp.concatenate([slot_ref[q : q + 1, :] for q in range(slot_ref.shape[0])], axis=1)


def first_kernel(capacity, chunks, groups, me_ref, slot_ref, x_ref, normed_ref, send_ref):
    wide = x_ref[...].astype(jnp.float32)
    normed_ref[...] = (
        wide * lax.rsqrt(jnp.sum(wide * wide, axis=-1, keepdims=True) + epsilon)
    ).astype(jnp.bfloat16)
    send_ref[...] = place(
        me_ref[0], flat(slot_ref), normed_ref[...], capacity, 0, chunks[0], groups, 1
    )


def rest_kernel(capacity, chunks, groups, me_ref, slot_ref, normed_ref, *out_refs):
    keeps, send_refs = out_refs[: len(chunks)], out_refs[len(chunks) :]
    slots, normed = flat(slot_ref), normed_ref[...]
    first = 0
    for step, size in enumerate(chunks):
        if step > 0:
            send_refs[step - 1][...] = place(
                me_ref[0], slots, normed, capacity, first, size, groups, 1
            )
        first += size
    first = 0
    for step, size in enumerate(chunks):
        keeps[step][...] = place(me_ref[0], slots, normed, capacity, first, size, groups, 0)
        first += size


def head(me, embeddings, slots, capacity, chunks, groups):
    rows, features = embeddings.shape
    half = [groups // 2 * size for size in chunks]

    def shape(count):
        return jax.ShapeDtypeStruct((count, features), jnp.bfloat16)

    def cost(count):
        return pl.CostEstimate(
            flops=2 * count * rows * features,
            bytes_accessed=2 * (rows + count) * features,
            transcendentals=0,
        )

    params = pltpu.CompilerParams(vmem_limit_bytes=24 * 2**20)
    normed, first_send = pl.pallas_call(
        functools.partial(first_kernel, capacity, chunks, groups),
        in_specs=[smem, vmem, vmem],
        out_specs=[vmem, vmem],
        out_shape=[shape(rows), shape(half[0])],
        compiler_params=params,
        cost_estimate=cost(half[0]),
        name="place_first",
    )(me, slots, embeddings)
    *placed, = pl.pallas_call(
        functools.partial(rest_kernel, capacity, chunks, groups),
        in_specs=[smem, vmem, vmem],
        out_specs=[vmem] * (2 * len(chunks) - 1),
        out_shape=[shape(count) for count in half + half[1:]],
        compiler_params=params,
        cost_estimate=cost(2 * sum(half) - half[0]),
        name="place_rest",
    )(me, slots, normed)
    return placed[: len(chunks)], [first_send] + placed[len(chunks) :]


def lane_fold(values):
    best = values[:, :lanes]
    for start in range(lanes, values.shape[1], lanes):
        best = jnp.maximum(best, values[:, start : start + lanes])
    return best


def gram_body(own_refs, piece_ref, row_refs, col_ref, col_start, holds_own):
    step = len(own_refs) - 1
    tile = 256
    nt = (((1,), (1,)), ((), ()))
    if holds_own:
        row_refs[step][...] = jnp.full(row_refs[step].shape, sentinel, jnp.float32)
    for first in range(0, piece_ref.shape[0], tile):
        x = piece_ref[first : first + tile, :]
        marks = x[:, :lanes].astype(jnp.float32).T[0:1, :]
        col_bias = jnp.where(marks > 1.5, dead_bias, 0.0)
        col_best = jnp.full((1, tile), sentinel, jnp.float32)
        for j in range(step + 1):
            own = own_refs[j][...]
            scores = lax.dot_general(own, x, nt, preferred_element_type=jnp.float32)
            usable = scores + col_bias
            if j == step:
                if holds_own and first < own.shape[0]:
                    rows = lax.broadcasted_iota(jnp.int32, usable.shape, 0)
                    cols = lax.broadcasted_iota(jnp.int32, usable.shape, 1)
                    usable = jnp.where(rows - cols == first, dead_bias, usable)
            else:
                row_bias = jnp.where(own[:, 0:1].astype(jnp.float32) > 1.5, dead_bias, 0.0)
                col_best = jnp.maximum(
                    col_best, jnp.max(scores + row_bias, axis=0, keepdims=True)
                )
            row_refs[j][...] = jnp.maximum(row_refs[j][...], lane_fold(usable))
        col_ref[0:1, col_start + first : col_start + first + tile] = col_best


def gram_kernel(first, step, pieces, *refs):
    news = step + 1 - first
    owns, refs = refs[: step + 1], refs[step + 1 :]
    blocks, refs = refs[: pieces * news], refs[pieces * news :]
    states, refs = refs[:first], refs[first:]
    rows, cols = refs[: step + 1], refs[step + 1 :]
    for state, row in zip(states, rows):
        row[...] = state[...]
    for k in range(news):
        now = first + k + 1
        for p in range(pieces):
            block = blocks[pieces * k + p]
            start = p * block.shape[0]
            gram_body(owns[:now], block, rows[:now], cols[k], start, p == 0)


def gram_last_kernel(step, relatives, chunks, groups, me_ref, *refs):
    members = len(relatives)
    owns, block, refs = refs[: step + 1], refs[step + 1], refs[step + 2 :]
    states, refs = refs[: step + 1], refs[step + 1 :]
    cols, refs = refs[: step + 1], refs[step + 1 :]
    out_ref, col, table = refs[:3]
    rows = refs[3:]
    for state, row in zip(states, rows):
        row[...] = state[...]
    gram_body(owns, block, rows, col, 0, False)
    first = 0
    for k, size in enumerate(chunks):
        row_k = jnp.max(rows[k][...].T, axis=0, keepdims=True)
        count = groups * size
        for p, relative in enumerate(relatives):
            source, shift = (col, 2 * count) if k == step and p >= 2 else (cols[k], 0)
            for r in range(groups):
                start = p * count + r * size - shift
                best = source[0:1, start : start + size]
                if p == 0:
                    best = jnp.maximum(best, row_k[:, r * size : (r + 1) * size])
                row = r * members + p
                table[row : row + 1, first : first + size] = best
        first += size
    for r in range(groups):
        for p, relative in enumerate(relatives):
            row = r * members + p
            target = (me_ref[0] ^ r) * members + (me_ref[1] ^ relative)
            out_ref[target] = table[row : row + 1, :]


def gram_params(owns, blocks):
    features = owns[0].shape[1]
    mine, others = sum(own.shape[0] for own in owns), sum(block.shape[0] for block in blocks)
    return dict(
        compiler_params=pltpu.CompilerParams(vmem_limit_bytes=24 * 2**20),
        cost_estimate=pl.CostEstimate(
            flops=2 * mine * others * features,
            bytes_accessed=2 * features * (mine + others),
            transcendentals=0,
        ),
    )


def gram_step(first, owns, blocks, states, pieces):
    step = len(owns) - 1
    row_shapes = [(own.shape[0], lanes) for own in owns]
    col_shapes = [(1, pieces * 2 * own.shape[0]) for own in owns[first:]]
    results = pl.pallas_call(
        functools.partial(gram_kernel, first, step, pieces),
        in_specs=[vmem] * (step + 1 + len(blocks) + first),
        out_specs=[vmem] * len(row_shapes + col_shapes),
        out_shape=[jax.ShapeDtypeStruct(s, jnp.float32) for s in row_shapes + col_shapes],
        name="gram_step",
        **gram_params(owns, blocks),
    )(*owns, *blocks, *states)
    return list(results[: step + 1]), list(results[step + 1 :])


def gram_last(me, owns, block, states, cols, relatives, chunks, groups):
    step = len(owns) - 1
    members = len(relatives)
    shape = (groups * members, 1, sum(chunks))
    return pl.pallas_call(
        functools.partial(gram_last_kernel, step, relatives, chunks, groups),
        in_specs=[smem] + [vmem] * (3 * step + 4),
        out_specs=vmem,
        out_shape=jax.ShapeDtypeStruct(shape, jnp.float32),
        scratch_shapes=[pltpu.VMEM((1, block.shape[0]), jnp.float32), pltpu.VMEM(shape[::2], jnp.float32)]
        + [pltpu.VMEM((own.shape[0], lanes), jnp.float32) for own in owns],
        name="gram_last",
        **gram_params(owns, [block]),
    )(me, *owns, block, *states, *cols)


def tail_kernel(capacity, members, slot_ref, part_ref, out_ref, table):
    groups = part_ref.shape[0] // members
    width = table.shape[1]
    table[...] = jnp.full(table.shape, sentinel, jnp.float32)
    for g in range(groups):
        table[g : g + 1, :capacity] = jnp.max(
            part_ref[g * members : (g + 1) * members], axis=0
        )
    lane = lax.broadcasted_iota(jnp.int32, (lanes, lanes), 1)
    for q in range(out_ref.shape[0]):
        slot = jnp.broadcast_to(slot_ref[q : q + 1, :], (lanes, lanes)).T
        best = jnp.full((lanes, lanes), sentinel, jnp.float32)
        for g in range(groups):
            for c in range(0, width, lanes):
                entry = table[g : g + 1, c : c + lanes]
                best = jnp.maximum(
                    best, jnp.where(slot - (g * capacity + c) == lane, entry, sentinel)
                )
        out_ref[q : q + 1, :] = jnp.max(best.T, axis=0, keepdims=True)


def tail(partials, slots, capacity, members):
    groups = partials.shape[0] // members
    width = -(-capacity // lanes) * lanes
    return pl.pallas_call(
        functools.partial(tail_kernel, capacity, members),
        in_specs=[vmem, vmem],
        out_specs=vmem,
        out_shape=jax.ShapeDtypeStruct(slots.shape, jnp.float32),
        scratch_shapes=[pltpu.VMEM((groups, width), jnp.float32)],
        name="pick_rows",
    )(slots, partials)


def on_device(embeddings, send_slot):
    row_count, features = embeddings.shape
    groups = lax.axis_size("grp")
    members = lax.axis_size("blk")
    slot_count = 2 * row_count
    capacity = slot_count // groups
    chunks = chunk_sizes(capacity)
    me = jnp.stack([lax.axis_index("grp"), lax.axis_index("blk")]).astype(jnp.int32)
    slots = send_slot.reshape(row_count // lanes, lanes)
    keeps, sends = head(me, embeddings, slots, capacity, chunks, groups)
    count, high = len(chunks), groups // 2
    last = count - 1

    sent, owns, done, pairs = {}, {}, {}, {}

    def rows(value, index, size):
        return value[index * size : (index + 1) * size]

    def block(step, z):
        size = chunks[step]
        near = first_near if step == 0 else sent["y", step + 1]
        return jnp.concatenate([rows(keeps[step], z, size), rows(near, z, size)], axis=0)

    def send(key, value, axis, size, bit, *earlier):
        held = [done[name] if name in done else sent[name] for name in earlier]
        sent[key] = swap(after(value, *held) if held else value, axis, size, bit)

    def send_z(step, z):
        early = [("z", step - 1, z)] if step >= 1 else []
        if step >= 2 and z == far[-1]:
            early += [("x", step - 2, 0)]
        if step >= 2 and z == 1:
            early += [("c", step - 2)]
        if 1 <= step < last and z == 1:
            early += [("y", step + 2)]
        send(("z", step, z), block(step, z), "grp", groups, 2 * z, *early)

    def collect(step):
        parts = [block(step, 0)]
        for z in range(1, high):
            parts.append(sent["z", step, z])
        owns[step] = jnp.concatenate(parts, axis=0)

    def send_x(step, cuts, between):
        total = owns[step].shape[0]
        cuts = [0] + [total * cut // 384 // 16 * 16 for cut in cuts] + [total]
        parts = [name for name in sent if name[:2] == ("x", step - 1)]
        for part in range(len(cuts) - 1):
            value = owns[step][cuts[part] : cuts[part + 1]]
            early = parts if part == 0 else between[part - 1]
            send(("x", step, part), value, "blk", members, 2, *early)

    def send_c(step, *early):
        across = [sent[name] for name in list(sent) if name[:2] == ("x", step)]
        pairs[step] = jnp.concatenate([owns[step]] + across, axis=0)
        send(("c", step), pairs[step], "blk", members, 1, *early)

    far = [high // 2] + [z for z in range(1, high) if z != high // 2]
    cut = sends[0].shape[0] // 32 * 16
    done["rest"] = sends[1]
    send(("y", 0), sends[0][:cut], "grp", groups, 1)
    send(("y", 1), sends[0][cut:], "grp", groups, 1, "rest")
    send(("y", 2), sends[1], "grp", groups, 1, ("y", 0))
    for step in range(2, count):
        early = ("y", 0) if step == 2 else ("y", step)
        send(("y", step + 1), sends[step], "grp", groups, 1, early)
    first_near = jnp.concatenate([sent["y", 0], sent["y", 1]], axis=0)
    for z in far:
        send_z(0, z)
    for step in range(1, count):
        collect(step - 1)
        for z in far:
            send_z(step, z)
        send_x(step - 1, [], [])
        send_c(step - 1, *[("z", step, z) for z in far])
    collect(last)
    mine = [owns[k] for k in range(count)]
    blocks = [block for k in range(last) for block in (pairs[k], sent["c", k])]
    states, cols = gram_step(0, mine[:last], blocks, [], 2)
    done["gram"] = cols[-1]
    send_x(last, [304], [["gram"]])
    send_c(last)
    states, half = gram_step(last, mine, [pairs[last]], states, 1)
    result = gram_last(
        me, mine, sent["c", last], states, cols + half, (0, 2, 1, 3), chunks, groups
    )
    homeward = lax.all_to_all(result, ("grp", "blk"), 0, 0, tiled=True)
    return tail(homeward, slots, capacity, members).reshape(row_count)


def solution(mesh):
    in_specs = (P(("grp", "blk"), None), P(("grp", "blk")))
    out_specs = P(("grp", "blk"))
    return jax.shard_map(
        on_device, mesh=mesh, in_specs=in_specs, out_specs=out_specs, check_vma=False
    )
```

```python
import functools

import jax
import jax.numpy as jnp
from jax import lax
from jax.experimental import pallas as pl
from jax.experimental.pallas import tpu as pltpu
from jax.sharding import PartitionSpec as P

sentinel = -3.0
epsilon = 1e-06
dead_mark = 2.0
dead_bias = -8.0
lanes = 128
smem = pl.BlockSpec(memory_space=pltpu.SMEM)
vmem = pl.BlockSpec(memory_space=pltpu.VMEM)


def chunk_sizes(capacity):
    count = 4 if capacity % 64 == 0 else 3
    return (capacity // count,) * count


def after(value, *earlier):
    return lax.optimization_barrier((value,) + earlier)[0]


def swap(value, axis, size, bit):
    return lax.ppermute(value, axis, [(i, i ^ bit) for i in range(size)])


def place(me, slots, normed, capacity, first, size, groups, low):
    shape = (groups // 2, size, 1)
    spot = lax.broadcasted_iota(jnp.int32, shape, 1) + first
    group = (lax.broadcasted_iota(jnp.int32, shape, 0) * 2 + low) ^ me
    wanted = (group * capacity + spot).reshape(groups // 2 * size, 1)
    pick = jnp.where(wanted == slots, 1.0, 0.0)
    live = jnp.max(pick, axis=1, keepdims=True)
    placed = jnp.dot(pick.astype(jnp.bfloat16), normed, preferred_element_type=jnp.float32)
    lane = lax.broadcasted_iota(jnp.int32, (1, placed.shape[1]), 1)
    mark = jnp.where(lane == 0, dead_mark, 0.0)
    return (placed + (1.0 - live) * mark).astype(jnp.bfloat16)


def flat(slot_ref):
    return jnp.concatenate([slot_ref[q : q + 1, :] for q in range(slot_ref.shape[0])], axis=1)


def first_kernel(capacity, chunks, groups, me_ref, slot_ref, x_ref, normed_ref, send_ref):
    wide = x_ref[...].astype(jnp.float32)
    normed_ref[...] = (
        wide * lax.rsqrt(jnp.sum(wide * wide, axis=-1, keepdims=True) + epsilon)
    ).astype(jnp.bfloat16)
    send_ref[...] = place(
        me_ref[0], flat(slot_ref), normed_ref[...], capacity, 0, chunks[0], groups, 1
    )


def rest_kernel(capacity, chunks, groups, me_ref, slot_ref, normed_ref, *out_refs):
    keeps, send_refs = out_refs[: len(chunks)], out_refs[len(chunks) :]
    slots, normed = flat(slot_ref), normed_ref[...]
    first = 0
    for step, size in enumerate(chunks):
        if step > 0:
            send_refs[step - 1][...] = place(
                me_ref[0], slots, normed, capacity, first, size, groups, 1
            )
        first += size
    first = 0
    for step, size in enumerate(chunks):
        keeps[step][...] = place(me_ref[0], slots, normed, capacity, first, size, groups, 0)
        first += size


def head(me, embeddings, slots, capacity, chunks, groups):
    rows, features = embeddings.shape
    half = [groups // 2 * size for size in chunks]

    def shape(count):
        return jax.ShapeDtypeStruct((count, features), jnp.bfloat16)

    def cost(count):
        return pl.CostEstimate(
            flops=2 * count * rows * features,
            bytes_accessed=2 * (rows + count) * features,
            transcendentals=0,
        )

    params = pltpu.CompilerParams(vmem_limit_bytes=24 * 2**20)
    normed, first_send = pl.pallas_call(
        functools.partial(first_kernel, capacity, chunks, groups),
        in_specs=[smem, vmem, vmem],
        out_specs=[vmem, vmem],
        out_shape=[shape(rows), shape(half[0])],
        compiler_params=params,
        cost_estimate=cost(half[0]),
        name="place_first",
    )(me, slots, embeddings)
    *placed, = pl.pallas_call(
        functools.partial(rest_kernel, capacity, chunks, groups),
        in_specs=[smem, vmem, vmem],
        out_specs=[vmem] * (2 * len(chunks) - 1),
        out_shape=[shape(count) for count in half + half[1:]],
        compiler_params=params,
        cost_estimate=cost(2 * sum(half) - half[0]),
        name="place_rest",
    )(me, slots, normed)
    return placed[: len(chunks)], [first_send] + placed[len(chunks) :]


def lane_fold(values):
    best = values[:, :lanes]
    for start in range(lanes, values.shape[1], lanes):
        best = jnp.maximum(best, values[:, start : start + lanes])
    return best


def gram_body(own_refs, piece_ref, row_refs, col_ref, col_start, holds_own):
    step = len(own_refs) - 1
    tile = 256
    nt = (((1,), (1,)), ((), ()))
    if holds_own:
        row_refs[step][...] = jnp.full(row_refs[step].shape, sentinel, jnp.float32)
    for first in range(0, piece_ref.shape[0], tile):
        x = piece_ref[first : first + tile, :]
        marks = x[:, :lanes].astype(jnp.float32).T[0:1, :]
        col_bias = jnp.where(marks > 1.5, dead_bias, 0.0)
        col_best = jnp.full((1, tile), sentinel, jnp.float32)
        for j in range(step + 1):
            own = own_refs[j][...]
            scores = lax.dot_general(own, x, nt, preferred_element_type=jnp.float32)
            usable = scores + col_bias
            if j == step:
                if holds_own and first < own.shape[0]:
                    rows = lax.broadcasted_iota(jnp.int32, usable.shape, 0)
                    cols = lax.broadcasted_iota(jnp.int32, usable.shape, 1)
                    usable = jnp.where(rows - cols == first, dead_bias, usable)
            else:
                row_bias = jnp.where(own[:, 0:1].astype(jnp.float32) > 1.5, dead_bias, 0.0)
                col_best = jnp.maximum(
                    col_best, jnp.max(scores + row_bias, axis=0, keepdims=True)
                )
            row_refs[j][...] = jnp.maximum(row_refs[j][...], lane_fold(usable))
        col_ref[0:1, col_start + first : col_start + first + tile] = col_best


def gram_kernel(first, step, pieces, *refs):
    news = step + 1 - first
    owns, refs = refs[: step + 1], refs[step + 1 :]
    blocks, refs = refs[: pieces * news], refs[pieces * news :]
    states, refs = refs[:first], refs[first:]
    rows, cols = refs[: step + 1], refs[step + 1 :]
    for state, row in zip(states, rows):
        row[...] = state[...]
    for k in range(news):
        now = first + k + 1
        for p in range(pieces):
            block = blocks[pieces * k + p]
            start = p * block.shape[0]
            gram_body(owns[:now], block, rows[:now], cols[k], start, p == 0)


def gram_last_kernel(step, relatives, chunks, groups, me_ref, *refs):
    members = len(relatives)
    owns, block, refs = refs[: step + 1], refs[step + 1], refs[step + 2 :]
    states, refs = refs[: step + 1], refs[step + 1 :]
    cols, refs = refs[: step + 1], refs[step + 1 :]
    out_ref, col, table = refs[:3]
    rows = refs[3:]
    for state, row in zip(states, rows):
        row[...] = state[...]
    gram_body(owns, block, rows, col, 0, False)
    first = 0
    for k, size in enumerate(chunks):
        row_k = jnp.max(rows[k][...].T, axis=0, keepdims=True)
        count = groups * size
        for p, relative in enumerate(relatives):
            source, shift = (col, 2 * count) if k == step and p >= 2 else (cols[k], 0)
            for r in range(groups):
                start = p * count + r * size - shift
                best = source[0:1, start : start + size]
                if p == 0:
                    best = jnp.maximum(best, row_k[:, r * size : (r + 1) * size])
                row = r * members + p
                table[row : row + 1, first : first + size] = best
        first += size
    for r in range(groups):
        for p, relative in enumerate(relatives):
            row = r * members + p
            target = (me_ref[0] ^ r) * members + (me_ref[1] ^ relative)
            out_ref[target] = table[row : row + 1, :]


def gram_params(owns, blocks):
    features = owns[0].shape[1]
    mine, others = sum(own.shape[0] for own in owns), sum(block.shape[0] for block in blocks)
    return dict(
        compiler_params=pltpu.CompilerParams(vmem_limit_bytes=24 * 2**20),
        cost_estimate=pl.CostEstimate(
            flops=2 * mine * others * features,
            bytes_accessed=2 * features * (mine + others),
            transcendentals=0,
        ),
    )


def gram_step(first, owns, blocks, states, pieces):
    step = len(owns) - 1
    row_shapes = [(own.shape[0], lanes) for own in owns]
    col_shapes = [(1, pieces * 2 * own.shape[0]) for own in owns[first:]]
    results = pl.pallas_call(
        functools.partial(gram_kernel, first, step, pieces),
        in_specs=[vmem] * (step + 1 + len(blocks) + first),
        out_specs=[vmem] * len(row_shapes + col_shapes),
        out_shape=[jax.ShapeDtypeStruct(s, jnp.float32) for s in row_shapes + col_shapes],
        name="gram_step",
        **gram_params(owns, blocks),
    )(*owns, *blocks, *states)
    return list(results[: step + 1]), list(results[step + 1 :])


def gram_last(me, owns, block, states, cols, relatives, chunks, groups):
    step = len(owns) - 1
    members = len(relatives)
    shape = (groups * members, 1, sum(chunks))
    return pl.pallas_call(
        functools.partial(gram_last_kernel, step, relatives, chunks, groups),
        in_specs=[smem] + [vmem] * (3 * step + 4),
        out_specs=vmem,
        out_shape=jax.ShapeDtypeStruct(shape, jnp.float32),
        scratch_shapes=[pltpu.VMEM((1, block.shape[0]), jnp.float32), pltpu.VMEM(shape[::2], jnp.float32)]
        + [pltpu.VMEM((own.shape[0], lanes), jnp.float32) for own in owns],
        name="gram_last",
        **gram_params(owns, [block]),
    )(me, *owns, block, *states, *cols)


def tail_kernel(capacity, members, slot_ref, part_ref, out_ref, table):
    groups = part_ref.shape[0] // members
    width = table.shape[1]
    table[...] = jnp.full(table.shape, sentinel, jnp.float32)
    for g in range(groups):
        table[g : g + 1, :capacity] = jnp.max(
            part_ref[g * members : (g + 1) * members], axis=0
        )
    lane = lax.broadcasted_iota(jnp.int32, (lanes, lanes), 1)
    for q in range(out_ref.shape[0]):
        slot = jnp.broadcast_to(slot_ref[q : q + 1, :], (lanes, lanes)).T
        best = jnp.full((lanes, lanes), sentinel, jnp.float32)
        for g in range(groups):
            for c in range(0, width, lanes):
                entry = table[g : g + 1, c : c + lanes]
                best = jnp.maximum(
                    best, jnp.where(slot - (g * capacity + c) == lane, entry, sentinel)
                )
        out_ref[q : q + 1, :] = jnp.max(best.T, axis=0, keepdims=True)


def tail(partials, slots, capacity, members):
    groups = partials.shape[0] // members
    width = -(-capacity // lanes) * lanes
    return pl.pallas_call(
        functools.partial(tail_kernel, capacity, members),
        in_specs=[vmem, vmem],
        out_specs=vmem,
        out_shape=jax.ShapeDtypeStruct(slots.shape, jnp.float32),
        scratch_shapes=[pltpu.VMEM((groups, width), jnp.float32)],
        name="pick_rows",
    )(slots, partials)


def on_device(embeddings, send_slot):
    row_count, features = embeddings.shape
    groups = lax.axis_size("grp")
    members = lax.axis_size("blk")
    slot_count = 2 * row_count
    capacity = slot_count // groups
    chunks = chunk_sizes(capacity)
    me = jnp.stack([lax.axis_index("grp"), lax.axis_index("blk")]).astype(jnp.int32)
    slots = send_slot.reshape(row_count // lanes, lanes)
    keeps, sends = head(me, embeddings, slots, capacity, chunks, groups)
    count, high = len(chunks), groups // 2
    last = count - 1

    sent, owns, done, pairs = {}, {}, {}, {}

    def rows(value, index, size):
        return value[index * size : (index + 1) * size]

    def block(step, z):
        size = chunks[step]
        near = first_near if step == 0 else sent["y", step + 1]
        return jnp.concatenate([rows(keeps[step], z, size), rows(near, z, size)], axis=0)

    def send(key, value, axis, size, bit, *earlier):
        held = [done[name] if name in done else sent[name] for name in earlier]
        sent[key] = swap(after(value, *held) if held else value, axis, size, bit)

    def send_z(step, z):
        early = [("z", step - 1, z)] if step >= 1 else []
        if step >= 2 and z == far[-1]:
            early += [("x", step - 2, 0)]
        if step >= 2 and z == 1:
            early += [("c", step - 2)]
        if step == 1 and z == 1:
            early += [("y", k + 1) for k in range(2, count)]
        send(("z", step, z), block(step, z), "grp", groups, 2 * z, *early)

    def collect(step):
        parts = [block(step, 0)]
        for z in range(1, high):
            parts.append(sent["z", step, z])
        owns[step] = jnp.concatenate(parts, axis=0)

    def send_x(step, cuts, between):
        total = owns[step].shape[0]
        cuts = [0] + [total * cut // 384 // 16 * 16 for cut in cuts] + [total]
        parts = [name for name in sent if name[:2] == ("x", step - 1)]
        for part in range(len(cuts) - 1):
            value = owns[step][cuts[part] : cuts[part + 1]]
            early = parts if part == 0 else between[part - 1]
            send(("x", step, part), value, "blk", members, 2, *early)

    def send_c(step, *early):
        across = [sent[name] for name in list(sent) if name[:2] == ("x", step)]
        pairs[step] = jnp.concatenate([owns[step]] + across, axis=0)
        send(("c", step), pairs[step], "blk", members, 1, *early)

    far = [high // 2] + [z for z in range(1, high) if z != high // 2]
    cut = sends[0].shape[0] // 32 * 16
    done["rest"] = sends[1]
    send(("y", 0), sends[0][:cut], "grp", groups, 1)
    send(("y", 1), sends[0][cut:], "grp", groups, 1, "rest")
    send(("y", 2), sends[1], "grp", groups, 1, ("y", 0))
    for step in range(2, count):
        early = ("y", 0) if step == 2 else ("y", step)
        send(("y", step + 1), sends[step], "grp", groups, 1, early)
    first_near = jnp.concatenate([sent["y", 0], sent["y", 1]], axis=0)
    for z in far:
        send_z(0, z)
    for step in range(1, count):
        collect(step - 1)
        for z in far:
            send_z(step, z)
        send_x(step - 1, [], [])
        send_c(step - 1, *[("z", step, z) for z in far])
    collect(last)
    mine = [owns[k] for k in range(count)]
    blocks = [block for k in range(last) for block in (pairs[k], sent["c", k])]
    states, cols = gram_step(0, mine[:last], blocks, [], 2)
    done["gram"] = cols[-1]
    send_x(last, [304], [["gram"]])
    send_c(last)
    states, half = gram_step(last, mine, [pairs[last]], states, 1)
    result = gram_last(
        me, mine, sent["c", last], states, cols + half, (0, 2, 1, 3), chunks, groups
    )
    homeward = lax.all_to_all(result, ("grp", "blk"), 0, 0, tiled=True)
    return tail(homeward, slots, capacity, members).reshape(row_count)


def solution(mesh):
    in_specs = (P(("grp", "blk"), None), P(("grp", "blk")))
    out_specs = P(("grp", "blk"))
    return jax.shard_map(
        on_device, mesh=mesh, in_specs=in_specs, out_specs=out_specs, check_vma=False
    )
```

```python
import functools

import jax
import jax.numpy as jnp
from jax import lax
from jax.experimental import pallas as pl
from jax.experimental.pallas import tpu as pltpu
from jax.sharding import PartitionSpec as P

sentinel = -3.0
epsilon = 1e-06
dead_mark = 2.0
dead_bias = -8.0
lanes = 128
smem = pl.BlockSpec(memory_space=pltpu.SMEM)
vmem = pl.BlockSpec(memory_space=pltpu.VMEM)


def chunk_sizes(capacity):
    count = 4 if capacity % 64 == 0 else 3
    return (capacity // count,) * count


def after(value, *earlier):
    return lax.optimization_barrier((value,) + earlier)[0]


def swap(value, axis, size, bit):
    return lax.ppermute(value, axis, [(i, i ^ bit) for i in range(size)])


def place(me, slots, normed, capacity, first, size, groups, low):
    shape = (groups // 2, size, 1)
    spot = lax.broadcasted_iota(jnp.int32, shape, 1) + first
    group = (lax.broadcasted_iota(jnp.int32, shape, 0) * 2 + low) ^ me
    wanted = (group * capacity + spot).reshape(groups // 2 * size, 1)
    pick = jnp.where(wanted == slots, 1.0, 0.0)
    live = jnp.max(pick, axis=1, keepdims=True)
    placed = jnp.dot(pick.astype(jnp.bfloat16), normed, preferred_element_type=jnp.float32)
    lane = lax.broadcasted_iota(jnp.int32, (1, placed.shape[1]), 1)
    mark = jnp.where(lane == 0, dead_mark, 0.0)
    return (placed + (1.0 - live) * mark).astype(jnp.bfloat16)


def flat(slot_ref):
    return jnp.concatenate([slot_ref[q : q + 1, :] for q in range(slot_ref.shape[0])], axis=1)


def first_kernel(capacity, chunks, groups, me_ref, slot_ref, x_ref, normed_ref, send_ref):
    wide = x_ref[...].astype(jnp.float32)
    normed_ref[...] = (
        wide * lax.rsqrt(jnp.sum(wide * wide, axis=-1, keepdims=True) + epsilon)
    ).astype(jnp.bfloat16)
    send_ref[...] = place(
        me_ref[0], flat(slot_ref), normed_ref[...], capacity, 0, chunks[0], groups, 1
    )


def rest_kernel(capacity, chunks, groups, me_ref, slot_ref, normed_ref, *out_refs):
    keeps, send_refs = out_refs[: len(chunks)], out_refs[len(chunks) :]
    slots, normed = flat(slot_ref), normed_ref[...]
    first = 0
    for step, size in enumerate(chunks):
        if step > 0:
            send_refs[step - 1][...] = place(
                me_ref[0], slots, normed, capacity, first, size, groups, 1
            )
        first += size
    first = 0
    for step, size in enumerate(chunks):
        keeps[step][...] = place(me_ref[0], slots, normed, capacity, first, size, groups, 0)
        first += size


def head(me, embeddings, slots, capacity, chunks, groups):
    rows, features = embeddings.shape
    half = [groups // 2 * size for size in chunks]

    def shape(count):
        return jax.ShapeDtypeStruct((count, features), jnp.bfloat16)

    def cost(count):
        return pl.CostEstimate(
            flops=2 * count * rows * features,
            bytes_accessed=2 * (rows + count) * features,
            transcendentals=0,
        )

    params = pltpu.CompilerParams(vmem_limit_bytes=24 * 2**20)
    normed, first_send = pl.pallas_call(
        functools.partial(first_kernel, capacity, chunks, groups),
        in_specs=[smem, vmem, vmem],
        out_specs=[vmem, vmem],
        out_shape=[shape(rows), shape(half[0])],
        compiler_params=params,
        cost_estimate=cost(half[0]),
        name="place_first",
    )(me, slots, embeddings)
    *placed, = pl.pallas_call(
        functools.partial(rest_kernel, capacity, chunks, groups),
        in_specs=[smem, vmem, vmem],
        out_specs=[vmem] * (2 * len(chunks) - 1),
        out_shape=[shape(count) for count in half + half[1:]],
        compiler_params=params,
        cost_estimate=cost(2 * sum(half) - half[0]),
        name="place_rest",
    )(me, slots, normed)
    return placed[: len(chunks)], [first_send] + placed[len(chunks) :]


def lane_fold(values):
    best = values[:, :lanes]
    for start in range(lanes, values.shape[1], lanes):
        best = jnp.maximum(best, values[:, start : start + lanes])
    return best


def gram_body(own_refs, piece_ref, row_refs, col_ref, col_start, holds_own):
    step = len(own_refs) - 1
    tile = 256
    nt = (((1,), (1,)), ((), ()))
    if holds_own:
        row_refs[step][...] = jnp.full(row_refs[step].shape, sentinel, jnp.float32)
    for first in range(0, piece_ref.shape[0], tile):
        x = piece_ref[first : first + tile, :]
        marks = x[:, :lanes].astype(jnp.float32).T[0:1, :]
        col_bias = jnp.where(marks > 1.5, dead_bias, 0.0)
        col_best = jnp.full((1, tile), sentinel, jnp.float32)
        for j in range(step + 1):
            own = own_refs[j][...]
            scores = lax.dot_general(own, x, nt, preferred_element_type=jnp.float32)
            usable = scores + col_bias
            if j == step:
                if holds_own and first < own.shape[0]:
                    rows = lax.broadcasted_iota(jnp.int32, usable.shape, 0)
                    cols = lax.broadcasted_iota(jnp.int32, usable.shape, 1)
                    usable = jnp.where(rows - cols == first, dead_bias, usable)
            else:
                row_bias = jnp.where(own[:, 0:1].astype(jnp.float32) > 1.5, dead_bias, 0.0)
                col_best = jnp.maximum(
                    col_best, jnp.max(scores + row_bias, axis=0, keepdims=True)
                )
            row_refs[j][...] = jnp.maximum(row_refs[j][...], lane_fold(usable))
        col_ref[0:1, col_start + first : col_start + first + tile] = col_best


def gram_kernel(first, step, pieces, *refs):
    news = step + 1 - first
    owns, refs = refs[: step + 1], refs[step + 1 :]
    blocks, refs = refs[: pieces * news], refs[pieces * news :]
    states, refs = refs[:first], refs[first:]
    rows, cols = refs[: step + 1], refs[step + 1 :]
    for state, row in zip(states, rows):
        row[...] = state[...]
    for k in range(news):
        now = first + k + 1
        for p in range(pieces):
            block = blocks[pieces * k + p]
            start = p * block.shape[0]
            gram_body(owns[:now], block, rows[:now], cols[k], start, p == 0)


def gram_last_kernel(step, relatives, chunks, groups, me_ref, *refs):
    members = len(relatives)
    owns, block, refs = refs[: step + 1], refs[step + 1], refs[step + 2 :]
    states, refs = refs[: step + 1], refs[step + 1 :]
    cols, refs = refs[: step + 1], refs[step + 1 :]
    out_ref, col, table = refs[:3]
    rows = refs[3:]
    for state, row in zip(states, rows):
        row[...] = state[...]
    gram_body(owns, block, rows, col, 0, False)
    first = 0
    for k, size in enumerate(chunks):
        row_k = jnp.max(rows[k][...].T, axis=0, keepdims=True)
        count = groups * size
        for p, relative in enumerate(relatives):
            source, shift = (col, 2 * count) if k == step and p >= 2 else (cols[k], 0)
            for r in range(groups):
                start = p * count + r * size - shift
                best = source[0:1, start : start + size]
                if p == 0:
                    best = jnp.maximum(best, row_k[:, r * size : (r + 1) * size])
                row = r * members + p
                table[row : row + 1, first : first + size] = best
        first += size
    for r in range(groups):
        for p, relative in enumerate(relatives):
            row = r * members + p
            target = (me_ref[0] ^ r) * members + (me_ref[1] ^ relative)
            out_ref[target] = table[row : row + 1, :]


def gram_params(owns, blocks):
    features = owns[0].shape[1]
    mine, others = sum(own.shape[0] for own in owns), sum(block.shape[0] for block in blocks)
    return dict(
        compiler_params=pltpu.CompilerParams(vmem_limit_bytes=24 * 2**20),
        cost_estimate=pl.CostEstimate(
            flops=2 * mine * others * features,
            bytes_accessed=2 * features * (mine + others),
            transcendentals=0,
        ),
    )


def gram_step(first, owns, blocks, states, pieces):
    step = len(owns) - 1
    row_shapes = [(own.shape[0], lanes) for own in owns]
    col_shapes = [(1, pieces * 2 * own.shape[0]) for own in owns[first:]]
    results = pl.pallas_call(
        functools.partial(gram_kernel, first, step, pieces),
        in_specs=[vmem] * (step + 1 + len(blocks) + first),
        out_specs=[vmem] * len(row_shapes + col_shapes),
        out_shape=[jax.ShapeDtypeStruct(s, jnp.float32) for s in row_shapes + col_shapes],
        name="gram_step",
        **gram_params(owns, blocks),
    )(*owns, *blocks, *states)
    return list(results[: step + 1]), list(results[step + 1 :])


def gram_last(me, owns, block, states, cols, relatives, chunks, groups):
    step = len(owns) - 1
    members = len(relatives)
    shape = (groups * members, 1, sum(chunks))
    return pl.pallas_call(
        functools.partial(gram_last_kernel, step, relatives, chunks, groups),
        in_specs=[smem] + [vmem] * (3 * step + 4),
        out_specs=vmem,
        out_shape=jax.ShapeDtypeStruct(shape, jnp.float32),
        scratch_shapes=[pltpu.VMEM((1, block.shape[0]), jnp.float32), pltpu.VMEM(shape[::2], jnp.float32)]
        + [pltpu.VMEM((own.shape[0], lanes), jnp.float32) for own in owns],
        name="gram_last",
        **gram_params(owns, [block]),
    )(me, *owns, block, *states, *cols)


def tail_kernel(capacity, members, slot_ref, part_ref, out_ref, table):
    groups = part_ref.shape[0] // members
    width = table.shape[1]
    table[...] = jnp.full(table.shape, sentinel, jnp.float32)
    for g in range(groups):
        table[g : g + 1, :capacity] = jnp.max(
            part_ref[g * members : (g + 1) * members], axis=0
        )
    lane = lax.broadcasted_iota(jnp.int32, (lanes, lanes), 1)
    for q in range(out_ref.shape[0]):
        slot = jnp.broadcast_to(slot_ref[q : q + 1, :], (lanes, lanes)).T
        best = jnp.full((lanes, lanes), sentinel, jnp.float32)
        for g in range(groups):
            for c in range(0, width, lanes):
                entry = table[g : g + 1, c : c + lanes]
                best = jnp.maximum(
                    best, jnp.where(slot - (g * capacity + c) == lane, entry, sentinel)
                )
        out_ref[q : q + 1, :] = jnp.max(best.T, axis=0, keepdims=True)


def tail(partials, slots, capacity, members):
    groups = partials.shape[0] // members
    width = -(-capacity // lanes) * lanes
    return pl.pallas_call(
        functools.partial(tail_kernel, capacity, members),
        in_specs=[vmem, vmem],
        out_specs=vmem,
        out_shape=jax.ShapeDtypeStruct(slots.shape, jnp.float32),
        scratch_shapes=[pltpu.VMEM((groups, width), jnp.float32)],
        name="pick_rows",
    )(slots, partials)


def on_device(embeddings, send_slot):
    row_count, features = embeddings.shape
    groups = lax.axis_size("grp")
    members = lax.axis_size("blk")
    slot_count = 2 * row_count
    capacity = slot_count // groups
    chunks = chunk_sizes(capacity)
    me = jnp.stack([lax.axis_index("grp"), lax.axis_index("blk")]).astype(jnp.int32)
    slots = send_slot.reshape(row_count // lanes, lanes)
    keeps, sends = head(me, embeddings, slots, capacity, chunks, groups)
    count, high = len(chunks), groups // 2
    last = count - 1

    sent, owns, done, pairs = {}, {}, {}, {}

    def rows(value, index, size):
        return value[index * size : (index + 1) * size]

    def block(step, z):
        size = chunks[step]
        near = first_near if step == 0 else sent["y", step + 1]
        return jnp.concatenate([rows(keeps[step], z, size), rows(near, z, size)], axis=0)

    def send(key, value, axis, size, bit, *earlier):
        held = [done[name] if name in done else sent[name] for name in earlier]
        sent[key] = swap(after(value, *held) if held else value, axis, size, bit)

    def send_z(step, z):
        early = [("z", step - 1, z)] if step >= 1 else []
        if step >= 2 and z == far[-1]:
            early += [("x", step - 2, 0)]
        if step >= 2 and z == 1:
            early += [("c", step - 2)]
        if step == 1 and z == 1:
            early += [("y", 3)]
        send(("z", step, z), block(step, z), "grp", groups, 2 * z, *early)

    def collect(step):
        parts = [block(step, 0)]
        for z in range(1, high):
            parts.append(sent["z", step, z])
        owns[step] = jnp.concatenate(parts, axis=0)

    def send_x(step, cuts, between):
        total = owns[step].shape[0]
        cuts = [0] + [total * cut // 384 // 16 * 16 for cut in cuts] + [total]
        parts = [name for name in sent if name[:2] == ("x", step - 1)]
        for part in range(len(cuts) - 1):
            value = owns[step][cuts[part] : cuts[part + 1]]
            early = parts if part == 0 else between[part - 1]
            if step == 1 and part == 0:
                early = early + [("y", count)]
            send(("x", step, part), value, "blk", members, 2, *early)

    def send_c(step, *early):
        across = [sent[name] for name in list(sent) if name[:2] == ("x", step)]
        pairs[step] = jnp.concatenate([owns[step]] + across, axis=0)
        send(("c", step), pairs[step], "blk", members, 1, *early)

    far = [high // 2] + [z for z in range(1, high) if z != high // 2]
    cut = sends[0].shape[0] // 32 * 16
    done["rest"] = sends[1]
    send(("y", 0), sends[0][:cut], "grp", groups, 1)
    send(("y", 1), sends[0][cut:], "grp", groups, 1, "rest")
    send(("y", 2), sends[1], "grp", groups, 1, ("y", 0))
    for step in range(2, count):
        early = ("y", 0) if step == 2 else ("y", step)
        send(("y", step + 1), sends[step], "grp", groups, 1, early)
    first_near = jnp.concatenate([sent["y", 0], sent["y", 1]], axis=0)
    for z in far:
        send_z(0, z)
    for step in range(1, count):
        collect(step - 1)
        for z in far:
            send_z(step, z)
        send_x(step - 1, [], [])
        send_c(step - 1, *[("z", step, z) for z in far])
    collect(last)
    mine = [owns[k] for k in range(count)]
    blocks = [block for k in range(last) for block in (pairs[k], sent["c", k])]
    states, cols = gram_step(0, mine[:last], blocks, [], 2)
    done["gram"] = cols[-1]
    send_x(last, [304], [["gram"]])
    send_c(last)
    states, half = gram_step(last, mine, [pairs[last]], states, 1)
    result = gram_last(
        me, mine, sent["c", last], states, cols + half, (0, 2, 1, 3), chunks, groups
    )
    homeward = lax.all_to_all(result, ("grp", "blk"), 0, 0, tiled=True)
    return tail(homeward, slots, capacity, members).reshape(row_count)


def solution(mesh):
    in_specs = (P(("grp", "blk"), None), P(("grp", "blk")))
    out_specs = P(("grp", "blk"))
    return jax.shard_map(
        on_device, mesh=mesh, in_specs=in_specs, out_specs=out_specs, check_vma=False
    )
```

```python
import functools

import jax
import jax.numpy as jnp
from jax import lax
from jax.experimental import pallas as pl
from jax.experimental.pallas import tpu as pltpu
from jax.sharding import PartitionSpec as P

sentinel = -3.0
epsilon = 1e-06
dead_mark = 2.0
dead_bias = -8.0
lanes = 128
smem = pl.BlockSpec(memory_space=pltpu.SMEM)
vmem = pl.BlockSpec(memory_space=pltpu.VMEM)


def chunk_sizes(capacity):
    count = 4 if capacity % 64 == 0 else 3
    return (capacity // count,) * count


def after(value, *earlier):
    return lax.optimization_barrier((value,) + earlier)[0]


def swap(value, axis, size, bit):
    return lax.ppermute(value, axis, [(i, i ^ bit) for i in range(size)])


def place(me, slots, normed, capacity, first, size, groups, low):
    shape = (groups // 2, size, 1)
    spot = lax.broadcasted_iota(jnp.int32, shape, 1) + first
    group = (lax.broadcasted_iota(jnp.int32, shape, 0) * 2 + low) ^ me
    wanted = (group * capacity + spot).reshape(groups // 2 * size, 1)
    pick = jnp.where(wanted == slots, 1.0, 0.0)
    live = jnp.max(pick, axis=1, keepdims=True)
    placed = jnp.dot(pick.astype(jnp.bfloat16), normed, preferred_element_type=jnp.float32)
    lane = lax.broadcasted_iota(jnp.int32, (1, placed.shape[1]), 1)
    mark = jnp.where(lane == 0, dead_mark, 0.0)
    return (placed + (1.0 - live) * mark).astype(jnp.bfloat16)


def flat(slot_ref):
    return jnp.concatenate([slot_ref[q : q + 1, :] for q in range(slot_ref.shape[0])], axis=1)


def first_kernel(capacity, chunks, groups, me_ref, slot_ref, x_ref, normed_ref, send_ref):
    wide = x_ref[...].astype(jnp.float32)
    normed_ref[...] = (
        wide * lax.rsqrt(jnp.sum(wide * wide, axis=-1, keepdims=True) + epsilon)
    ).astype(jnp.bfloat16)
    send_ref[...] = place(
        me_ref[0], flat(slot_ref), normed_ref[...], capacity, 0, chunks[0], groups, 1
    )


def rest_kernel(capacity, chunks, groups, me_ref, slot_ref, normed_ref, *out_refs):
    keeps, send_refs = out_refs[:-2], out_refs[-2:]
    slots, normed = flat(slot_ref), normed_ref[...]
    first, row = 0, 0
    for step, size in enumerate(chunks):
        placed = place(me_ref[0], slots, normed, capacity, first, size, groups, 1) if step else None
        if step == 1:
            send_refs[0][...] = placed
        elif step > 1:
            send_refs[1][row : row + placed.shape[0], :] = placed
            row += placed.shape[0]
        first += size
    first = 0
    for step, size in enumerate(chunks):
        keeps[step][...] = place(me_ref[0], slots, normed, capacity, first, size, groups, 0)
        first += size


def head(me, embeddings, slots, capacity, chunks, groups):
    rows, features = embeddings.shape
    half = [groups // 2 * size for size in chunks]

    def shape(count):
        return jax.ShapeDtypeStruct((count, features), jnp.bfloat16)

    def cost(count):
        return pl.CostEstimate(
            flops=2 * count * rows * features,
            bytes_accessed=2 * (rows + count) * features,
            transcendentals=0,
        )

    params = pltpu.CompilerParams(vmem_limit_bytes=24 * 2**20)
    normed, first_send = pl.pallas_call(
        functools.partial(first_kernel, capacity, chunks, groups),
        in_specs=[smem, vmem, vmem],
        out_specs=[vmem, vmem],
        out_shape=[shape(rows), shape(half[0])],
        compiler_params=params,
        cost_estimate=cost(half[0]),
        name="place_first",
    )(me, slots, embeddings)
    *keeps, next_send, rest_send = pl.pallas_call(
        functools.partial(rest_kernel, capacity, chunks, groups),
        in_specs=[smem, vmem, vmem],
        out_specs=[vmem] * (len(chunks) + 2),
        out_shape=[shape(count) for count in half + [half[1], sum(half[2:])]],
        compiler_params=params,
        cost_estimate=cost(2 * sum(half) - half[0]),
        name="place_rest",
    )(me, slots, normed)
    return keeps, first_send, next_send, rest_send


def lane_fold(values):
    best = values[:, :lanes]
    for start in range(lanes, values.shape[1], lanes):
        best = jnp.maximum(best, values[:, start : start + lanes])
    return best


def gram_body(own_refs, piece_ref, row_refs, col_ref, col_start, holds_own):
    step = len(own_refs) - 1
    tile = 256
    nt = (((1,), (1,)), ((), ()))
    if holds_own:
        row_refs[step][...] = jnp.full(row_refs[step].shape, sentinel, jnp.float32)
    for first in range(0, piece_ref.shape[0], tile):
        x = piece_ref[first : first + tile, :]
        marks = x[:, :lanes].astype(jnp.float32).T[0:1, :]
        col_bias = jnp.where(marks > 1.5, dead_bias, 0.0)
        col_best = jnp.full((1, tile), sentinel, jnp.float32)
        for j in range(step + 1):
            own = own_refs[j][...]
            scores = lax.dot_general(own, x, nt, preferred_element_type=jnp.float32)
            usable = scores + col_bias
            if j == step:
                if holds_own and first < own.shape[0]:
                    rows = lax.broadcasted_iota(jnp.int32, usable.shape, 0)
                    cols = lax.broadcasted_iota(jnp.int32, usable.shape, 1)
                    usable = jnp.where(rows - cols == first, dead_bias, usable)
            else:
                row_bias = jnp.where(own[:, 0:1].astype(jnp.float32) > 1.5, dead_bias, 0.0)
                col_best = jnp.maximum(
                    col_best, jnp.max(scores + row_bias, axis=0, keepdims=True)
                )
            row_refs[j][...] = jnp.maximum(row_refs[j][...], lane_fold(usable))
        col_ref[0:1, col_start + first : col_start + first + tile] = col_best


def gram_kernel(first, step, pieces, *refs):
    news = step + 1 - first
    owns, refs = refs[: step + 1], refs[step + 1 :]
    blocks, refs = refs[: pieces * news], refs[pieces * news :]
    states, refs = refs[:first], refs[first:]
    rows, cols = refs[: step + 1], refs[step + 1 :]
    for state, row in zip(states, rows):
        row[...] = state[...]
    for k in range(news):
        now = first + k + 1
        for p in range(pieces):
            block = blocks[pieces * k + p]
            start = p * block.shape[0]
            gram_body(owns[:now], block, rows[:now], cols[k], start, p == 0)


def gram_last_kernel(step, relatives, chunks, groups, me_ref, *refs):
    members = len(relatives)
    owns, block, refs = refs[: step + 1], refs[step + 1], refs[step + 2 :]
    states, refs = refs[: step + 1], refs[step + 1 :]
    cols, refs = refs[: step + 1], refs[step + 1 :]
    out_ref, col, table = refs[:3]
    rows = refs[3:]
    for state, row in zip(states, rows):
        row[...] = state[...]
    gram_body(owns, block, rows, col, 0, False)
    first = 0
    for k, size in enumerate(chunks):
        row_k = jnp.max(rows[k][...].T, axis=0, keepdims=True)
        count = groups * size
        for p, relative in enumerate(relatives):
            source, shift = (col, 2 * count) if k == step and p >= 2 else (cols[k], 0)
            for r in range(groups):
                start = p * count + r * size - shift
                best = source[0:1, start : start + size]
                if p == 0:
                    best = jnp.maximum(best, row_k[:, r * size : (r + 1) * size])
                row = r * members + p
                table[row : row + 1, first : first + size] = best
        first += size
    for r in range(groups):
        for p, relative in enumerate(relatives):
            row = r * members + p
            target = (me_ref[0] ^ r) * members + (me_ref[1] ^ relative)
            out_ref[target] = table[row : row + 1, :]


def gram_params(owns, blocks):
    features = owns[0].shape[1]
    mine, others = sum(own.shape[0] for own in owns), sum(block.shape[0] for block in blocks)
    return dict(
        compiler_params=pltpu.CompilerParams(vmem_limit_bytes=24 * 2**20),
        cost_estimate=pl.CostEstimate(
            flops=2 * mine * others * features,
            bytes_accessed=2 * features * (mine + others),
            transcendentals=0,
        ),
    )


def gram_step(first, owns, blocks, states, pieces):
    step = len(owns) - 1
    row_shapes = [(own.shape[0], lanes) for own in owns]
    col_shapes = [(1, pieces * 2 * own.shape[0]) for own in owns[first:]]
    results = pl.pallas_call(
        functools.partial(gram_kernel, first, step, pieces),
        in_specs=[vmem] * (step + 1 + len(blocks) + first),
        out_specs=[vmem] * len(row_shapes + col_shapes),
        out_shape=[jax.ShapeDtypeStruct(s, jnp.float32) for s in row_shapes + col_shapes],
        name="gram_step",
        **gram_params(owns, blocks),
    )(*owns, *blocks, *states)
    return list(results[: step + 1]), list(results[step + 1 :])


def gram_last(me, owns, block, states, cols, relatives, chunks, groups):
    step = len(owns) - 1
    members = len(relatives)
    shape = (groups * members, 1, sum(chunks))
    return pl.pallas_call(
        functools.partial(gram_last_kernel, step, relatives, chunks, groups),
        in_specs=[smem] + [vmem] * (3 * step + 4),
        out_specs=vmem,
        out_shape=jax.ShapeDtypeStruct(shape, jnp.float32),
        scratch_shapes=[pltpu.VMEM((1, block.shape[0]), jnp.float32), pltpu.VMEM(shape[::2], jnp.float32)]
        + [pltpu.VMEM((own.shape[0], lanes), jnp.float32) for own in owns],
        name="gram_last",
        **gram_params(owns, [block]),
    )(me, *owns, block, *states, *cols)


def tail_kernel(capacity, members, slot_ref, part_ref, out_ref, table):
    groups = part_ref.shape[0] // members
    width = table.shape[1]
    table[...] = jnp.full(table.shape, sentinel, jnp.float32)
    for g in range(groups):
        table[g : g + 1, :capacity] = jnp.max(
            part_ref[g * members : (g + 1) * members], axis=0
        )
    lane = lax.broadcasted_iota(jnp.int32, (lanes, lanes), 1)
    for q in range(out_ref.shape[0]):
        slot = jnp.broadcast_to(slot_ref[q : q + 1, :], (lanes, lanes)).T
        best = jnp.full((lanes, lanes), sentinel, jnp.float32)
        for g in range(groups):
            for c in range(0, width, lanes):
                entry = table[g : g + 1, c : c + lanes]
                best = jnp.maximum(
                    best, jnp.where(slot - (g * capacity + c) == lane, entry, sentinel)
                )
        out_ref[q : q + 1, :] = jnp.max(best.T, axis=0, keepdims=True)


def tail(partials, slots, capacity, members):
    groups = partials.shape[0] // members
    width = -(-capacity // lanes) * lanes
    return pl.pallas_call(
        functools.partial(tail_kernel, capacity, members),
        in_specs=[vmem, vmem],
        out_specs=vmem,
        out_shape=jax.ShapeDtypeStruct(slots.shape, jnp.float32),
        scratch_shapes=[pltpu.VMEM((groups, width), jnp.float32)],
        name="pick_rows",
    )(slots, partials)


def on_device(embeddings, send_slot):
    row_count, features = embeddings.shape
    groups = lax.axis_size("grp")
    members = lax.axis_size("blk")
    slot_count = 2 * row_count
    capacity = slot_count // groups
    chunks = chunk_sizes(capacity)
    me = jnp.stack([lax.axis_index("grp"), lax.axis_index("blk")]).astype(jnp.int32)
    slots = send_slot.reshape(row_count // lanes, lanes)
    keeps, first_send, next_send, rest_send = head(me, embeddings, slots, capacity, chunks, groups)
    count, high = len(chunks), groups // 2
    last = count - 1

    sent, owns, done, pairs = {}, {}, {}, {}

    def rows(value, index, size):
        return value[index * size : (index + 1) * size]

    def block(step, z):
        size = chunks[step]
        near = first_near if step == 0 else sent["y", min(step, 2) + 1]
        skip = sum(chunks[2:step]) * high
        return jnp.concatenate(
            [rows(keeps[step], z, size), rows(near[skip:], z, size)], axis=0
        )

    def send(key, value, axis, size, bit, *earlier):
        held = [done[name] if name in done else sent[name] for name in earlier]
        sent[key] = swap(after(value, *held) if held else value, axis, size, bit)

    def send_z(step, z):
        early = [("z", step - 1, z)] if step >= 1 else []
        if step >= 2 and z == far[-1]:
            early += [("x", step - 2, 0)]
        if step >= 2 and z == 1:
            early += [("c", step - 2)]
        if step == 1 and z == 1:
            early += [("y", 3)]
        send(("z", step, z), block(step, z), "grp", groups, 2 * z, *early)

    def collect(step):
        parts = [block(step, 0)]
        for z in range(1, high):
            parts.append(sent["z", step, z])
        owns[step] = jnp.concatenate(parts, axis=0)

    def send_x(step, cuts, between):
        total = owns[step].shape[0]
        cuts = [0] + [total * cut // 384 // 16 * 16 for cut in cuts] + [total]
        parts = [name for name in sent if name[:2] == ("x", step - 1)]
        for part in range(len(cuts) - 1):
            value = owns[step][cuts[part] : cuts[part + 1]]
            early = parts if part == 0 else between[part - 1]
            send(("x", step, part), value, "blk", members, 2, *early)

    def send_c(step, *early):
        across = [sent[name] for name in list(sent) if name[:2] == ("x", step)]
        pairs[step] = jnp.concatenate([owns[step]] + across, axis=0)
        send(("c", step), pairs[step], "blk", members, 1, *early)

    far = [high // 2] + [z for z in range(1, high) if z != high // 2]
    cut = first_send.shape[0] // 32 * 16
    done["rest"] = rest_send
    send(("y", 0), first_send[:cut], "grp", groups, 1)
    send(("y", 1), first_send[cut:], "grp", groups, 1, "rest")
    send(("y", 2), next_send, "grp", groups, 1, ("y", 0))
    send(("y", 3), rest_send, "grp", groups, 1, ("y", 0))
    first_near = jnp.concatenate([sent["y", 0], sent["y", 1]], axis=0)
    for z in far:
        send_z(0, z)
    for step in range(1, count):
        collect(step - 1)
        for z in far:
            send_z(step, z)
        send_x(step - 1, [], [])
        send_c(step - 1, *[("z", step, z) for z in far])
    collect(last)
    mine = [owns[k] for k in range(count)]
    blocks = [block for k in range(last) for block in (pairs[k], sent["c", k])]
    states, cols = gram_step(0, mine[:last], blocks, [], 2)
    done["gram"] = cols[-1]
    send_x(last, [304], [["gram"]])
    send_c(last)
    states, half = gram_step(last, mine, [pairs[last]], states, 1)
    result = gram_last(
        me, mine, sent["c", last], states, cols + half, (0, 2, 1, 3), chunks, groups
    )
    homeward = lax.all_to_all(result, ("grp", "blk"), 0, 0, tiled=True)
    return tail(homeward, slots, capacity, members).reshape(row_count)


def solution(mesh):
    in_specs = (P(("grp", "blk"), None), P(("grp", "blk")))
    out_specs = P(("grp", "blk"))
    return jax.shard_map(
        on_device, mesh=mesh, in_specs=in_specs, out_specs=out_specs, check_vma=False
    )
```
